128 devices in a mesh: blk: 8 (over x, core), inner: 16 (over y, z).
Axes of the slice: x: 4, y: 4, z: 4, core: 2. Of those that a mesh axis runs over, the one named last changes fastest.
Arguments:
- sheet_plasma_quantities: float32 [8, 4, 1024, 2048], P(None, None, 'blk', 'inner'), may hold values from -6 to 6
- speeds: float32 [3, 4, 1024, 2048], P(None, None, 'blk', 'inner'), may hold values from -1 to 1
- source_matrix: float32 [8, 8], replicated, may hold values from -2 to 2
- pedersen: float32 [2048, 4096], P('blk', 'inner'), may hold values from 0.05 to 1
- owners: int32 [32768, 1], P(('blk', 'inner')), may hold values from 0 to 127; in each aligned block of 256 rows (0 to 255, 256 to 511, ...) at most 4 rows name the same one
- tile_positions: int32 [32768], P(('blk', 'inner')), may hold values from 0 to 1023
Outputs:
- updated_plasma_quantities: float32 [8, 4, 1024, 2048], P(None, None, 'blk', 'inner')
- potential: float32 [2048, 4096], P('blk', 'inner')
- heating: float32 [2048, 4096], P('blk', 'inner')
- block_potential_heat: float32 [32768, 128], P(('blk', 'inner'))
The draws below stay inside these ranges and needn't reach their ends.
Inputs may be any that keep to these rules, and one draw needn't show every extreme that they name: `owners`: within the rows of one device (aligned blocks of 256 boundary blocks) no owner is named more than 4 times.
All inputs are finite; a program needn't handle non-finite values.
Results may differ from the reference program's by a relative error of at most 0.00045.
Values sent between devices are 32-bit elements; how exact they have to be, the bound alone decides.
A program may use at most 192 MiB of HBM per device.

```python
import math
import jax
import jax.numpy as jnp
import numpy as np
from jax import lax

PLASMA_QUANTITY = 8
BLOCK = 8
SHELL_LAYERS = 4
CX = 128
CY = 128
STEPS = 2
NLAT = 2048
NLON = 4096
MORD = 256
LDEG = 256
SHEET_ZONES_EAST = 1024
SHEET_ZONES_NORTH = 2048
BB_DEV = 256
CAP = 4
BBLOCKS = 32768
LAT_DEV = 256
LON_DEV = 256
TILES_DEV = 1024
N_BLK = 8
N_INNER = 16


def plant(drawn, key, least, high):
    place = [jax.random.randint(jax.random.fold_in(key, axis), (), 0, length) for axis, length in enumerate(drawn.shape)]
    longest = drawn.shape.index(max(drawn.shape))
    beside = place[:longest] + [(place[longest] + 1) % drawn.shape[longest]] + place[longest + 1:]
    return drawn.at[tuple(place)].set(least).at[tuple(beside)].set(high)


def shard_levels(stream_key, dims, cuts, low, top_value):
    gain, own = 1.0, jax.random.fold_in(stream_key, 6)
    for axis_at, parts in cuts:
        draws = jnp.exp(jax.random.uniform(jax.random.fold_in(own, axis_at), (parts,), jnp.float32, low / len(cuts), top_value / len(cuts)))
        gain = gain * jnp.repeat(draws, dims[axis_at] // parts).reshape([-1 if axis == axis_at else 1 for axis in range(len(dims))])
    return gain


def routed_block(own_key, own, number, rows, number_of, top, most, skew):
    sequence = jax.random.permutation(own_key, number_of)
    packed, usual = portions_of(number_of, rows * top, most, skew, True), portions_of(number_of, rows * top, most, skew, False)
    places = jnp.arange(number_of)

    def named(tallies, rotation):
        used = int((tallies > 0).sum())
        fixed = max(1, used // 4)
        moved = fixed + (places - fixed + rotation * (used - fixed)) % max(1, number_of - fixed)
        return jnp.zeros((number_of,), jnp.int32).at[sequence[jnp.where(places < fixed, places, moved)]].set(jnp.asarray(tallies, jnp.int32))

    tallies = jnp.where(number % 4 == 0, named(packed, number // 4), named(usual, number - number // 4 - 1))
    mixed = jax.random.permutation(jax.random.fold_in(own, 3), number_of)
    source_of, receiver = mixed[0:number_of // 2 * 2:2], mixed[1:number_of // 2 * 2:2]
    margin = jnp.minimum(tallies[source_of] - 1, most - tallies[receiver]) // 2
    margin = jnp.where((source_of == sequence[0]) | (receiver == sequence[0]) | (tallies[receiver] == 0), 0, jnp.maximum(margin, 0))
    moved = jax.random.randint(jax.random.fold_in(own, 4), (number_of // 2,), 0, 1 << 20) % (margin + 1)
    tallies = tallies.at[source_of].add(-moved).at[receiver].add(moved)
    labels = jnp.searchsorted(jnp.cumsum(tallies), jnp.arange(rows * top), side="right").astype(jnp.int32)
    table = labels.reshape(top, rows).T
    table = table[jax.random.permutation(jax.random.fold_in(own, 1), rows)]
    rotation = jax.random.randint(jax.random.fold_in(own, 2), (rows, 1), 0, top)
    return jnp.take_along_axis(table, (jnp.arange(top)[None, :] + rotation) % top, axis=1)


def portions_of(count, total, limit, slope, full):
    weights = [(1 << 20) // math.isqrt(rank ** slope) + 1 for rank in range(1, count + 1)]
    largest = limit if full else min(limit, max(-(-total // count), total * weights[0] // sum(weights)))
    least = 1 if total - largest >= count - 1 else 0
    given, rest = [largest] + [least] * (count - 1), total - largest - least * (count - 1)
    while rest > 0:
        movable = [i for i in range(1, count) if given[i] < largest] or [i for i in range(1, count) if given[i] < limit]
        whole, budget = sum([weights[i] for i in movable]), rest
        for i in movable:
            more = min(limit - given[i], max(1, budget * weights[i] // whole), rest)
            given[i] = given[i] + more
            rest = rest - more
    return np.array(given)


def noise(stream_key, shape, scale, reach, cuts=(), held_as=jnp.bfloat16):
    entries = scale * jax.random.normal(stream_key, shape, jnp.float32)
    if cuts:
        entries = entries * shard_levels(stream_key, shape, cuts, -0.22, 0.18)
    return jnp.clip(entries, -reach, reach).astype(held_as)


def setup_inputs(seed: int = 0) -> dict:
    seeds = jax.random.split(jax.random.key(seed), 7)
    sheet_plasma_quantities = noise(seeds[0], (PLASMA_QUANTITY, SHELL_LAYERS, SHEET_ZONES_EAST, SHEET_ZONES_NORTH), 1.0, 6.0, ((2, 8), (3, 16)), jnp.float32)
    speeds = jnp.clip(jax.random.uniform(seeds[1], (3, SHELL_LAYERS, SHEET_ZONES_EAST, SHEET_ZONES_NORTH), jnp.float32, -1.0, 1.0) * shard_levels(seeds[1], (3, SHELL_LAYERS, SHEET_ZONES_EAST, SHEET_ZONES_NORTH), ((2, 8), (3, 16)), -0.4, 0.0), -1.0, 1.0)
    source_matrix = noise(seeds[2], (PLASMA_QUANTITY, PLASMA_QUANTITY), PLASMA_QUANTITY ** -0.5, 2.0, (), jnp.float32)
    pedersen = jnp.clip(jnp.exp(math.log(1.0) - 2.9957323 * jax.random.uniform(seeds[3], (NLAT, NLON), jnp.float32) ** shard_levels(seeds[3], (NLAT, NLON), ((0, 8), (1, 16)), -0.2, 0.2)), 0.05, 1.0)
    owners_keys = jax.random.split(jax.random.fold_in(seeds[4], 1), BBLOCKS // BB_DEV)
    owners_turns = jax.random.permutation(jax.random.fold_in(seeds[4], 3), BBLOCKS // BB_DEV)
    owners = jax.vmap(lambda own, number: routed_block(jax.random.fold_in(seeds[4], 2), own, number, BB_DEV, N_BLK * N_INNER, 1, CAP, 2))(owners_keys, owners_turns).reshape((BBLOCKS, 1))
    tile_positions = plant(jax.random.randint(seeds[5], (BBLOCKS,), 0, TILES_DEV), jax.random.fold_in(seeds[5], 1), 0, TILES_DEV - 1).astype(jnp.int32)
    return dict(sheet_plasma_quantities=sheet_plasma_quantities, speeds=speeds, source_matrix=source_matrix, pedersen=pedersen, owners=owners, tile_positions=tile_positions)


time_step = 0.3
screening = 2.0
potential_gain = 4096.0
highest = lax.Precision.HIGHEST

def legendre_tables(degree_count, order_count):
    degree = jnp.arange(degree_count, dtype=jnp.int32).astype(jnp.float32)[:, None]
    orders_of = jnp.arange(order_count, dtype=jnp.int32).astype(jnp.float32)[None, :]
    is_above = degree > orders_of
    spread = jnp.where(is_above, degree * degree - orders_of * orders_of, 1.0)
    numerator = jnp.where(is_above, 4.0 * degree * degree - 1.0, 1.0)
    ratio_up = jnp.where(is_above, jnp.sqrt(numerator / spread), 0.0)
    shifted = jnp.concatenate([jnp.ones((1, order_count), jnp.float32), ratio_up[:-1]], axis=0)
    beyond = degree >= orders_of + 2.0
    ratio_down = jnp.where(beyond, ratio_up / jnp.where(beyond, shifted, 1.0), 0.0)
    start_mask = jnp.where(degree == orders_of, 1.0, 0.0)
    counter = jnp.arange(1, order_count, dtype=jnp.int32).astype(jnp.float32)
    log_start = 0.5 * jnp.log(jnp.float32(0.5)) + jnp.concatenate([jnp.zeros(1, jnp.float32), jnp.cumsum(0.5 * jnp.log((2.0 * counter + 1.0) / (2.0 * counter)))])
    return (ratio_up, ratio_down, start_mask, log_start)

def recur(previous, older, ratio_row, down_row, start_row, starting, cosine):
    return start_row[:, None] * starting + ratio_row[:, None] * cosine[None, :] * previous - down_row[:, None] * older

def fourier_rows(first_row, row_count, first_col, col_count, lon_total):
    row_ids = first_row + jnp.arange(row_count, dtype=jnp.int32)
    orders_of = row_ids // 2
    parity = row_ids % 2
    col_ids = first_col + jnp.arange(col_count, dtype=jnp.int32)
    phase_int = orders_of[:, None] * col_ids[None, :] % lon_total
    phase_angle = phase_int.astype(jnp.float32) * (2.0 * math.pi / lon_total)
    return (orders_of, parity, phase_angle)

def analysis_basis(parity, phase_angle, lon_total):
    return jnp.where(parity[:, None] == 0, jnp.cos(phase_angle), jnp.sin(phase_angle)) / lon_total

def synthesis_basis(orders_of, parity, phase_angle):
    weight = jnp.where(orders_of == 0, 1.0, 2.0)
    cosines = jnp.cos(phase_angle)
    sine_rows = jnp.sin(phase_angle)
    values_of = jnp.where(parity[:, None] == 0, cosines, sine_rows) * weight[:, None]
    slopes_of = jnp.where(parity[:, None] == 0, -sine_rows, cosines) * (orders_of.astype(jnp.float32) * weight)[:, None]
    return (values_of, slopes_of)

def advance_slab(grown_field, speeds, source_matrix):
    centre = grown_field[:, :, 1:-1, 1:-1]
    along_x = speeds[0][None] * grown_field
    faces_x = 0.5 * (along_x[:, :, :-1] + along_x[:, :, 1:]) - 0.5 * (grown_field[:, :, 1:] - grown_field[:, :, :-1])
    change_x = (faces_x[:, :, 1:] - faces_x[:, :, :-1])[:, :, :, 1:-1]
    along_y = speeds[1][None] * grown_field
    faces_y = 0.5 * (along_y[:, :, :, :-1] + along_y[:, :, :, 1:]) - 0.5 * (grown_field[:, :, :, 1:] - grown_field[:, :, :, :-1])
    change_y = (faces_y[:, :, :, 1:] - faces_y[:, :, :, :-1])[:, :, 1:-1]
    z_padding = ((0, 0), (1, 1), (0, 0), (0, 0))
    padded_z = jnp.pad(centre, z_padding)
    along_z = jnp.pad(speeds[2][:, 1:-1, 1:-1][None] * centre, z_padding)
    faces_z = 0.5 * (along_z[:, :-1] + along_z[:, 1:]) - 0.5 * (padded_z[:, 1:] - padded_z[:, :-1])
    change_z = faces_z[:, 1:] - faces_z[:, :-1]
    mixing = jnp.einsum('vw,wzxy->vzxy', source_matrix, centre, precision=highest)
    return centre - time_step * (change_x + change_y + change_z) + time_step * mixing

def joule(potential, above_rows, below_rows, azimuthal, row_global, sine, pedersen, rows_total):
    spacing = 2.0 / rows_total
    central = (above_rows - below_rows) / (2.0 * spacing)
    lower_edge = (above_rows - potential) / spacing
    upper_edge = (potential - below_rows) / spacing
    slope_x = jnp.where((row_global == 0)[:, None], lower_edge, jnp.where((row_global == rows_total - 1)[:, None], upper_edge, central))
    polar_field = sine[:, None] * slope_x
    eastward = azimuthal / sine[:, None]
    return pedersen * (polar_field * polar_field + eastward * eastward)

def reference(sheet_plasma_quantities, speeds, source_matrix, pedersen, owners, tile_positions):
    border_width = ((0, 0), (0, 0), (1, 1), (1, 1))
    bordered_speeds = jnp.pad(speeds, border_width)
    updated_plasma_quantities = sheet_plasma_quantities
    for sweep_index in range(STEPS):
        updated_plasma_quantities = advance_slab(jnp.pad(updated_plasma_quantities, border_width), bordered_speeds, source_matrix)
    current_solution = updated_plasma_quantities[PLASMA_QUANTITY - 1, 1] - updated_plasma_quantities[PLASMA_QUANTITY - 1, 0]
    block_faces = current_solution.reshape(N_BLK, CX // BLOCK, BLOCK, N_INNER, CY // BLOCK, BLOCK)
    block_faces = block_faces.transpose(0, 3, 1, 4, 2, 5).reshape(BBLOCKS, BLOCK * BLOCK)
    tile_rows = LAT_DEV // BLOCK
    tile_cols = LON_DEV // BLOCK
    target = owners[:, 0] * TILES_DEV + tile_positions
    deposits = jax.ops.segment_sum(block_faces, target, num_segments=N_BLK * N_INNER * TILES_DEV)
    forcing = deposits.reshape(N_BLK, N_INNER, tile_rows, tile_cols, BLOCK, BLOCK)
    forcing = forcing.transpose(0, 2, 4, 1, 3, 5).reshape(NLAT, NLON)
    orders_of, parity, phase_angle = fourier_rows(0, 2 * MORD, 0, NLON, NLON)
    analysis = analysis_basis(parity, phase_angle, NLON)
    spectrum = lax.dot_general(analysis, forcing, (((1,), (1,)), ((), ())), precision=highest)
    spectrum = spectrum.reshape(MORD, 2, NLAT)
    spacing = 2.0 / NLAT
    row_global = jnp.arange(NLAT, dtype=jnp.int32)
    cosine = -1.0 + (2.0 * row_global.astype(jnp.float32) + 1.0) / NLAT
    sine = jnp.sqrt(1.0 - cosine * cosine)
    ratio_up, ratio_down, start_mask, log_start = legendre_tables(LDEG, MORD)
    order_float = jnp.arange(MORD, dtype=jnp.int32).astype(jnp.float32)
    starting = jnp.exp(log_start[:, None] + order_float[:, None] * jnp.log(sine)[None, :])
    rows_table = (ratio_up, ratio_down, start_mask)
    empty = jnp.zeros((MORD, NLAT), jnp.float32)

    def forward(carry, table_rows):
        previous, older = carry
        present = recur(previous, older, table_rows[0], table_rows[1], table_rows[2], starting, cosine)
        return ((present, previous), spacing * lax.optimization_barrier(jnp.sum(present[:, None, :] * spectrum, axis=2)))
    final_pair, coefficients = lax.scan(forward, (empty, empty), rows_table)
    degree_float = jnp.arange(LDEG, dtype=jnp.int32).astype(jnp.float32)
    solved = potential_gain * coefficients / (degree_float * (degree_float + 1.0) + screening)[:, None, None]

    def backward(carry, inputs):
        previous, older, running = carry
        present = recur(previous, older, inputs[0], inputs[1], inputs[2], starting, cosine)
        return ((present, previous, running + present[:, None, :] * inputs[3][:, :, None]), None)
    zero_total = jnp.zeros((MORD, 2, NLAT), jnp.float32)
    final_state, unused = lax.scan(backward, (empty, empty, zero_total), rows_table + (solved,))
    synthesis = final_state[2].reshape(2 * MORD, NLAT)
    values_of, slopes_of = synthesis_basis(orders_of, parity, phase_angle)
    potential = lax.dot_general(synthesis, values_of, (((0,), (0,)), ((), ())), precision=highest)
    azimuthal = lax.dot_general(synthesis, slopes_of, (((0,), (0,)), ((), ())), precision=highest)
    zero_row = jnp.zeros((1, NLON), jnp.float32)
    above_rows = jnp.concatenate([potential[1:], zero_row], axis=0)
    below_rows = jnp.concatenate([zero_row, potential[:-1]], axis=0)
    heating = joule(potential, above_rows, below_rows, azimuthal, row_global, sine, pedersen, NLAT)

    def to_tiles(grid):
        shaped = grid.reshape(N_BLK, tile_rows, BLOCK, N_INNER, tile_cols, BLOCK)
        return shaped.transpose(0, 3, 1, 4, 2, 5).reshape(N_BLK * N_INNER * TILES_DEV, BLOCK * BLOCK)
    block_potential_heat = jnp.concatenate([to_tiles(potential)[target], to_tiles(heating)[target]], axis=1)
    return (updated_plasma_quantities, potential, heating, block_potential_heat)
```

```python
import functools
import math

import jax
import jax.numpy as jnp
import numpy as np
from jax import lax
from jax.experimental import pallas as pl
from jax.experimental.pallas import tpu as pltpu
from jax.sharding import PartitionSpec as P

F32 = jnp.float32
BF16 = jnp.bfloat16
I32 = jnp.int32
MESH = pl.DeviceIdType.MESH
BLOCK = 8
PAIRS = 8
SCREENING = 2.0
GAIN = 4096.0


def iota(shape, dim):
    return lax.broadcasted_iota(I32, shape, dim)


def split(value):
    high = value.astype(BF16)
    return high, (value - high.astype(F32)).astype(BF16)


def split3(value):
    high = value.astype(BF16)
    rest = value - high.astype(F32)
    middle = rest.astype(BF16)
    return high, middle, (rest - middle.astype(F32)).astype(BF16)


def dot(left, right, dims=((1,), (0,))):
    return lax.dot_general(left, right, (dims, ((), ())), preferred_element_type=F32)


def dot3(left, right, dims):
    lh, ll = left
    rh, rl = right
    return dot(lh, rh, dims) + dot(ll, rh, dims) + dot(lh, rl, dims)


def spectral_tables(blk_count, inner_count, lat_dev, lon_dev):
    orders = PAIRS * 2 * inner_count
    degrees = orders
    lon_total = lon_dev * inner_count
    first = np.arange(inner_count * PAIRS).reshape(inner_count, 1, PAIRS)
    order_of = np.concatenate([first, orders - 1 - first], axis=1).reshape(-1)
    cols = np.arange(lon_dev)
    phase = (order_of[:, None] * cols[None, :] % lon_total) * (2.0 * math.pi / lon_total)
    wave = np.stack([np.cos(phase), np.sin(phase)]).astype(np.float32)
    turn = (order_of[:, None] * (np.arange(inner_count) * lon_dev)[None, :] % lon_total) * (
        2.0 * math.pi / lon_total
    )
    twiddle = np.zeros((order_of.shape[0], 128), np.float32)
    twiddle[:, :inner_count] = np.cos(turn)
    twiddle[:, 32 : 32 + inner_count] = np.sin(turn)
    twiddle[:, 64] = order_of
    twiddle[:, 65] = np.where(order_of == 0, 1.0, 2.0)

    turns = -(-(degrees + 1) // 16)
    steps = turns * 16
    table = np.zeros((inner_count, turns + 1, PAIRS, 128), np.float32)

    def up(degree, order):
        return np.sqrt(
            np.float32(4.0 * degree * degree - 1.0) / np.float32(degree * degree - order * order)
        )

    counter = np.arange(1, orders, dtype=np.float64)
    log_start = 0.5 * np.log(0.5) + np.concatenate(
        [np.zeros(1), np.cumsum(0.5 * np.log((2.0 * counter + 1.0) / (2.0 * counter)))]
    )
    for pair in range(inner_count * PAIRS):
        place, lane = divmod(pair, PAIRS)
        low, partner = pair, orders - 1 - pair
        table[place, turns, lane, :4] = [low, log_start[low], partner, log_start[partner]]
        for step in range(degrees + 1):
            if step <= low:
                order, degree, kind = partner, partner + step, 3
            else:
                order, degree, kind = low, step - 1, 2
            turn_at, offset = divmod(step, 16)
            if degree == order:
                table[place, turn_at, lane, kind * 16 + offset] = 1.0
                continue
            ratio = up(degree, order)
            table[place, turn_at, lane, offset] = ratio
            if degree >= order + 2:
                table[place, turn_at, lane, 16 + offset] = ratio / up(degree - 1, order)
    return wave, twiddle, table, steps


def kernel(
    sizes,
    u_ref,
    w_ref,
    mix_ref,
    ped_ref,
    owner_ref,
    tile_ref,
    wave_ref,
    twiddle_ref,
    table_ref,
    out_ref,
    pot_ref,
    heat_ref,
    blocks_ref,
    coef,
    u1,
    edge_send_x,
    edge_send_y,
    edge_recv_x,
    edge_recv_y,
    turned,
    sel_t,
    label_ref,
    face_send,
    face_recv,
    forcing,
    base_ref,
    values_ref,
    spec_send,
    spec_recv,
    ratios,
    leg,
    mask_ref,
    coef_send,
    coef_recv,
    syn_all,
    rim_recv,
    grids,
    wide,
    reply_send,
    reply_recv,
    edge_sems,
    send_sems,
    recv_sems,
    rim_sems,
    local_sem,
):
    na, nb, steps = sizes
    count = na * nb
    lat, lon = ped_ref.shape
    rows_total, cols_total = lat * na, lon * nb
    cap = face_send.shape[1]
    slots = count * cap
    a, b = lax.axis_index("blk"), lax.axis_index("inner")
    me = a * nb + b
    orders = PAIRS * 2 * nb
    spec_rows = 2 * orders

    def remote(src, dst, send_sem, recv_sem, device):
        pltpu.make_async_remote_copy(
            src_ref=src,
            dst_ref=dst,
            send_sem=send_sem,
            recv_sem=recv_sem,
            device_id=device,
            device_id_type=MESH,
        ).start()

    def take(ref, sem):
        pltpu.make_async_copy(ref, ref, sem).wait()

    up_a, down_a = lax.rem(a + 1, na), lax.rem(a + na - 1, na)
    up_b, down_b = lax.rem(b + 1, nb), lax.rem(b + nb - 1, nb)

    barrier = pltpu.get_barrier_semaphore()

    def greet(offset, carry):
        peer = lax.rem(me + offset, count)
        pl.semaphore_signal(
            barrier, inc=1, device_id=(peer // nb, lax.rem(peer, nb)), device_id_type=MESH
        )
        return carry

    lax.fori_loop(1, count, greet, 0)
    fetch = pltpu.make_async_copy(table_ref.at[b], ratios, local_sem)
    fetch.start()

    row = iota((128, 128), 0)
    lane = iota((128, 128), 1)
    mixing = [
        [0.3 * mix_ref[v, w] + (0.1 if v == w else 0.0) for w in range(8)] for v in range(8)
    ]

    def make_coef(z, carry):
        wx, wy = 0.15 * w_ref[0, z], 0.15 * w_ref[1, z]
        coef[0, z] = jnp.where(row == 127, 0.0, 0.15 + wx)
        coef[1, z] = jnp.where(row == 0, 0.0, 0.15 - wx)
        coef[2, z] = jnp.where(lane == 127, 0.0, 0.15 + wy)
        coef[3, z] = jnp.where(lane == 0, 0.0, 0.15 - wy)
        below = 0.15 + 0.15 * w_ref[2, jnp.maximum(z - 1, 0)]
        above = 0.15 - 0.15 * w_ref[2, jnp.minimum(z + 1, 3)]
        coef[4, z] = jnp.where(z > 0, below, 0.0)
        coef[5, z] = jnp.where(z < 3, above, 0.0)
        coef[6, z] = jnp.where(lane == 0, 0.15 - wy, 0.15 + wy)
        return carry

    lax.fori_loop(0, 4, make_coef, 0)

    def make_edges(src, sweep):
        for v in range(8):
            for z in range(4):
                j = v * 4 + z
                last = (0.15 + 0.15 * w_ref[0, z, 120:128, :]) * src[v, z, 120:128, :]
                first = (0.15 - 0.15 * w_ref[0, z, 0:8, :]) * src[v, z, 0:8, :]
                edge_send_x[sweep, 0, j : j + 1, :] = last[7:8, :]
                edge_send_x[sweep, 1, j : j + 1, :] = first[0:1, :]

        def pack(j, packed):
            rolled = pltpu.roll(coef[6, lax.rem(j, 4)] * src[j // 4, lax.rem(j, 4)], 2 * j + 1, 1)
            return jnp.where((lane == 2 * j) | (lane == 2 * j + 1), rolled, packed)

        turned[...] = lax.fori_loop(0, 32, pack, jnp.zeros((128, 128), F32)).T
        edge_send_y[sweep, 0] = turned[pl.ds(0, 32, stride=2), :]
        edge_send_y[sweep, 1] = turned[pl.ds(1, 32, stride=2), :]

    def send_edges(sweep):
        for side, device in ((0, (up_a, b)), (1, (down_a, b))):
            at = sweep * 4 + side
            remote(
                edge_send_x.at[sweep, side],
                edge_recv_x.at[sweep, side],
                edge_sems.at[0, at],
                edge_sems.at[1, at],
                device,
            )
        for side, device in ((0, (a, up_b)), (1, (a, down_b))):
            at = sweep * 4 + 2 + side
            remote(
                edge_send_y.at[sweep, side],
                edge_recv_y.at[sweep, side],
                edge_sems.at[0, at],
                edge_sems.at[1, at],
                device,
            )

    def wait_edges(sweep):
        for side in range(2):
            take(edge_recv_x.at[sweep, side], edge_sems.at[1, sweep * 4 + side])
            take(edge_recv_y.at[sweep, side], edge_sems.at[1, sweep * 4 + 2 + side])
        turned[...] = jnp.zeros((128, 128), F32)
        turned[pl.ds(0, 32, stride=2), :] = jnp.where(b < nb - 1, edge_recv_y[sweep, 1], 0.0)
        turned[pl.ds(1, 32, stride=2), :] = jnp.where(b > 0, edge_recv_y[sweep, 0], 0.0)
        turned[...] = turned[...].T

    def advance(src, dst, v, z):
        u = src[v, z]
        total = mixing[v][0] * src[0, z]
        for w in range(1, 8):
            total = total + mixing[v][w] * src[w, z]
        total = total + pltpu.roll(coef[0, z] * u, 1, 0) + pltpu.roll(coef[1, z] * u, 127, 0)
        total = total + pltpu.roll(coef[2, z] * u, 1, 1) + pltpu.roll(coef[3, z] * u, 127, 1)
        total = total + coef[4, z] * src[v, jnp.maximum(z - 1, 0)]
        total = total + coef[5, z] * src[v, jnp.minimum(z + 1, 3)]
        dst[v, z] = total

    def mend(dst, sweep, v, z):
        j = v * 4 + z
        rolled = pltpu.roll(turned[...], 127 - 2 * j, 1)
        dst[v, z] = dst[v, z] + jnp.where((lane == 0) | (lane == 127), rolled, 0.0)
        row8 = iota((8, 128), 0)
        from_down = jnp.where(a > 0, edge_recv_x[sweep, 0, pl.ds(j, 1), :], 0.0)
        from_up = jnp.where(a < na - 1, edge_recv_x[sweep, 1, pl.ds(j, 1), :], 0.0)
        dst[v, z, 0:8, :] = dst[v, z, 0:8, :] + jnp.where(row8 == 0, from_down, 0.0)
        dst[v, z, 120:128, :] = dst[v, z, 120:128, :] + jnp.where(row8 == 7, from_up, 0.0)

    make_edges(u_ref, 0)
    pl.semaphore_wait(barrier, count - 1)
    send_edges(0)

    def first_step(z, carry):
        for v in range(8):
            advance(u_ref, u1, v, z)
        return carry

    lax.fori_loop(0, 4, first_step, 0)

    owner = owner_ref[...]
    owner_hot = jnp.where(iota((256, 128), 1) == owner, 1.0, 0.0)
    earlier = jnp.where(iota((256, 256), 0) > iota((256, 256), 1), 1.0, 0.0).astype(BF16)
    before = dot(earlier, owner_hot.astype(BF16))
    rank = jnp.sum(before * owner_hot, axis=1, keepdims=True)
    slot = owner.astype(F32) * float(cap) + rank
    slot_row = jnp.broadcast_to(slot, (256, 128)).T[0:1, :]
    sel = jnp.where(iota((slots, 256), 0).astype(F32) == slot_row, 1.0, 0.0).astype(BF16)
    flip = jnp.where(iota((256, 256), 0) == (iota((256, 256), 1) ^ 7), 1.0, 0.0).astype(BF16)
    sel_t[...] = dot(sel, flip).astype(BF16)
    tile_high, tile_low = split(jnp.broadcast_to(tile_ref[...].astype(F32), (256, 128)))
    label_ref[...] = dot(sel, tile_high) + dot(sel, tile_low)

    wait_edges(0)

    def first_mend(j, carry):
        mend(u1, 0, j // 4, lax.rem(j, 4))
        return carry

    lax.fori_loop(0, 32, first_mend, 0)
    make_edges(u1, 1)
    send_edges(1)
    for z in (0, 1):
        advance(u1, out_ref, 7, z)
    wait_edges(1)
    for z in (0, 1):
        mend(out_ref, 1, 7, z)
    current = out_ref[7, 1] - out_ref[7, 0]

    halves = [pltpu.roll(current, 64, 1).reshape(16, 8, 128), current.reshape(16, 8, 128)]
    group = iota((16, 8, 128), 2) // 8
    faces = []
    for half in range(2):
        face = jnp.zeros((16, 8, 128), F32)
        for r in range(8):
            spread = jnp.broadcast_to(halves[half][:, r : r + 1, :], (16, 8, 128))
            moved = pltpu.roll(spread, 8 * r + 8, 2, stride=8, stride_axis=1)
            face = jnp.where(group == r, moved, face)
        faces.append(face)
    faces = jnp.stack(faces, axis=1).reshape(256, 128)
    face_high, face_low = split(faces)
    routed = dot(sel_t[...], face_high) + dot(sel_t[...], face_low)
    lane_slot = iota((slots, 128), 1)
    routed = jnp.where(lane_slot < 64, routed, label_ref[...])
    face_send[...] = routed.reshape(count, cap, 128)

    def send_all(src, dst, at):
        def one(offset, carry):
            peer = lax.rem(me + offset, count)
            remote(
                src.at[peer],
                dst.at[me],
                send_sems.at[at],
                recv_sems.at[at],
                (peer // nb, lax.rem(peer, nb)),
            )
            return carry

        lax.fori_loop(1, count, one, 0)
        dst[me] = src[me]

    send_all(face_send, face_recv, 0)

    def second_step(z, carry):
        for v in range(7):
            advance(u1, out_ref, v, z)
        return carry

    lax.fori_loop(0, 4, second_step, 0)
    for z in (2, 3):
        advance(u1, out_ref, 7, z)

    def second_mend(j, carry):
        mend(out_ref, 1, j // 4, lax.rem(j, 4))
        return carry

    lax.fori_loop(0, 28, second_mend, 0)
    for z in (2, 3):
        mend(out_ref, 1, 7, z)

    def per_row(column):
        picked = jnp.sum(
            jnp.where(iota((orders, 128), 1) == column, twiddle_ref[...], 0.0),
            axis=1,
            keepdims=True,
        )
        return picked

    cos_turn, sin_turn = per_row(b), per_row(b + 32)
    order_col, weight_col = per_row(64), per_row(65)
    cos_wave, sin_wave = wave_ref[0], wave_ref[1]
    cosine = (cos_turn * cos_wave - sin_turn * sin_wave).reshape(nb, 2, 1, PAIRS, lon)
    sine = (sin_turn * cos_wave + cos_turn * sin_wave).reshape(nb, 2, 1, PAIRS, lon)

    def rows_of(even, odd):
        return jnp.concatenate([even, odd], axis=2).reshape(spec_rows, lon)

    base = rows_of(cosine, sine)
    base_high, base_low = split(base * (1.0 / cols_total))
    base_ref[0] = base_high
    base_ref[1] = base_low
    weight = weight_col.reshape(nb, 2, 1, PAIRS, 1)
    slope_weight = (weight_col * order_col).reshape(nb, 2, 1, PAIRS, 1)
    value_high, value_low = split(rows_of(cosine * weight, sine * weight))
    values_ref[0, :, 0:lon] = value_high
    values_ref[1, :, 0:lon] = value_low
    slope_high, slope_low = split(rows_of(-sine * slope_weight, cosine * slope_weight))
    values_ref[0, :, lon : 2 * lon] = slope_high
    values_ref[1, :, lon : 2 * lon] = slope_low

    take(face_recv.at[pl.ds(0, count - 1)], recv_sems.at[0])
    got = face_recv[...].reshape(slots, 128)
    swapped = pltpu.roll(got, 64, 1)
    label = jnp.where(lane_slot < 64, swapped, got).astype(I32)
    face = jnp.where(lane_slot < 64, got, swapped)
    tile_row, tile_col = label >> 5, label & 31
    tile_row_t = tile_row.astype(F32).T.astype(I32)
    scatter = jnp.where(iota((32, slots), 0) == tile_row_t[0:32, :], 1.0, 0.0).astype(BF16)
    scatter = jnp.concatenate([scatter, scatter], axis=1)
    col_masks = [
        jnp.where((lane_slot >> 3) + 16 * half == tile_col, 1.0, 0.0).astype(BF16)
        for half in range(2)
    ]

    def spread_bit(value, width):
        moved = pltpu.roll(value, width, 1)
        bit = (lane_slot & width) == 0
        return [jnp.where(bit, value, moved), jnp.where(bit, moved, value)]

    lines = [face]
    for width in (32, 16, 8):
        lines = [part for line in lines for part in spread_bit(line, width)]
    for r in range(8):
        line_high, line_low = split(lines[r])
        right = jnp.concatenate(
            [
                jnp.concatenate([part * mask for mask in col_masks], axis=1)
                for part in (line_high, line_low)
            ],
            axis=0,
        )
        rows = dot(scatter, right)
        forcing[0, pl.ds(r, 32, stride=8), :] = rows[:, 0:128]
        forcing[1, pl.ds(r, 32, stride=8), :] = rows[:, 128:256]

    force = split(jnp.concatenate([forcing[0], forcing[1]], axis=1))
    spectrum = dot3((base_ref[0], base_ref[1]), force, ((1,), (1,)))
    spec_send[...] = spectrum.reshape(nb, 4 * PAIRS, lat)

    def send_chunk(offset, carry):
        peer = lax.rem(b + offset, nb)
        remote(
            spec_send.at[peer], spec_recv.at[b], send_sems.at[1], recv_sems.at[1], (a, peer)
        )
        return carry

    lax.fori_loop(1, nb, send_chunk, 0)
    spec_recv[b] = spec_send[b]

    fetch.wait()
    row_of_lane = a * lat + iota((PAIRS, lat), 1)
    x = -1.0 + (2.0 * row_of_lane.astype(F32) + 1.0) / rows_total
    log_sine = jnp.log(jnp.sqrt(1.0 - x * x))
    turns = steps // 16
    heads = ratios[turns]
    low_start = jnp.exp(heads[:, 1:2] + heads[:, 0:1] * log_sine)
    high_start = jnp.exp(heads[:, 3:4] + heads[:, 2:3] * log_sine)

    def build(turn, carry):
        previous, older = carry
        block = ratios[turn]
        made = []
        for offset in range(16):
            up = block[:, offset : offset + 1]
            down = block[:, 16 + offset : 17 + offset]
            begin_low = block[:, 32 + offset : 33 + offset]
            begin_high = block[:, 48 + offset : 49 + offset]
            present = (
                begin_low * low_start + begin_high * high_start + up * x * previous - down * older
            )
            made.append(present)
            older, previous = previous, present
        where = pl.ds(pl.multiple_of(turn * 128, 128), 128)
        for at, part in enumerate(split3(jnp.concatenate(made, axis=0))):
            leg[at, where, :] = part
        return previous, older

    empty = jnp.zeros((PAIRS, lat), F32)
    lax.fori_loop(0, turns, build, (empty, empty))

    width = steps * PAIRS
    at_step = iota((PAIRS, width), 1) // PAIRS
    at_pair = lax.rem(iota((PAIRS, width), 1), PAIRS)
    order_low = b * PAIRS + at_pair
    is_high = at_step <= order_low
    degree = jnp.where(is_high, orders - 1 - order_low + at_step, at_step - 1).astype(F32)
    scale = (2.0 / rows_total) * GAIN / (degree * (degree + 1.0) + SCREENING)
    scale = jnp.where(at_step <= orders, scale, 0.0)
    mine = at_pair == iota((PAIRS, width), 0)
    mask_ref[0] = jnp.where(mine & jnp.logical_not(is_high), scale, 0.0)
    mask_ref[1] = jnp.where(mine & is_high, scale, 0.0)

    take(spec_recv.at[pl.ds(0, nb - 1)], recv_sems.at[1])
    spec = spec_recv[0]
    for at in range(1, nb):
        spec = spec + spec_recv[at]
    spec_high, spec_low = split(spec)
    both = dot(jnp.concatenate([spec_high, spec_low], axis=0), leg[0], ((1,), (1,)))
    wide_sums = both[0:32] + both[32:64] + dot(spec_high, leg[1], ((1,), (1,)))
    for parity in range(2):
        low_rows = wide_sums[parity * 8 : parity * 8 + 8]
        high_rows = wide_sums[16 + parity * 8 : 24 + parity * 8]
        kept = low_rows * mask_ref[0] + high_rows * mask_ref[1]
        coef_send[parity : parity + 1, :] = jnp.sum(kept, axis=0, keepdims=True)

    def send_coef(offset, carry):
        peer = lax.rem(a + offset, na)
        remote(coef_send, coef_recv.at[a], send_sems.at[2], recv_sems.at[2], (peer, b))
        return carry

    lax.fori_loop(1, na, send_coef, 0)
    coef_recv[a] = coef_send[...]
    take(coef_recv.at[pl.ds(0, na - 1)], recv_sems.at[2])
    solved = coef_recv[0]
    for at in range(1, na):
        solved = solved + coef_recv[at]
    expanded = []
    for kind in range(2):
        for parity in range(2):
            expanded.append(
                jnp.where(
                    mask_ref[kind] != 0.0,
                    jnp.broadcast_to(solved[parity : parity + 1, :], (PAIRS, width)),
                    0.0,
                )
            )
    solved_high, solved_low = split(jnp.concatenate(expanded, axis=0))
    solved_both = jnp.concatenate([solved_high, solved_low], axis=0)
    fine = dot(solved_high, leg[2])
    both = dot(solved_both, leg[0])
    middle = dot(solved_both, leg[1])
    syn_all[b] = both[0:32] + (both[32:64] + (middle[0:32] + (middle[32:64] + fine)))

    def send_syn(offset, carry):
        peer = lax.rem(b + offset, nb)
        remote(syn_all.at[b], syn_all.at[b], send_sems.at[3], recv_sems.at[3], (a, peer))
        return carry

    lax.fori_loop(1, nb, send_syn, 0)
    take(syn_all.at[pl.ds(0, nb - 1)], recv_sems.at[3])

    syn_high, syn_middle, syn_low = split3(syn_all[...].reshape(spec_rows, lat).T)
    syn_three = jnp.concatenate([syn_high, syn_middle, syn_low], axis=0)
    syn_two = jnp.concatenate([syn_high, syn_middle], axis=0)
    coarse = dot(syn_three, values_ref[0, :, 0:lon])
    rest = dot(syn_two, values_ref[1, :, 0:lon])
    pot_ref[...] = coarse[0:lat] + (
        coarse[lat : 2 * lat] + (rest[0:lat] + (coarse[2 * lat :] + rest[lat:]))
    )
    remote(pot_ref.at[pl.ds(lat - 8, 8)], rim_recv.at[0], rim_sems.at[0, 0], rim_sems.at[1, 0], (up_a, b))
    remote(pot_ref.at[pl.ds(0, 8)], rim_recv.at[1], rim_sems.at[0, 1], rim_sems.at[1, 1], (down_a, b))
    turned_slopes = dot(syn_two, values_ref[0, :, lon : 2 * lon])
    azimuthal = turned_slopes[0:lat] + (
        turned_slopes[lat:] + dot(syn_high, values_ref[1, :, lon : 2 * lon])
    )
    grid_row = iota((lat, 1), 0)
    global_row = a * lat + grid_row
    x_col = -1.0 + (2.0 * global_row.astype(F32) + 1.0) / rows_total
    sine_col = jnp.sqrt(1.0 - x_col * x_col)
    eastward = azimuthal / sine_col
    potential = pot_ref[...]
    take(rim_recv.at[0], rim_sems.at[1, 0])
    take(rim_recv.at[1], rim_sems.at[1, 1])
    above = jnp.where(grid_row == lat - 1, rim_recv[1, 0:1, :], pltpu.roll(potential, lat - 1, 0))
    below = jnp.where(grid_row == 0, rim_recv[0, 7:8, :], pltpu.roll(potential, 1, 0))
    inverse = rows_total / 2.0
    at_first, at_last = global_row == 0, global_row == rows_total - 1
    slope = (jnp.where(at_last, potential, above) - jnp.where(at_first, potential, below)) * (
        jnp.where(at_first | at_last, inverse, 0.5 * inverse)
    )
    polar = sine_col * slope
    heating = ped_ref[...] * (polar * polar + eastward * eastward)
    heat_ref[...] = heating

    grids[0] = potential[:, 0:128]
    grids[1] = potential[:, 128:256]
    grids[2] = heating[:, 0:128]
    grids[3] = heating[:, 128:256]
    pick = iota((slots, 128), 1)
    pick = jnp.where((pick < 96) & ((pick & 31) == tile_row), 1.0, 0.0).astype(BF16)
    bits = [(tile_col & (1 << at)) != 0 for at in range(5)]
    upper = lane_slot >= 64
    for r in range(8):
        rows = jnp.concatenate([grids[at, pl.ds(r, 32, stride=8), :] for at in range(4)], axis=1)
        high, middle, low = split3(rows)
        parts = jnp.concatenate([high, middle, low, jnp.zeros_like(low)], axis=0)
        picked = dot(pick, parts)
        pot = jnp.where(bits[4], picked[:, 128:256], picked[:, 0:128])
        heat = jnp.where(bits[4], picked[:, 384:512], picked[:, 256:384])
        wide[r] = jnp.where(
            upper,
            jnp.where(bits[3], heat, pltpu.roll(heat, 64, 1)),
            jnp.where(bits[3], pltpu.roll(pot, 64, 1), pot),
        )

    def join(first, second, at):
        width = 8 << at
        return jnp.where(
            (lane_slot & width) == 0,
            jnp.where(bits[at], pltpu.roll(first, 128 - width, 1), first),
            jnp.where(bits[at], second, pltpu.roll(second, width, 1)),
        )

    quads = [join(wide[r], wide[r + 4], 2) for r in range(4)]
    twos = [join(quads[r], quads[r + 2], 1) for r in range(2)]
    reply_send[...] = join(twos[0], twos[1], 0).reshape(count, cap, 128)
    send_all(reply_send, reply_recv, 4)

    owner_back = owner_ref[...]
    hot_back = jnp.where(iota((256, 128), 1) == owner_back, 1.0, 0.0)
    rank_back = jnp.sum(dot(earlier, hot_back.astype(BF16)) * hot_back, axis=1, keepdims=True)
    slot_back = owner_back.astype(F32) * float(cap) + rank_back
    chosen = jnp.where(iota((256, slots), 1).astype(F32) == slot_back, 1.0, 0.0).astype(BF16)
    take(reply_recv.at[pl.ds(0, count - 1)], recv_sems.at[4])
    back_high, back_low = split(reply_recv[...].reshape(slots, 128))
    blocks_ref[...] = dot(chosen, back_high) + dot(chosen, back_low)

    for sweep in range(2):
        for side in range(2):
            take(edge_send_x.at[sweep, side], edge_sems.at[0, sweep * 4 + side])
            take(edge_send_y.at[sweep, side], edge_sems.at[0, sweep * 4 + 2 + side])
    take(face_send.at[pl.ds(0, count - 1)], send_sems.at[0])
    take(spec_send.at[pl.ds(0, nb - 1)], send_sems.at[1])
    take(coef_recv.at[pl.ds(0, na - 1)], send_sems.at[2])
    take(syn_all.at[pl.ds(0, nb - 1)], send_sems.at[3])
    take(reply_send.at[pl.ds(0, count - 1)], send_sems.at[4])
    take(rim_recv.at[0], rim_sems.at[0, 0])
    take(rim_recv.at[1], rim_sems.at[0, 1])


def solution(mesh):
    na, nb = mesh.shape["blk"], mesh.shape["inner"]
    count = na * nb

    def shards(slab, speeds, source_matrix, pedersen, owners, tile_positions):
        lat, lon = pedersen.shape
        blocks = owners.shape[0]
        cap = max(2, 2 * blocks // count)
        slots = count * cap
        orders = PAIRS * 2 * nb
        wave, twiddle, table, steps = spectral_tables(na, nb, lat, lon)
        width = steps * PAIRS
        vmem = pl.BlockSpec(memory_space=pltpu.VMEM)
        dma = pltpu.SemaphoreType.DMA
        outs = (
            jax.ShapeDtypeStruct(slab.shape, F32),
            jax.ShapeDtypeStruct((lat, lon), F32),
            jax.ShapeDtypeStruct((lat, lon), F32),
            jax.ShapeDtypeStruct((blocks, 128), F32),
        )
        return pl.pallas_call(
            functools.partial(kernel, (na, nb, steps)),
            out_shape=outs,
            in_specs=[
                vmem,
                vmem,
                pl.BlockSpec(memory_space=pltpu.SMEM),
                vmem,
                vmem,
                vmem,
                vmem,
                vmem,
                pl.BlockSpec(memory_space=pl.ANY),
            ],
            out_specs=(vmem,) * 4,
            scratch_shapes=[
                pltpu.VMEM((7, 4, 128, 128), F32),
                pltpu.VMEM((8, 4, 128, 128), F32),
                pltpu.VMEM((2, 2, 32, 128), F32),
                pltpu.VMEM((2, 2, 32, 128), F32),
                pltpu.VMEM((2, 2, 32, 128), F32),
                pltpu.VMEM((2, 2, 32, 128), F32),
                pltpu.VMEM((128, 128), F32),
                pltpu.VMEM((slots, 256), BF16),
                pltpu.VMEM((slots, 128), F32),
                pltpu.VMEM((count, cap, 128), F32),
                pltpu.VMEM((count, cap, 128), F32),
                pltpu.VMEM((2, lat, 128), F32),
                pltpu.VMEM((2, 2 * orders, lon), BF16),
                pltpu.VMEM((2, 2 * orders, 2 * lon), BF16),
                pltpu.VMEM((nb, 4 * PAIRS, lat), F32),
                pltpu.VMEM((nb, 4 * PAIRS, lat), F32),
                pltpu.VMEM((steps // 16 + 1, PAIRS, 128), F32),
                pltpu.VMEM((3, width, lat), BF16),
                pltpu.VMEM((2, PAIRS, width), F32),
                pltpu.VMEM((2, width), F32),
                pltpu.VMEM((na, 2, width), F32),
                pltpu.VMEM((nb, 4 * PAIRS, lat), F32),
                pltpu.VMEM((2, 8, lon), F32),
                pltpu.VMEM((4, lat, 128), F32),
                pltpu.VMEM((8, slots, 128), F32),
                pltpu.VMEM((count, cap, 128), F32),
                pltpu.VMEM((count, cap, 128), F32),
                dma((2, 8)),
                dma((5,)),
                dma((5,)),
                dma((2, 2)),
                dma,
            ],
            compiler_params=pltpu.CompilerParams(
                collective_id=0, has_side_effects=True, vmem_limit_bytes=56 * 1024 * 1024
            ),
        )(
            slab,
            speeds,
            source_matrix,
            pedersen,
            owners,
            tile_positions[:, None],
            jnp.asarray(wave),
            jnp.asarray(twiddle),
            jnp.asarray(table),
        )

    in_specs = (
        P(None, None, "blk", "inner"),
        P(None, None, "blk", "inner"),
        P(),
        P("blk", "inner"),
        P(("blk", "inner"), None),
        P(("blk", "inner")),
    )
    out_specs = (
        P(None, None, "blk", "inner"),
        P("blk", "inner"),
        P("blk", "inner"),
        P(("blk", "inner"), None),
    )
    return jax.shard_map(shards, mesh=mesh, in_specs=in_specs, out_specs=out_specs, check_vma=False)
```

```python
import functools
import math

import jax
import jax.numpy as jnp
import numpy as np
from jax import lax
from jax.experimental import pallas as pl
from jax.experimental.pallas import tpu as pltpu
from jax.sharding import PartitionSpec as P

F32 = jnp.float32
BF16 = jnp.bfloat16
I32 = jnp.int32
MESH = pl.DeviceIdType.MESH
BLOCK = 8
PAIRS = 8
SCREENING = 2.0
GAIN = 4096.0


def iota(shape, dim):
    return lax.broadcasted_iota(I32, shape, dim)


def split(value):
    high = value.astype(BF16)
    return high, (value - high.astype(F32)).astype(BF16)


def split3(value):
    high = value.astype(BF16)
    rest = value - high.astype(F32)
    middle = rest.astype(BF16)
    return high, middle, (rest - middle.astype(F32)).astype(BF16)


def dot(left, right, dims=((1,), (0,))):
    return lax.dot_general(left, right, (dims, ((), ())), preferred_element_type=F32)


def dot3(left, right, dims):
    lh, ll = left
    rh, rl = right
    return dot(lh, rh, dims) + dot(ll, rh, dims) + dot(lh, rl, dims)


def spectral_tables(blk_count, inner_count, lat_dev, lon_dev):
    orders = PAIRS * 2 * inner_count
    degrees = orders
    lon_total = lon_dev * inner_count
    first = np.arange(inner_count * PAIRS).reshape(inner_count, 1, PAIRS)
    order_of = np.concatenate([first, orders - 1 - first], axis=1).reshape(-1)
    cols = np.arange(lon_dev)
    phase = (order_of[:, None] * cols[None, :] % lon_total) * (2.0 * math.pi / lon_total)
    wave = np.stack([np.cos(phase), np.sin(phase)]).astype(np.float32)
    turn = (order_of[:, None] * (np.arange(inner_count) * lon_dev)[None, :] % lon_total) * (
        2.0 * math.pi / lon_total
    )
    twiddle = np.zeros((order_of.shape[0], 128), np.float32)
    twiddle[:, :inner_count] = np.cos(turn)
    twiddle[:, 32 : 32 + inner_count] = np.sin(turn)
    twiddle[:, 64] = order_of
    twiddle[:, 65] = np.where(order_of == 0, 1.0, 2.0)

    turns = -(-(degrees + 1) // 16)
    steps = turns * 16
    table = np.zeros((inner_count, turns + 1, PAIRS, 128), np.float32)

    def up(degree, order):
        return np.sqrt(
            np.float32(4.0 * degree * degree - 1.0) / np.float32(degree * degree - order * order)
        )

    counter = np.arange(1, orders, dtype=np.float64)
    log_start = 0.5 * np.log(0.5) + np.concatenate(
        [np.zeros(1), np.cumsum(0.5 * np.log((2.0 * counter + 1.0) / (2.0 * counter)))]
    )
    for pair in range(inner_count * PAIRS):
        place, lane = divmod(pair, PAIRS)
        low, partner = pair, orders - 1 - pair
        table[place, turns, lane, :4] = [low, log_start[low], partner, log_start[partner]]
        for step in range(degrees + 1):
            if step <= low:
                order, degree, kind = partner, partner + step, 3
            else:
                order, degree, kind = low, step - 1, 2
            turn_at, offset = divmod(step, 16)
            if degree == order:
                table[place, turn_at, lane, kind * 16 + offset] = 1.0
                continue
            ratio = up(degree, order)
            table[place, turn_at, lane, offset] = ratio
            if degree >= order + 2:
                table[place, turn_at, lane, 16 + offset] = ratio / up(degree - 1, order)
    return wave, twiddle, table, steps


def kernel(
    sizes,
    u_hbm,
    w_hbm,
    mix_ref,
    ped_hbm,
    owner_ref,
    tile_ref,
    wave_hbm,
    twiddle_hbm,
    table_hbm,
    out_ref,
    pot_ref,
    heat_ref,
    blocks_ref,
    u_ref,
    w_ref,
    ped_ref,
    wave_ref,
    twiddle_ref,
    ratios,
    coef,
    u1,
    first_send_x,
    first_send_y,
    first_recv_x,
    first_recv_y,
    rest_send_x,
    rest_send_y,
    rest_recv_x,
    rest_recv_y,
    face_send_x,
    face_send_y,
    face_recv_x,
    face_recv_y,
    last_send_x,
    last_send_y,
    last_recv_x,
    last_recv_y,
    turned,
    sel_t,
    label_ref,
    face_send,
    face_recv,
    forcing,
    base_ref,
    values_ref,
    spec_send,
    spec_recv,
    leg,
    mask_ref,
    coef_send,
    coef_recv,
    syn_all,
    rim_send,
    rim_recv,
    grids,
    wide,
    reply_send,
    reply_recv,
    edge_sems,
    send_sems,
    recv_sems,
    rim_sems,
    in_sems,
    ready,
):
    na, nb, steps = sizes
    count = na * nb
    lat, lon = ped_ref.shape
    rows_total, cols_total = lat * na, lon * nb
    cap = face_send.shape[1]
    slots = count * cap
    a, b = lax.axis_index("blk"), lax.axis_index("inner")
    me = a * nb + b
    orders = PAIRS * 2 * nb
    spec_rows = 2 * orders

    nx, nz = na // 2, min(4, nb)
    ny = nb // nz
    chip_x, core, chip_y, chip_z = a // 2, lax.rem(a, 2), b // nz, lax.rem(b, nz)
    peer_a = {
        (dx, dc): lax.rem(chip_x + dx, nx) * 2 + lax.rem(core + dc, 2)
        for dx in range(nx)
        for dc in range(2)
    }
    peer_b = {
        (dy, dz): lax.rem(chip_y + dy, ny) * nz + lax.rem(chip_z + dz, nz)
        for dy in range(ny)
        for dz in range(nz)
    }

    def hops(move):
        dx, dc, dy, dz = move
        return 2 * (min(dx, nx - dx) + min(dy, ny - dy) + min(dz, nz - dz)) + dc

    moves = sorted(
        [(dx, dc, dy, dz) for dx, dc in peer_a for dy, dz in peer_b if (dx, dc, dy, dz) != (0, 0, 0, 0)],
        key=hops,
        reverse=True,
    )
    blk_moves = [move for move in moves if move[2:] == (0, 0)]
    inner_moves = [move for move in moves if move[:2] == (0, 0)]

    def device(move):
        return peer_a[move[:2]], peer_b[move[2:]]

    def remote(src, dst, send_sem, recv_sem, target):
        pltpu.make_async_remote_copy(
            src_ref=src,
            dst_ref=dst,
            send_sem=send_sem,
            recv_sem=recv_sem,
            device_id=target,
            device_id_type=MESH,
        ).start()

    def take(ref, sem):
        pltpu.make_async_copy(ref, ref, sem).wait()

    def signal(sem, target):
        pl.semaphore_signal(sem, inc=1, device_id=target, device_id_type=MESH)

    up_a, down_a = lax.rem(a + 1, na), lax.rem(a + na - 1, na)
    up_b, down_b = lax.rem(b + 1, nb), lax.rem(b + nb - 1, nb)

    barrier = pltpu.get_barrier_semaphore()
    y_moves = [move for move in inner_moves if move[3] == 0]
    z_moves = [move for move in inner_moves if move[2] == 0]
    greeted = [device(move) for move in blk_moves + y_moves + z_moves]
    greeted += [(a, up_b), (a, down_b)]
    for target in greeted:
        signal(barrier, target)
    fetches = [
        pltpu.make_async_copy(src, dst, in_sems.at[at])
        for at, (src, dst) in enumerate(
            [
                (w_hbm, w_ref),
                (u_hbm, u_ref),
                (twiddle_hbm, twiddle_ref),
                (wave_hbm, wave_ref),
                (table_hbm.at[b], ratios),
                (ped_hbm, ped_ref),
            ]
        )
    ]
    for fetch in fetches:
        fetch.start()

    row = iota((128, 128), 0)
    lane = iota((128, 128), 1)
    row8 = iota((8, 128), 0)
    fetches[0].wait()

    def make_coef(z, carry):
        wx, wy = 0.15 * w_ref[0, z], 0.15 * w_ref[1, z]
        coef[0, z] = jnp.where(row == 127, 0.0, 0.15 + wx)
        coef[1, z] = jnp.where(row == 0, 0.0, 0.15 - wx)
        coef[2, z] = jnp.where(lane == 127, 0.0, 0.15 + wy)
        coef[3, z] = jnp.where(lane == 0, 0.0, 0.15 - wy)
        below = 0.15 + 0.15 * w_ref[2, jnp.maximum(z - 1, 0)]
        above = 0.15 - 0.15 * w_ref[2, jnp.minimum(z + 1, 3)]
        coef[4, z] = jnp.where(z > 0, below, 0.0)
        coef[5, z] = jnp.where(z < 3, above, 0.0)
        coef[6, z] = jnp.where(lane == 0, 0.15 - wy, 0.15 + wy)
        return carry

    lax.fori_loop(0, 4, make_coef, 0)
    fetches[1].wait()

    def pack(src, items, send_x, send_y):
        packed = jnp.zeros((128, 128), F32)
        for k, (v, z) in enumerate(items):
            last = (0.15 + 0.15 * w_ref[0, z, 120:128, :]) * src[v, z, 120:128, :]
            first = (0.15 - 0.15 * w_ref[0, z, 0:8, :]) * src[v, z, 0:8, :]
            send_x[0, k : k + 1, :] = last[7:8, :]
            send_x[1, k : k + 1, :] = first[0:1, :]
            rolled = pltpu.roll(coef[6, z] * src[v, z], 2 * k + 1, 1)
            packed = jnp.where((lane == 2 * k) | (lane == 2 * k + 1), rolled, packed)
        send_y[...] = packed.T[0 : send_y.shape[0], :]

    def send_edges(at, send_x, send_y, recv_x, recv_y):
        for side, target in ((0, (up_a, b)), (1, (down_a, b))):
            remote(
                send_x.at[side],
                recv_x.at[side],
                edge_sems.at[0, at, side],
                edge_sems.at[1, at, side],
                target,
            )
        for side, target in ((0, (a, up_b)), (1, (a, down_b))):
            remote(
                send_y,
                recv_y.at[side],
                edge_sems.at[0, at, 2 + side],
                edge_sems.at[1, at, 2 + side],
                target,
            )

    def wait_edges(at, recv_x, recv_y):
        for side in range(2):
            take(recv_x.at[side], edge_sems.at[1, at, side])
            take(recv_y.at[side], edge_sems.at[1, at, 2 + side])
        rows = recv_y.shape[1]
        odd = (iota((rows, 128), 0) & 1) == 1
        up = jnp.where(b > 0, recv_y[0], 0.0)
        down = jnp.where(b < nb - 1, recv_y[1], 0.0)
        mixed = jnp.where(odd, pltpu.roll(up, 1, 0), pltpu.roll(down, rows - 1, 0))
        if rows < 128:
            mixed = jnp.concatenate([mixed, jnp.zeros((128 - rows, 128), F32)], axis=0)
        turned[...] = mixed.T

    def drain_edges(at, send_x, send_y):
        for side in range(2):
            take(send_x.at[side], edge_sems.at[0, at, side])
            take(send_y, edge_sems.at[0, at, 2 + side])

    def mend(dst, recv_x, k, v, z):
        rolled = pltpu.roll(turned[...], 127 - 2 * k, 1)
        whole = dst[v, z] + jnp.where((lane == 0) | (lane == 127), rolled, 0.0)
        from_down = jnp.where(a > 0, recv_x[0, k : k + 1, :], 0.0)
        from_up = jnp.where(a < na - 1, recv_x[1, k : k + 1, :], 0.0)
        dst[v, z, 8:120, :] = whole[8:120]
        dst[v, z, 0:8, :] = whole[0:8] + jnp.where(row8 == 0, from_down, 0.0)
        dst[v, z, 120:128, :] = whole[120:128] + jnp.where(row8 == 7, from_up, 0.0)

    def advance(src, dst, v, z):
        u = src[v, z]
        total = mix_ref[v, 0] * src[0, z]
        for w in range(1, 8):
            total = total + mix_ref[v, w] * src[w, z]
        total = 0.3 * total + 0.1 * u
        total = total + pltpu.roll(coef[0, z] * u, 1, 0) + pltpu.roll(coef[1, z] * u, 127, 0)
        total = total + pltpu.roll(coef[2, z] * u, 1, 1) + pltpu.roll(coef[3, z] * u, 127, 1)
        if not (isinstance(z, int) and z == 0):
            total = total + coef[4, z] * src[v, z - 1 if isinstance(z, int) else jnp.maximum(z - 1, 0)]
        if not (isinstance(z, int) and z == 3):
            total = total + coef[5, z] * src[v, z + 1 if isinstance(z, int) else jnp.minimum(z + 1, 3)]
        dst[v, z] = total

    def advance_all(src, dst, vs, z):
        def one(v, carry):
            advance(src, dst, v, z)
            return carry

        lax.fori_loop(0, vs, one, 0)

    near = [(v, z) for z in (0, 1) for v in range(8)] + [(7, 2)]
    far = [(v, 2) for v in range(7)] + [(v, 3) for v in range(8)]
    faced = [(7, 0), (7, 1)]
    later = [(v, z) for z in range(4) for v in range(8) if (v, z) not in faced]
    first = (first_send_x, first_send_y, first_recv_x, first_recv_y)
    rest = (rest_send_x, rest_send_y, rest_recv_x, rest_recv_y)
    of_faces = (face_send_x, face_send_y, face_recv_x, face_recv_y)
    last = (last_send_x, last_send_y, last_recv_x, last_recv_y)

    pack(u_ref, near, first_send_x, first_send_y)
    pl.semaphore_wait(barrier, len(greeted))
    send_edges(0, *first)
    for move in y_moves:
        signal(ready.at[0], device(move))
    for z in (0, 1):
        advance_all(u_ref, u1, 8, z)
    advance(u_ref, u1, 7, 2)
    if y_moves:
        pl.semaphore_wait(ready.at[0], len(y_moves))
    for move in blk_moves:
        signal(ready.at[1], device(move))
    wait_edges(0, first_recv_x, first_recv_y)
    for k, (v, z) in enumerate(near):
        mend(u1, first_recv_x, k, v, z)

    pack(u1, faced, face_send_x, face_send_y)
    send_edges(1, *of_faces)
    for z in (0, 1):
        advance(u1, out_ref, 7, z)

    owner = jnp.broadcast_to(owner_ref[...].astype(F32), (128, 256)).T.astype(I32)
    owner_hot = jnp.where(iota((256, 128), 1) == owner, 1.0, 0.0)
    earlier = jnp.where(iota((256, 256), 0) > iota((256, 256), 1), 1.0, 0.0).astype(BF16)
    before = dot(earlier, owner_hot.astype(BF16))
    rank = jnp.sum(before * owner_hot, axis=1, keepdims=True)
    slot = owner.astype(F32) * float(cap) + rank
    slot_row = slot.T[0:1, :]
    sel = jnp.where(iota((slots, 256), 0).astype(F32) == slot_row, 1.0, 0.0).astype(BF16)
    flip = jnp.where(iota((256, 256), 0) == (iota((256, 256), 1) ^ 7), 1.0, 0.0).astype(BF16)
    sel_t[...] = dot(sel, flip).astype(BF16)
    tile_high, tile_low = split(jnp.broadcast_to(tile_ref[...].astype(F32), (128, 256)).T)
    label_ref[...] = dot(sel, tile_high) + dot(sel, tile_low)
    pack(u_ref, far, rest_send_x, rest_send_y)
    send_edges(2, *rest)

    wait_edges(1, face_recv_x, face_recv_y)
    for k, (v, z) in enumerate(faced):
        mend(out_ref, face_recv_x, k, v, z)
    current = out_ref[7, 1] - out_ref[7, 0]

    halves = [pltpu.roll(current, 64, 1).reshape(16, 8, 128), current.reshape(16, 8, 128)]
    group = iota((16, 8, 128), 2) // 8
    faces = []
    for half in range(2):
        face = jnp.zeros((16, 8, 128), F32)
        for r in range(8):
            spread = jnp.broadcast_to(halves[half][:, r : r + 1, :], (16, 8, 128))
            moved = pltpu.roll(spread, 8 * r + 8, 2, stride=8, stride_axis=1)
            face = jnp.where(group == r, moved, face)
        faces.append(face)
    faces = jnp.stack(faces, axis=1).reshape(256, 128)
    face_high, face_low = split(faces)
    routed = dot(sel_t[...], face_high) + dot(sel_t[...], face_low)
    lane_slot = iota((slots, 128), 1)
    routed = jnp.where(lane_slot < 64, routed, label_ref[...])
    face_send[...] = routed.reshape(count, cap, 128)

    def send_all(src, dst, at):
        for move in moves:
            peer_of_a, peer_of_b = device(move)
            remote(
                src.at[peer_of_a * nb + peer_of_b],
                dst.at[me],
                send_sems.at[at],
                recv_sems.at[at],
                (peer_of_a, peer_of_b),
            )
        dst[me] = src[me]

    pl.semaphore_wait(ready.at[1], len(blk_moves))
    send_all(face_send, face_recv, 0)

    advance_all(u_ref, u1, 7, 2)
    advance_all(u_ref, u1, 8, 3)
    wait_edges(2, rest_recv_x, rest_recv_y)
    for k, (v, z) in enumerate(far):
        mend(u1, rest_recv_x, k, v, z)
    pack(u1, later, last_send_x, last_send_y)
    send_edges(3, *last)

    def second_step(z, carry):
        advance_all(u1, out_ref, 7, z)
        return carry

    lax.fori_loop(0, 4, second_step, 0)
    for z in (2, 3):
        advance(u1, out_ref, 7, z)

    fetches[2].wait()
    fetches[3].wait()

    def per_row(column):
        return jnp.sum(
            jnp.where(iota((orders, 128), 1) == column, twiddle_ref[...], 0.0),
            axis=1,
            keepdims=True,
        )

    def rows_of(even, odd):
        return jnp.concatenate([even, odd], axis=2).reshape(spec_rows, lon)

    def waves():
        cos_turn, sin_turn = per_row(b), per_row(b + 32)
        cos_wave, sin_wave = wave_ref[0], wave_ref[1]
        cosine = (cos_turn * cos_wave - sin_turn * sin_wave).reshape(nb, 2, 1, PAIRS, lon)
        sine = (sin_turn * cos_wave + cos_turn * sin_wave).reshape(nb, 2, 1, PAIRS, lon)
        return cosine, sine

    cosine, sine = waves()
    base_high, base_low = split(rows_of(cosine, sine) * (1.0 / cols_total))
    base_ref[0] = base_high
    base_ref[1] = base_low

    wait_edges(3, last_recv_x, last_recv_y)
    for k, (v, z) in enumerate(later):
        mend(out_ref, last_recv_x, k, v, z)

    take(face_recv.at[pl.ds(0, count - 1)], recv_sems.at[0])
    got = face_recv[...].reshape(slots, 128)
    swapped = pltpu.roll(got, 64, 1)
    label = jnp.where(lane_slot < 64, swapped, got).astype(I32)
    face = jnp.where(lane_slot < 64, got, swapped)
    tile_row, tile_col = label >> 5, label & 31
    tile_row_t = tile_row.astype(F32).T.astype(I32)
    scatter = jnp.where(iota((32, slots), 0) == tile_row_t[0:32, :], 1.0, 0.0).astype(BF16)
    scatter = jnp.concatenate([scatter, scatter], axis=1)
    col_masks = [
        jnp.where((lane_slot >> 3) + 16 * half == tile_col, 1.0, 0.0).astype(BF16)
        for half in range(2)
    ]

    def spread_bit(value, width):
        moved = pltpu.roll(value, width, 1)
        bit = (lane_slot & width) == 0
        return [jnp.where(bit, value, moved), jnp.where(bit, moved, value)]

    lines = [face]
    for width in (32, 16, 8):
        lines = [part for line in lines for part in spread_bit(line, width)]
    for r in range(8):
        line_high, line_low = split(lines[r])
        right = jnp.concatenate(
            [
                jnp.concatenate([part * mask for mask in col_masks], axis=1)
                for part in (line_high, line_low)
            ],
            axis=0,
        )
        rows = dot(scatter, right)
        forcing[0, pl.ds(r, 32, stride=8), :] = rows[:, 0:128]
        forcing[1, pl.ds(r, 32, stride=8), :] = rows[:, 128:256]

    force = split(jnp.concatenate([forcing[0], forcing[1]], axis=1))
    spectrum = dot3((base_ref[0], base_ref[1]), force, ((1,), (1,)))
    spec_send[...] = spectrum.reshape(nb, 4 * PAIRS, lat)
    for move in inner_moves:
        peer = peer_b[move[2:]]
        remote(spec_send.at[peer], spec_recv.at[b], send_sems.at[1], recv_sems.at[1], (a, peer))
    spec_recv[b] = spec_send[b]

    fetches[4].wait()
    row_of_lane = a * lat + iota((PAIRS, lat), 1)
    x = -1.0 + (2.0 * row_of_lane.astype(F32) + 1.0) / rows_total
    log_sine = jnp.log(jnp.sqrt(1.0 - x * x))
    turns = steps // 16
    heads = ratios[turns]
    low_start = jnp.exp(heads[:, 1:2] + heads[:, 0:1] * log_sine)
    high_start = jnp.exp(heads[:, 3:4] + heads[:, 2:3] * log_sine)

    def build(turn, carry):
        previous, older = carry
        block = ratios[turn]
        made = []
        for offset in range(16):
            up = block[:, offset : offset + 1]
            down = block[:, 16 + offset : 17 + offset]
            begin_low = block[:, 32 + offset : 33 + offset]
            begin_high = block[:, 48 + offset : 49 + offset]
            present = (
                begin_low * low_start + begin_high * high_start + up * x * previous - down * older
            )
            made.append(present)
            older, previous = previous, present
        where = pl.ds(pl.multiple_of(turn * 128, 128), 128)
        for at, part in enumerate(split3(jnp.concatenate(made, axis=0))):
            leg[at, where, :] = part
        return previous, older

    empty = jnp.zeros((PAIRS, lat), F32)
    lax.fori_loop(0, turns, build, (empty, empty))

    width = steps * PAIRS
    at_step = iota((PAIRS, width), 1) // PAIRS
    at_pair = lax.rem(iota((PAIRS, width), 1), PAIRS)
    order_low = b * PAIRS + at_pair
    is_high = at_step <= order_low
    degree = jnp.where(is_high, orders - 1 - order_low + at_step, at_step - 1).astype(F32)
    scale = (2.0 / rows_total) * GAIN / (degree * (degree + 1.0) + SCREENING)
    scale = jnp.where(at_step <= orders, scale, 0.0)
    mine = at_pair == iota((PAIRS, width), 0)
    mask_ref[0] = jnp.where(mine & jnp.logical_not(is_high), scale, 0.0)
    mask_ref[1] = jnp.where(mine & is_high, scale, 0.0)

    order_col, weight_col = per_row(64), per_row(65)
    cosine, sine = waves()
    weight = weight_col.reshape(nb, 2, 1, PAIRS, 1)
    slope_weight = (weight_col * order_col).reshape(nb, 2, 1, PAIRS, 1)
    value_high, value_low = split(rows_of(cosine * weight, sine * weight))
    values_ref[0, :, 0:lon] = value_high
    values_ref[1, :, 0:lon] = value_low
    slope_high, slope_low = split(rows_of(-sine * slope_weight, cosine * slope_weight))
    values_ref[0, :, lon : 2 * lon] = slope_high
    values_ref[1, :, lon : 2 * lon] = slope_low

    take(spec_recv.at[pl.ds(0, nb - 1)], recv_sems.at[1])
    spec = spec_recv[0]
    for at in range(1, nb):
        spec = spec + spec_recv[at]
    spec_high, spec_low = split(spec)
    both = dot(jnp.concatenate([spec_high, spec_low], axis=0), leg[0], ((1,), (1,)))
    wide_sums = both[0:32] + both[32:64] + dot(spec_high, leg[1], ((1,), (1,)))
    for parity in range(2):
        low_rows = wide_sums[parity * 8 : parity * 8 + 8]
        high_rows = wide_sums[16 + parity * 8 : 24 + parity * 8]
        kept = low_rows * mask_ref[0] + high_rows * mask_ref[1]
        coef_send[parity : parity + 1, :] = jnp.sum(kept, axis=0, keepdims=True)
    for move in blk_moves:
        remote(
            coef_send,
            coef_recv.at[a],
            send_sems.at[2],
            recv_sems.at[2],
            (peer_a[move[:2]], b),
        )
    coef_recv[a] = coef_send[...]
    take(coef_recv.at[pl.ds(0, na - 1)], recv_sems.at[2])
    solved = coef_recv[0]
    for at in range(1, na):
        solved = solved + coef_recv[at]
    expanded = []
    for kind in range(2):
        for parity in range(2):
            expanded.append(
                jnp.where(
                    mask_ref[kind] != 0.0,
                    jnp.broadcast_to(solved[parity : parity + 1, :], (PAIRS, width)),
                    0.0,
                )
            )
    solved_high, solved_low = split(jnp.concatenate(expanded, axis=0))
    solved_both = jnp.concatenate([solved_high, solved_low], axis=0)
    fine = dot(solved_high, leg[2])
    both = dot(solved_both, leg[0])
    middle = dot(solved_both, leg[1])
    syn_all[b] = both[0:32] + (both[32:64] + (middle[0:32] + (middle[32:64] + fine)))
    for move in inner_moves:
        remote(
            syn_all.at[b],
            syn_all.at[b],
            send_sems.at[3],
            recv_sems.at[3],
            (a, peer_b[move[2:]]),
        )
    take(syn_all.at[pl.ds(0, nb - 1)], recv_sems.at[3])

    syn_high, syn_middle, syn_low = split3(syn_all[...].reshape(spec_rows, lat).T)

    def potential_of(high, middle, low):
        rows = high.shape[0]
        coarse = dot(jnp.concatenate([high, middle, low], axis=0), values_ref[0, :, 0:lon])
        rest_of = dot(jnp.concatenate([high, middle], axis=0), values_ref[1, :, 0:lon])
        return coarse[0:rows] + (
            coarse[rows : 2 * rows] + (rest_of[0:rows] + (coarse[2 * rows :] + rest_of[rows:]))
        )

    def rims_of(part):
        return jnp.concatenate([part[0:16], part[lat - 16 :]], axis=0)

    rims = potential_of(rims_of(syn_high), rims_of(syn_middle), rims_of(syn_low))
    rim_send[0] = rims[0:8]
    rim_send[1] = rims[24:32]
    remote(rim_send.at[1], rim_recv.at[0], rim_sems.at[0, 0], rim_sems.at[1, 0], (up_a, b))
    remote(rim_send.at[0], rim_recv.at[1], rim_sems.at[0, 1], rim_sems.at[1, 1], (down_a, b))
    potential = potential_of(syn_high, syn_middle, syn_low)
    pot_ref[...] = potential
    turned_slopes = dot(
        jnp.concatenate([syn_high, syn_middle], axis=0), values_ref[0, :, lon : 2 * lon]
    )
    azimuthal = turned_slopes[0:lat] + (
        turned_slopes[lat:] + dot(syn_high, values_ref[1, :, lon : 2 * lon])
    )
    fetches[5].wait()
    grid_row = iota((lat, 1), 0)
    global_row = a * lat + grid_row
    x_col = -1.0 + (2.0 * global_row.astype(F32) + 1.0) / rows_total
    sine_col = jnp.sqrt(1.0 - x_col * x_col)
    eastward = azimuthal / sine_col
    take(rim_recv.at[0], rim_sems.at[1, 0])
    take(rim_recv.at[1], rim_sems.at[1, 1])
    above = jnp.where(grid_row == lat - 1, rim_recv[1, 0:1, :], pltpu.roll(potential, lat - 1, 0))
    below = jnp.where(grid_row == 0, rim_recv[0, 7:8, :], pltpu.roll(potential, 1, 0))
    inverse = rows_total / 2.0
    at_first, at_last = global_row == 0, global_row == rows_total - 1
    slope = (jnp.where(at_last, potential, above) - jnp.where(at_first, potential, below)) * (
        jnp.where(at_first | at_last, inverse, 0.5 * inverse)
    )
    polar = sine_col * slope
    heating = ped_ref[...] * (polar * polar + eastward * eastward)
    heat_ref[...] = heating

    grids[0] = potential[:, 0:128]
    grids[1] = potential[:, 128:256]
    grids[2] = heating[:, 0:128]
    grids[3] = heating[:, 128:256]
    pick = iota((slots, 128), 1)
    pick = jnp.where((pick < 96) & ((pick & 31) == tile_row), 1.0, 0.0).astype(BF16)
    bits = [(tile_col & (1 << at)) != 0 for at in range(5)]
    upper = lane_slot >= 64
    for r in range(8):
        rows = jnp.concatenate([grids[at, pl.ds(r, 32, stride=8), :] for at in range(4)], axis=1)
        high, middle, low = split3(rows)
        parts = jnp.concatenate([high, middle, low, jnp.zeros_like(low)], axis=0)
        picked = dot(pick, parts)
        pot = jnp.where(bits[4], picked[:, 128:256], picked[:, 0:128])
        heat = jnp.where(bits[4], picked[:, 384:512], picked[:, 256:384])
        wide[r] = jnp.where(
            upper,
            jnp.where(bits[3], heat, pltpu.roll(heat, 64, 1)),
            jnp.where(bits[3], pltpu.roll(pot, 64, 1), pot),
        )

    def join(first, second, at):
        width = 8 << at
        return jnp.where(
            (lane_slot & width) == 0,
            jnp.where(bits[at], pltpu.roll(first, 128 - width, 1), first),
            jnp.where(bits[at], second, pltpu.roll(second, width, 1)),
        )

    quads = [join(wide[r], wide[r + 4], 2) for r in range(4)]
    twos = [join(quads[r], quads[r + 2], 1) for r in range(2)]
    reply_send[...] = join(twos[0], twos[1], 0).reshape(count, cap, 128)
    send_all(reply_send, reply_recv, 4)
    chosen = jnp.where(iota((256, slots), 1).astype(F32) == slot[:, 0:1], 1.0, 0.0).astype(BF16)
    take(reply_recv.at[pl.ds(0, count - 1)], recv_sems.at[4])
    back_high, back_low = split(reply_recv[...].reshape(slots, 128))
    blocks_ref[...] = dot(chosen, back_high) + dot(chosen, back_low)

    for at, (sent_x, sent_y, _, _) in enumerate((first, of_faces, rest, last)):
        drain_edges(at, sent_x, sent_y)
    take(face_send.at[pl.ds(0, count - 1)], send_sems.at[0])
    take(spec_send.at[pl.ds(0, nb - 1)], send_sems.at[1])
    take(coef_recv.at[pl.ds(0, na - 1)], send_sems.at[2])
    take(syn_all.at[pl.ds(0, nb - 1)], send_sems.at[3])
    take(reply_send.at[pl.ds(0, count - 1)], send_sems.at[4])
    take(rim_send.at[0], rim_sems.at[0, 1])
    take(rim_send.at[1], rim_sems.at[0, 0])


def write_out(slab_ref, *refs):
    results, (targets, sems) = (slab_ref,) + refs[:3], (refs[3:7], refs[7])
    copies = [
        pltpu.make_async_copy(results[0].at[v], targets[0].at[v], sems.at[v]) for v in range(8)
    ]
    copies += [
        pltpu.make_async_copy(results[at], targets[at], sems.at[7 + at]) for at in range(1, 4)
    ]
    for copy in copies:
        copy.start()
    for copy in copies:
        copy.wait()


def solution(mesh):
    na, nb = mesh.shape["blk"], mesh.shape["inner"]
    count = na * nb

    def shards(slab, speeds, source_matrix, pedersen, owners, tile_positions):
        lat, lon = pedersen.shape
        blocks = owners.shape[0]
        cap = max(2, 2 * blocks // count)
        slots = count * cap
        orders = PAIRS * 2 * nb
        wave, twiddle, table, steps = spectral_tables(na, nb, lat, lon)
        width = steps * PAIRS
        vmem = pl.BlockSpec(memory_space=pltpu.VMEM)
        hbm = pl.BlockSpec(memory_space=pltpu.HBM)
        dma = pltpu.SemaphoreType.DMA
        shapes = (slab.shape, (lat, lon), (lat, lon), (blocks, 128))

        def edges(rows_x, rows_y):
            return [
                pltpu.VMEM((2, rows_x, 128), F32),
                pltpu.VMEM((rows_y, 128), F32),
                pltpu.VMEM((2, rows_x, 128), F32),
                pltpu.VMEM((2, rows_y, 128), F32),
            ]

        results = pl.pallas_call(
            functools.partial(kernel, (na, nb, steps)),
            out_shape=tuple(jax.ShapeDtypeStruct(shape, F32) for shape in shapes),
            in_specs=[
                hbm,
                hbm,
                pl.BlockSpec(memory_space=pltpu.SMEM),
                hbm,
                vmem,
                vmem,
                hbm,
                hbm,
                hbm,
            ],
            out_specs=(vmem,) * 4,
            scratch_shapes=[
                pltpu.VMEM(slab.shape, F32),
                pltpu.VMEM(speeds.shape, F32),
                pltpu.VMEM((lat, lon), F32),
                pltpu.VMEM(wave.shape, F32),
                pltpu.VMEM(twiddle.shape, F32),
                pltpu.VMEM((steps // 16 + 1, PAIRS, 128), F32),
                pltpu.VMEM((7, 4, 128, 128), F32),
                pltpu.VMEM((8, 4, 128, 128), F32),
                *edges(24, 40),
                *edges(16, 32),
                *edges(8, 8),
                *edges(32, 64),
                pltpu.VMEM((128, 128), F32),
                pltpu.VMEM((slots, 256), BF16),
                pltpu.VMEM((slots, 128), F32),
                pltpu.VMEM((count, cap, 128), F32),
                pltpu.VMEM((count, cap, 128), F32),
                pltpu.VMEM((2, lat, 128), F32),
                pltpu.VMEM((2, 2 * orders, lon), BF16),
                pltpu.VMEM((2, 2 * orders, 2 * lon), BF16),
                pltpu.VMEM((nb, 4 * PAIRS, lat), F32),
                pltpu.VMEM((nb, 4 * PAIRS, lat), F32),
                pltpu.VMEM((3, width, lat), BF16),
                pltpu.VMEM((2, PAIRS, width), F32),
                pltpu.VMEM((2, width), F32),
                pltpu.VMEM((na, 2, width), F32),
                pltpu.VMEM((nb, 4 * PAIRS, lat), F32),
                pltpu.VMEM((2, 8, lon), F32),
                pltpu.VMEM((2, 8, lon), F32),
                pltpu.VMEM((4, lat, 128), F32),
                pltpu.VMEM((8, slots, 128), F32),
                pltpu.VMEM((count, cap, 128), F32),
                pltpu.VMEM((count, cap, 128), F32),
                dma((2, 4, 4)),
                dma((5,)),
                dma((5,)),
                dma((2, 2)),
                dma((6,)),
                pltpu.SemaphoreType.REGULAR((2,)),
            ],
            compiler_params=pltpu.CompilerParams(
                collective_id=0, has_side_effects=True, vmem_limit_bytes=40 * 1024 * 1024
            ),
        )(
            slab,
            speeds,
            source_matrix,
            pedersen,
            owners.reshape(1, blocks),
            tile_positions.reshape(1, blocks),
            jnp.asarray(wave),
            jnp.asarray(twiddle),
            jnp.asarray(table),
        )
        return pl.pallas_call(
            write_out,
            out_shape=tuple(jax.ShapeDtypeStruct(shape, F32) for shape in shapes),
            in_specs=[vmem] * 4,
            out_specs=(hbm,) * 4,
            scratch_shapes=[dma((11,))],
        )(*results)

    in_specs = (
        P(None, None, "blk", "inner"),
        P(None, None, "blk", "inner"),
        P(),
        P("blk", "inner"),
        P(("blk", "inner"), None),
        P(("blk", "inner")),
    )
    out_specs = (
        P(None, None, "blk", "inner"),
        P("blk", "inner"),
        P("blk", "inner"),
        P(("blk", "inner"), None),
    )
    return jax.shard_map(shards, mesh=mesh, in_specs=in_specs, out_specs=out_specs, check_vma=False)
```

```python
import functools
import math

import jax
import jax.numpy as jnp
import numpy as np
from jax import lax
from jax.experimental import pallas as pl
from jax.experimental.pallas import tpu as pltpu
from jax.sharding import PartitionSpec as P

F32 = jnp.float32
BF16 = jnp.bfloat16
I32 = jnp.int32
MESH = pl.DeviceIdType.MESH
BLOCK = 8
PAIRS = 8
SCREENING = 2.0
GAIN = 4096.0
VMEM_LIMIT = 60 * 1024 * 1024


def iota(shape, dim):
    return lax.broadcasted_iota(I32, shape, dim)


def split(value):
    high = value.astype(BF16)
    return high, (value - high.astype(F32)).astype(BF16)


def split3(value):
    high = value.astype(BF16)
    rest = value - high.astype(F32)
    middle = rest.astype(BF16)
    return high, middle, (rest - middle.astype(F32)).astype(BF16)


def dot(left, right, dims=((1,), (0,))):
    return lax.dot_general(left, right, (dims, ((), ())), preferred_element_type=F32)


def dot3(left, right, dims):
    lh, ll = left
    rh, rl = right
    return dot(lh, rh, dims) + dot(ll, rh, dims) + dot(lh, rl, dims)


def spectral_tables(blk_count, inner_count, lat_dev, lon_dev):
    orders = PAIRS * 2 * inner_count
    degrees = orders
    lon_total = lon_dev * inner_count
    first = np.arange(inner_count * PAIRS).reshape(inner_count, 1, PAIRS)
    order_of = np.concatenate([first, orders - 1 - first], axis=1).reshape(-1)
    cols = np.arange(lon_dev)
    phase = (order_of[:, None] * cols[None, :] % lon_total) * (2.0 * math.pi / lon_total)
    wave = np.stack([np.cos(phase), np.sin(phase)]).astype(np.float32)
    turn = (order_of[:, None] * (np.arange(inner_count) * lon_dev)[None, :] % lon_total) * (
        2.0 * math.pi / lon_total
    )
    twiddle = np.zeros((order_of.shape[0], 128), np.float32)
    twiddle[:, :inner_count] = np.cos(turn)
    twiddle[:, 32 : 32 + inner_count] = np.sin(turn)
    twiddle[:, 64] = order_of
    twiddle[:, 65] = np.where(order_of == 0, 1.0, 2.0)

    turns = -(-(degrees + 1) // 16)
    steps = turns * 16
    table = np.zeros((inner_count, turns + 1, PAIRS, 128), np.float32)

    def up(degree, order):
        return np.sqrt(
            np.float32(4.0 * degree * degree - 1.0) / np.float32(degree * degree - order * order)
        )

    counter = np.arange(1, orders, dtype=np.float64)
    log_start = 0.5 * np.log(0.5) + np.concatenate(
        [np.zeros(1), np.cumsum(0.5 * np.log((2.0 * counter + 1.0) / (2.0 * counter)))]
    )
    for pair in range(inner_count * PAIRS):
        place, lane = divmod(pair, PAIRS)
        low, partner = pair, orders - 1 - pair
        table[place, turns, lane, :4] = [low, log_start[low], partner, log_start[partner]]
        for step in range(degrees + 1):
            if step <= low:
                order, degree, kind = partner, partner + step, 3
            else:
                order, degree, kind = low, step - 1, 2
            turn_at, offset = divmod(step, 16)
            if degree == order:
                table[place, turn_at, lane, kind * 16 + offset] = 1.0
                continue
            ratio = up(degree, order)
            table[place, turn_at, lane, offset] = ratio
            if degree >= order + 2:
                table[place, turn_at, lane, 16 + offset] = ratio / up(degree - 1, order)
    return wave, twiddle, table, steps


def kernel(
    sizes,
    u_hbm,
    w_hbm,
    mix_ref,
    ped_hbm,
    owner_ref,
    tile_ref,
    wave_hbm,
    twiddle_hbm,
    table_hbm,
    out_hbm,
    pot_hbm,
    heat_hbm,
    blocks_hbm,
    out_ref,
    pot_ref,
    heat_ref,
    blocks_ref,
    u_ref,
    w_ref,
    ped_ref,
    wave_ref,
    twiddle_ref,
    ratios,
    coef,
    u1,
    first_send_x,
    first_send_y,
    first_recv_x,
    first_recv_y,
    rest_send_x,
    rest_send_y,
    rest_recv_x,
    rest_recv_y,
    face_send_x,
    face_send_y,
    face_recv_x,
    face_recv_y,
    last_send_x,
    last_send_y,
    last_recv_x,
    last_recv_y,
    turned,
    sel_t,
    label_ref,
    face_send,
    face_recv,
    forcing,
    base_ref,
    values_ref,
    spec_send,
    spec_recv,
    leg,
    mask_ref,
    coef_send,
    coef_recv,
    syn_all,
    rim_send,
    rim_recv,
    grids,
    wide,
    reply_send,
    reply_recv,
    edge_sems,
    send_sems,
    recv_sems,
    rim_sems,
    in_sems,
    out_sems,
    ready,
):
    na, nb, steps = sizes
    count = na * nb
    lat, lon = ped_ref.shape
    rows_total, cols_total = lat * na, lon * nb
    cap = face_send.shape[1]
    slots = count * cap
    a, b = lax.axis_index("blk"), lax.axis_index("inner")
    me = a * nb + b
    orders = PAIRS * 2 * nb
    spec_rows = 2 * orders

    nx, nz = na // 2, min(4, nb)
    ny = nb // nz
    chip_x, core, chip_y, chip_z = a // 2, lax.rem(a, 2), b // nz, lax.rem(b, nz)
    peer_a = {
        (dx, dc): lax.rem(chip_x + dx, nx) * 2 + lax.rem(core + dc, 2)
        for dx in range(nx)
        for dc in range(2)
    }
    peer_b = {
        (dy, dz): lax.rem(chip_y + dy, ny) * nz + lax.rem(chip_z + dz, nz)
        for dy in range(ny)
        for dz in range(nz)
    }

    def hops(move):
        dx, dc, dy, dz = move
        return 2 * (min(dx, nx - dx) + min(dy, ny - dy) + min(dz, nz - dz)) + dc

    moves = sorted(
        [(dx, dc, dy, dz) for dx, dc in peer_a for dy, dz in peer_b if (dx, dc, dy, dz) != (0, 0, 0, 0)],
        key=hops,
        reverse=True,
    )
    blk_moves = [move for move in moves if move[2:] == (0, 0)]
    inner_moves = [move for move in moves if move[:2] == (0, 0)]

    def device(move):
        return peer_a[move[:2]], peer_b[move[2:]]

    def remote(src, dst, send_sem, recv_sem, target):
        pltpu.make_async_remote_copy(
            src_ref=src,
            dst_ref=dst,
            send_sem=send_sem,
            recv_sem=recv_sem,
            device_id=target,
            device_id_type=MESH,
        ).start()

    def take(ref, sem):
        pltpu.make_async_copy(ref, ref, sem).wait()

    def signal(sem, target):
        pl.semaphore_signal(sem, inc=1, device_id=target, device_id_type=MESH)

    up_a, down_a = lax.rem(a + 1, na), lax.rem(a + na - 1, na)
    up_b, down_b = lax.rem(b + 1, nb), lax.rem(b + nb - 1, nb)

    barrier = pltpu.get_barrier_semaphore()
    y_moves = [move for move in inner_moves if move[3] == 0]
    z_moves = [move for move in inner_moves if move[2] == 0]
    greeted = [device(move) for move in blk_moves + y_moves + z_moves]
    greeted += [(a, up_b), (a, down_b)]
    for target in greeted:
        signal(barrier, target)
    fetches = [
        pltpu.make_async_copy(src, dst, in_sems.at[at])
        for at, (src, dst) in enumerate(
            [
                (w_hbm, w_ref),
                (u_hbm, u_ref),
                (twiddle_hbm, twiddle_ref),
                (wave_hbm, wave_ref),
                (table_hbm.at[b], ratios),
                (ped_hbm, ped_ref),
            ]
        )
    ]
    for fetch in fetches:
        fetch.start()

    row = iota((128, 128), 0)
    lane = iota((128, 128), 1)
    row8 = iota((8, 128), 0)
    fetches[0].wait()

    def make_coef(z, carry):
        wx, wy = 0.15 * w_ref[0, z], 0.15 * w_ref[1, z]
        coef[0, z] = jnp.where(row == 127, 0.0, 0.15 + wx)
        coef[1, z] = jnp.where(row == 0, 0.0, 0.15 - wx)
        coef[2, z] = jnp.where(lane == 127, 0.0, 0.15 + wy)
        coef[3, z] = jnp.where(lane == 0, 0.0, 0.15 - wy)
        below = 0.15 + 0.15 * w_ref[2, jnp.maximum(z - 1, 0)]
        above = 0.15 - 0.15 * w_ref[2, jnp.minimum(z + 1, 3)]
        coef[4, z] = jnp.where(z > 0, below, 0.0)
        coef[5, z] = jnp.where(z < 3, above, 0.0)
        coef[6, z] = jnp.where(lane == 0, 0.15 - wy, 0.15 + wy)
        return carry

    lax.fori_loop(0, 4, make_coef, 0)
    fetches[1].wait()

    def pack(src, items, send_x, send_y):
        packed = jnp.zeros((128, 128), F32)
        for k, (v, z) in enumerate(items):
            last = (0.15 + 0.15 * w_ref[0, z, 120:128, :]) * src[v, z, 120:128, :]
            first = (0.15 - 0.15 * w_ref[0, z, 0:8, :]) * src[v, z, 0:8, :]
            send_x[0, k : k + 1, :] = last[7:8, :]
            send_x[1, k : k + 1, :] = first[0:1, :]
            rolled = pltpu.roll(coef[6, z] * src[v, z], 2 * k + 1, 1)
            packed = jnp.where((lane == 2 * k) | (lane == 2 * k + 1), rolled, packed)
        send_y[...] = packed.T[0 : send_y.shape[0], :]

    def send_edges(at, send_x, send_y, recv_x, recv_y):
        for side, target in ((0, (up_a, b)), (1, (down_a, b))):
            remote(
                send_x.at[side],
                recv_x.at[side],
                edge_sems.at[0, at, side],
                edge_sems.at[1, at, side],
                target,
            )
        for side, target in ((0, (a, up_b)), (1, (a, down_b))):
            remote(
                send_y,
                recv_y.at[side],
                edge_sems.at[0, at, 2 + side],
                edge_sems.at[1, at, 2 + side],
                target,
            )

    def wait_edges(at, recv_x, recv_y):
        for side in range(2):
            take(recv_x.at[side], edge_sems.at[1, at, side])
            take(recv_y.at[side], edge_sems.at[1, at, 2 + side])
        rows = recv_y.shape[1]
        odd = (iota((rows, 128), 0) & 1) == 1
        up = jnp.where(b > 0, recv_y[0], 0.0)
        down = jnp.where(b < nb - 1, recv_y[1], 0.0)
        mixed = jnp.where(odd, pltpu.roll(up, 1, 0), pltpu.roll(down, rows - 1, 0))
        if rows < 128:
            mixed = jnp.concatenate([mixed, jnp.zeros((128 - rows, 128), F32)], axis=0)
        turned[...] = mixed.T

    def drain_edges(at, send_x, send_y):
        for side in range(2):
            take(send_x.at[side], edge_sems.at[0, at, side])
            take(send_y, edge_sems.at[0, at, 2 + side])

    def mend(dst, recv_x, k, v, z):
        rolled = pltpu.roll(turned[...], 127 - 2 * k, 1)
        whole = dst[v, z] + jnp.where((lane == 0) | (lane == 127), rolled, 0.0)
        from_down = jnp.where(a > 0, recv_x[0, k : k + 1, :], 0.0)
        from_up = jnp.where(a < na - 1, recv_x[1, k : k + 1, :], 0.0)
        dst[v, z, 8:120, :] = whole[8:120]
        dst[v, z, 0:8, :] = whole[0:8] + jnp.where(row8 == 0, from_down, 0.0)
        dst[v, z, 120:128, :] = whole[120:128] + jnp.where(row8 == 7, from_up, 0.0)

    def advance(src, dst, v, z):
        u = src[v, z]
        total = mix_ref[v, 0] * src[0, z]
        for w in range(1, 8):
            total = total + mix_ref[v, w] * src[w, z]
        total = 0.3 * total + 0.1 * u
        total = total + pltpu.roll(coef[0, z] * u, 1, 0) + pltpu.roll(coef[1, z] * u, 127, 0)
        total = total + pltpu.roll(coef[2, z] * u, 1, 1) + pltpu.roll(coef[3, z] * u, 127, 1)
        if not (isinstance(z, int) and z == 0):
            total = total + coef[4, z] * src[v, z - 1 if isinstance(z, int) else jnp.maximum(z - 1, 0)]
        if not (isinstance(z, int) and z == 3):
            total = total + coef[5, z] * src[v, z + 1 if isinstance(z, int) else jnp.minimum(z + 1, 3)]
        dst[v, z] = total

    def advance_all(src, dst, vs, z):
        def one(v, carry):
            advance(src, dst, v, z)
            return carry

        lax.fori_loop(0, vs, one, 0)

    near = [(v, z) for z in (0, 1) for v in range(8)] + [(7, 2)]
    far = [(v, 2) for v in range(7)] + [(v, 3) for v in range(8)]
    faced = [(7, 0), (7, 1)]
    later = [(v, z) for z in range(4) for v in range(8) if (v, z) not in faced]
    first = (first_send_x, first_send_y, first_recv_x, first_recv_y)
    rest = (rest_send_x, rest_send_y, rest_recv_x, rest_recv_y)
    of_faces = (face_send_x, face_send_y, face_recv_x, face_recv_y)
    last = (last_send_x, last_send_y, last_recv_x, last_recv_y)

    pack(u_ref, near, first_send_x, first_send_y)
    pl.semaphore_wait(barrier, len(greeted))
    send_edges(0, *first)
    for move in y_moves:
        signal(ready.at[0], device(move))
    for z in (0, 1):
        advance_all(u_ref, u1, 8, z)
    advance(u_ref, u1, 7, 2)
    if y_moves:
        pl.semaphore_wait(ready.at[0], len(y_moves))
    for move in blk_moves:
        signal(ready.at[1], device(move))
    wait_edges(0, first_recv_x, first_recv_y)
    for k, (v, z) in enumerate(near):
        mend(u1, first_recv_x, k, v, z)

    pack(u1, faced, face_send_x, face_send_y)
    send_edges(1, *of_faces)
    for z in (0, 1):
        advance(u1, out_ref, 7, z)

    owner = jnp.broadcast_to(owner_ref[...].astype(F32), (128, 256)).T.astype(I32)
    owner_hot = jnp.where(iota((256, 128), 1) == owner, 1.0, 0.0)
    earlier = jnp.where(iota((256, 256), 0) > iota((256, 256), 1), 1.0, 0.0).astype(BF16)
    before = dot(earlier, owner_hot.astype(BF16))
    rank = jnp.sum(before * owner_hot, axis=1, keepdims=True)
    slot = owner.astype(F32) * float(cap) + rank
    slot_row = slot.T[0:1, :]
    sel = jnp.where(iota((slots, 256), 0).astype(F32) == slot_row, 1.0, 0.0).astype(BF16)
    flip = jnp.where(iota((256, 256), 0) == (iota((256, 256), 1) ^ 7), 1.0, 0.0).astype(BF16)
    sel_t[...] = dot(sel, flip).astype(BF16)
    tile_high, tile_low = split(jnp.broadcast_to(tile_ref[...].astype(F32), (128, 256)).T)
    label_ref[...] = dot(sel, tile_high) + dot(sel, tile_low)
    pack(u_ref, far, rest_send_x, rest_send_y)
    send_edges(2, *rest)

    wait_edges(1, face_recv_x, face_recv_y)
    for k, (v, z) in enumerate(faced):
        mend(out_ref, face_recv_x, k, v, z)
    current = out_ref[7, 1] - out_ref[7, 0]

    halves = [pltpu.roll(current, 64, 1).reshape(16, 8, 128), current.reshape(16, 8, 128)]
    group = iota((16, 8, 128), 2) // 8
    faces = []
    for half in range(2):
        face = jnp.zeros((16, 8, 128), F32)
        for r in range(8):
            spread = jnp.broadcast_to(halves[half][:, r : r + 1, :], (16, 8, 128))
            moved = pltpu.roll(spread, 8 * r + 8, 2, stride=8, stride_axis=1)
            face = jnp.where(group == r, moved, face)
        faces.append(face)
    faces = jnp.stack(faces, axis=1).reshape(256, 128)
    face_high, face_low = split(faces)
    routed = dot(sel_t[...], face_high) + dot(sel_t[...], face_low)
    lane_slot = iota((slots, 128), 1)
    routed = jnp.where(lane_slot < 64, routed, label_ref[...])
    face_send[...] = routed.reshape(count, cap, 128)

    def send_all(src, dst, at):
        for move in moves:
            peer_of_a, peer_of_b = device(move)
            remote(
                src.at[peer_of_a * nb + peer_of_b],
                dst.at[me],
                send_sems.at[at],
                recv_sems.at[at],
                (peer_of_a, peer_of_b),
            )
        dst[me] = src[me]

    pl.semaphore_wait(ready.at[1], len(blk_moves))
    send_all(face_send, face_recv, 0)

    advance_all(u_ref, u1, 7, 2)
    advance_all(u_ref, u1, 8, 3)
    wait_edges(2, rest_recv_x, rest_recv_y)
    for k, (v, z) in enumerate(far):
        mend(u1, rest_recv_x, k, v, z)
    pack(u1, later, last_send_x, last_send_y)
    send_edges(3, *last)

    def second_step(z, carry):
        advance_all(u1, out_ref, 7, z)
        return carry

    lax.fori_loop(0, 4, second_step, 0)
    for z in (2, 3):
        advance(u1, out_ref, 7, z)

    fetches[2].wait()
    fetches[3].wait()

    def per_row(column):
        return jnp.sum(
            jnp.where(iota((orders, 128), 1) == column, twiddle_ref[...], 0.0),
            axis=1,
            keepdims=True,
        )

    def rows_of(even, odd):
        return jnp.concatenate([even, odd], axis=2).reshape(spec_rows, lon)

    def waves():
        cos_turn, sin_turn = per_row(b), per_row(b + 32)
        cos_wave, sin_wave = wave_ref[0], wave_ref[1]
        cosine = (cos_turn * cos_wave - sin_turn * sin_wave).reshape(nb, 2, 1, PAIRS, lon)
        sine = (sin_turn * cos_wave + cos_turn * sin_wave).reshape(nb, 2, 1, PAIRS, lon)
        return cosine, sine

    cosine, sine = waves()
    base_high, base_low = split(rows_of(cosine, sine) * (1.0 / cols_total))
    base_ref[0] = base_high
    base_ref[1] = base_low

    wait_edges(3, last_recv_x, last_recv_y)
    for k, (v, z) in enumerate(later):
        mend(out_ref, last_recv_x, k, v, z)
    stores = [
        pltpu.make_async_copy(src, dst, out_sems.at[at])
        for at, (src, dst) in enumerate(
            [
                (out_ref, out_hbm),
                (pot_ref, pot_hbm),
                (heat_ref, heat_hbm),
                (blocks_ref, blocks_hbm),
            ]
        )
    ]
    stores[0].start()

    take(face_recv.at[pl.ds(0, count - 1)], recv_sems.at[0])
    got = face_recv[...].reshape(slots, 128)
    swapped = pltpu.roll(got, 64, 1)
    label = jnp.where(lane_slot < 64, swapped, got).astype(I32)
    face = jnp.where(lane_slot < 64, got, swapped)
    tile_row, tile_col = label >> 5, label & 31
    tile_row_t = tile_row.astype(F32).T.astype(I32)
    scatter = jnp.where(iota((32, slots), 0) == tile_row_t[0:32, :], 1.0, 0.0).astype(BF16)
    scatter = jnp.concatenate([scatter, scatter], axis=1)
    col_masks = [
        jnp.where((lane_slot >> 3) + 16 * half == tile_col, 1.0, 0.0).astype(BF16)
        for half in range(2)
    ]

    def spread_bit(value, width):
        moved = pltpu.roll(value, width, 1)
        bit = (lane_slot & width) == 0
        return [jnp.where(bit, value, moved), jnp.where(bit, moved, value)]

    lines = [face]
    for width in (32, 16, 8):
        lines = [part for line in lines for part in spread_bit(line, width)]
    for r in range(8):
        line_high, line_low = split(lines[r])
        right = jnp.concatenate(
            [
                jnp.concatenate([part * mask for mask in col_masks], axis=1)
                for part in (line_high, line_low)
            ],
            axis=0,
        )
        rows = dot(scatter, right)
        forcing[0, pl.ds(r, 32, stride=8), :] = rows[:, 0:128]
        forcing[1, pl.ds(r, 32, stride=8), :] = rows[:, 128:256]

    force = split(jnp.concatenate([forcing[0], forcing[1]], axis=1))
    spectrum = dot3((base_ref[0], base_ref[1]), force, ((1,), (1,)))
    spec_send[...] = spectrum.reshape(nb, 4 * PAIRS, lat)
    for move in inner_moves:
        peer = peer_b[move[2:]]
        remote(spec_send.at[peer], spec_recv.at[b], send_sems.at[1], recv_sems.at[1], (a, peer))
    spec_recv[b] = spec_send[b]

    fetches[4].wait()
    row_of_lane = a * lat + iota((PAIRS, lat), 1)
    x = -1.0 + (2.0 * row_of_lane.astype(F32) + 1.0) / rows_total
    log_sine = jnp.log(jnp.sqrt(1.0 - x * x))
    turns = steps // 16
    heads = ratios[turns]
    low_start = jnp.exp(heads[:, 1:2] + heads[:, 0:1] * log_sine)
    high_start = jnp.exp(heads[:, 3:4] + heads[:, 2:3] * log_sine)

    def build(turn, carry):
        previous, older = carry
        block = ratios[turn]
        made = []
        for offset in range(16):
            up = block[:, offset : offset + 1]
            down = block[:, 16 + offset : 17 + offset]
            begin_low = block[:, 32 + offset : 33 + offset]
            begin_high = block[:, 48 + offset : 49 + offset]
            present = (
                begin_low * low_start + begin_high * high_start + up * x * previous - down * older
            )
            made.append(present)
            older, previous = previous, present
        where = pl.ds(pl.multiple_of(turn * 128, 128), 128)
        for at, part in enumerate(split3(jnp.concatenate(made, axis=0))):
            leg[at, where, :] = part
        return previous, older

    empty = jnp.zeros((PAIRS, lat), F32)
    lax.fori_loop(0, turns, build, (empty, empty))

    width = steps * PAIRS
    at_step = iota((PAIRS, width), 1) // PAIRS
    at_pair = lax.rem(iota((PAIRS, width), 1), PAIRS)
    order_low = b * PAIRS + at_pair
    is_high = at_step <= order_low
    degree = jnp.where(is_high, orders - 1 - order_low + at_step, at_step - 1).astype(F32)
    scale = (2.0 / rows_total) * GAIN / (degree * (degree + 1.0) + SCREENING)
    scale = jnp.where(at_step <= orders, scale, 0.0)
    mine = at_pair == iota((PAIRS, width), 0)
    mask_ref[0] = jnp.where(mine & jnp.logical_not(is_high), scale, 0.0)
    mask_ref[1] = jnp.where(mine & is_high, scale, 0.0)

    order_col, weight_col = per_row(64), per_row(65)
    cosine, sine = waves()
    weight = weight_col.reshape(nb, 2, 1, PAIRS, 1)
    slope_weight = (weight_col * order_col).reshape(nb, 2, 1, PAIRS, 1)
    value_high, value_low = split(rows_of(cosine * weight, sine * weight))
    values_ref[0, :, 0:lon] = value_high
    values_ref[1, :, 0:lon] = value_low
    slope_high, slope_low = split(rows_of(-sine * slope_weight, cosine * slope_weight))
    values_ref[0, :, lon : 2 * lon] = slope_high
    values_ref[1, :, lon : 2 * lon] = slope_low

    take(spec_recv.at[pl.ds(0, nb - 1)], recv_sems.at[1])
    spec = spec_recv[0]
    for at in range(1, nb):
        spec = spec + spec_recv[at]
    spec_high, spec_low = split(spec)
    both = dot(jnp.concatenate([spec_high, spec_low], axis=0), leg[0], ((1,), (1,)))
    wide_sums = both[0:32] + both[32:64] + dot(spec_high, leg[1], ((1,), (1,)))
    for parity in range(2):
        low_rows = wide_sums[parity * 8 : parity * 8 + 8]
        high_rows = wide_sums[16 + parity * 8 : 24 + parity * 8]
        kept = low_rows * mask_ref[0] + high_rows * mask_ref[1]
        coef_send[parity : parity + 1, :] = jnp.sum(kept, axis=0, keepdims=True)
    for move in blk_moves:
        remote(
            coef_send,
            coef_recv.at[a],
            send_sems.at[2],
            recv_sems.at[2],
            (peer_a[move[:2]], b),
        )
    coef_recv[a] = coef_send[...]
    take(coef_recv.at[pl.ds(0, na - 1)], recv_sems.at[2])
    solved = coef_recv[0]
    for at in range(1, na):
        solved = solved + coef_recv[at]
    expanded = []
    for kind in range(2):
        for parity in range(2):
            expanded.append(
                jnp.where(
                    mask_ref[kind] != 0.0,
                    jnp.broadcast_to(solved[parity : parity + 1, :], (PAIRS, width)),
                    0.0,
                )
            )
    solved_high, solved_low = split(jnp.concatenate(expanded, axis=0))
    solved_both = jnp.concatenate([solved_high, solved_low], axis=0)
    fine = dot(solved_high, leg[2])
    both = dot(solved_both, leg[0])
    middle = dot(solved_both, leg[1])
    syn_all[b] = both[0:32] + (both[32:64] + (middle[0:32] + (middle[32:64] + fine)))
    for move in inner_moves:
        remote(
            syn_all.at[b],
            syn_all.at[b],
            send_sems.at[3],
            recv_sems.at[3],
            (a, peer_b[move[2:]]),
        )
    take(syn_all.at[pl.ds(0, nb - 1)], recv_sems.at[3])

    syn_high, syn_middle, syn_low = split3(syn_all[...].reshape(spec_rows, lat).T)

    def potential_of(high, middle, low):
        rows = high.shape[0]
        coarse = dot(jnp.concatenate([high, middle, low], axis=0), values_ref[0, :, 0:lon])
        rest_of = dot(jnp.concatenate([high, middle], axis=0), values_ref[1, :, 0:lon])
        return coarse[0:rows] + (
            coarse[rows : 2 * rows] + (rest_of[0:rows] + (coarse[2 * rows :] + rest_of[rows:]))
        )

    def rims_of(part):
        return jnp.concatenate([part[0:16], part[lat - 16 :]], axis=0)

    rims = potential_of(rims_of(syn_high), rims_of(syn_middle), rims_of(syn_low))
    rim_send[0] = rims[0:8]
    rim_send[1] = rims[24:32]
    remote(rim_send.at[1], rim_recv.at[0], rim_sems.at[0, 0], rim_sems.at[1, 0], (up_a, b))
    remote(rim_send.at[0], rim_recv.at[1], rim_sems.at[0, 1], rim_sems.at[1, 1], (down_a, b))
    potential = potential_of(syn_high, syn_middle, syn_low)
    pot_ref[...] = potential
    stores[1].start()
    turned_slopes = dot(
        jnp.concatenate([syn_high, syn_middle], axis=0), values_ref[0, :, lon : 2 * lon]
    )
    azimuthal = turned_slopes[0:lat] + (
        turned_slopes[lat:] + dot(syn_high, values_ref[1, :, lon : 2 * lon])
    )
    fetches[5].wait()
    grid_row = iota((lat, 1), 0)
    global_row = a * lat + grid_row
    x_col = -1.0 + (2.0 * global_row.astype(F32) + 1.0) / rows_total
    sine_col = jnp.sqrt(1.0 - x_col * x_col)
    eastward = azimuthal / sine_col
    take(rim_recv.at[0], rim_sems.at[1, 0])
    take(rim_recv.at[1], rim_sems.at[1, 1])
    above = jnp.where(grid_row == lat - 1, rim_recv[1, 0:1, :], pltpu.roll(potential, lat - 1, 0))
    below = jnp.where(grid_row == 0, rim_recv[0, 7:8, :], pltpu.roll(potential, 1, 0))
    inverse = rows_total / 2.0
    at_first, at_last = global_row == 0, global_row == rows_total - 1
    slope = (jnp.where(at_last, potential, above) - jnp.where(at_first, potential, below)) * (
        jnp.where(at_first | at_last, inverse, 0.5 * inverse)
    )
    polar = sine_col * slope
    heating = ped_ref[...] * (polar * polar + eastward * eastward)
    heat_ref[...] = heating
    stores[2].start()

    grids[0] = potential[:, 0:128]
    grids[1] = potential[:, 128:256]
    grids[2] = heating[:, 0:128]
    grids[3] = heating[:, 128:256]
    pick = iota((slots, 128), 1)
    pick = jnp.where((pick < 96) & ((pick & 31) == tile_row), 1.0, 0.0).astype(BF16)
    bits = [(tile_col & (1 << at)) != 0 for at in range(5)]
    upper = lane_slot >= 64
    for r in range(8):
        rows = jnp.concatenate([grids[at, pl.ds(r, 32, stride=8), :] for at in range(4)], axis=1)
        high, middle, low = split3(rows)
        parts = jnp.concatenate([high, middle, low, jnp.zeros_like(low)], axis=0)
        picked = dot(pick, parts)
        pot = jnp.where(bits[4], picked[:, 128:256], picked[:, 0:128])
        heat = jnp.where(bits[4], picked[:, 384:512], picked[:, 256:384])
        wide[r] = jnp.where(
            upper,
            jnp.where(bits[3], heat, pltpu.roll(heat, 64, 1)),
            jnp.where(bits[3], pltpu.roll(pot, 64, 1), pot),
        )

    def join(first, second, at):
        width = 8 << at
        return jnp.where(
            (lane_slot & width) == 0,
            jnp.where(bits[at], pltpu.roll(first, 128 - width, 1), first),
            jnp.where(bits[at], second, pltpu.roll(second, width, 1)),
        )

    quads = [join(wide[r], wide[r + 4], 2) for r in range(4)]
    twos = [join(quads[r], quads[r + 2], 1) for r in range(2)]
    reply_send[...] = join(twos[0], twos[1], 0).reshape(count, cap, 128)
    send_all(reply_send, reply_recv, 4)
    chosen = jnp.where(iota((256, slots), 1).astype(F32) == slot[:, 0:1], 1.0, 0.0).astype(BF16)
    take(reply_recv.at[pl.ds(0, count - 1)], recv_sems.at[4])
    back_high, back_low = split(reply_recv[...].reshape(slots, 128))
    blocks_ref[...] = dot(chosen, back_high) + dot(chosen, back_low)

    stores[3].start()

    for store in stores:
        store.wait()
    for at, (sent_x, sent_y, _, _) in enumerate((first, of_faces, rest, last)):
        drain_edges(at, sent_x, sent_y)
    take(face_send.at[pl.ds(0, count - 1)], send_sems.at[0])
    take(spec_send.at[pl.ds(0, nb - 1)], send_sems.at[1])
    take(coef_recv.at[pl.ds(0, na - 1)], send_sems.at[2])
    take(syn_all.at[pl.ds(0, nb - 1)], send_sems.at[3])
    take(reply_send.at[pl.ds(0, count - 1)], send_sems.at[4])
    take(rim_send.at[0], rim_sems.at[0, 1])
    take(rim_send.at[1], rim_sems.at[0, 0])


def write_out(slab, potential, heating, blocks, *refs):
    sources, targets, held = (slab, potential, heating, blocks), refs[0:4], refs[4:8]
    sems = refs[8]
    pieces = [(0, lambda ref, v=v: ref.at[v]) for v in range(8)]
    pieces += [(at, lambda ref: ref) for at in range(1, 4)]
    reads = [
        pltpu.make_async_copy(view(sources[at]), view(held[at]), sems.at[0, k])
        for k, (at, view) in enumerate(pieces)
    ]
    writes = [
        pltpu.make_async_copy(view(held[at]), view(targets[at]), sems.at[1, k])
        for k, (at, view) in enumerate(pieces)
    ]
    for read in reads:
        read.start()
    for read, write in zip(reads, writes):
        read.wait()
        write.start()
    for write in writes:
        write.wait()


def solution(mesh):
    na, nb = mesh.shape["blk"], mesh.shape["inner"]
    count = na * nb

    def shards(slab, speeds, source_matrix, pedersen, owners, tile_positions):
        lat, lon = pedersen.shape
        blocks = owners.shape[0]
        cap = max(2, 2 * blocks // count)
        slots = count * cap
        orders = PAIRS * 2 * nb
        wave, twiddle, table, steps = spectral_tables(na, nb, lat, lon)
        width = steps * PAIRS
        vmem = pl.BlockSpec(memory_space=pltpu.VMEM)
        hbm = pl.BlockSpec(memory_space=pl.ANY)
        dma = pltpu.SemaphoreType.DMA
        shapes = (slab.shape, (lat, lon), (lat, lon), (blocks, 128))

        def edges(rows_x, rows_y):
            return [
                pltpu.VMEM((2, rows_x, 128), F32),
                pltpu.VMEM((rows_y, 128), F32),
                pltpu.VMEM((2, rows_x, 128), F32),
                pltpu.VMEM((2, rows_y, 128), F32),
            ]

        results = pl.pallas_call(
            functools.partial(kernel, (na, nb, steps)),
            out_shape=tuple(jax.ShapeDtypeStruct(shape, F32) for shape in shapes),
            in_specs=[
                hbm,
                hbm,
                pl.BlockSpec(memory_space=pltpu.SMEM),
                hbm,
                vmem,
                vmem,
                hbm,
                hbm,
                hbm,
            ],
            out_specs=(hbm,) * 4,
            scratch_shapes=[
                *(pltpu.VMEM(shape, F32) for shape in shapes),
                pltpu.VMEM(slab.shape, F32),
                pltpu.VMEM(speeds.shape, F32),
                pltpu.VMEM((lat, lon), F32),
                pltpu.VMEM(wave.shape, F32),
                pltpu.VMEM(twiddle.shape, F32),
                pltpu.VMEM((steps // 16 + 1, PAIRS, 128), F32),
                pltpu.VMEM((7, 4, 128, 128), F32),
                pltpu.VMEM((8, 4, 128, 128), F32),
                *edges(24, 40),
                *edges(16, 32),
                *edges(8, 8),
                *edges(32, 64),
                pltpu.VMEM((128, 128), F32),
                pltpu.VMEM((slots, 256), BF16),
                pltpu.VMEM((slots, 128), F32),
                pltpu.VMEM((count, cap, 128), F32),
                pltpu.VMEM((count, cap, 128), F32),
                pltpu.VMEM((2, lat, 128), F32),
                pltpu.VMEM((2, 2 * orders, lon), BF16),
                pltpu.VMEM((2, 2 * orders, 2 * lon), BF16),
                pltpu.VMEM((nb, 4 * PAIRS, lat), F32),
                pltpu.VMEM((nb, 4 * PAIRS, lat), F32),
                pltpu.VMEM((3, width, lat), BF16),
                pltpu.VMEM((2, PAIRS, width), F32),
                pltpu.VMEM((2, width), F32),
                pltpu.VMEM((na, 2, width), F32),
                pltpu.VMEM((nb, 4 * PAIRS, lat), F32),
                pltpu.VMEM((2, 8, lon), F32),
                pltpu.VMEM((2, 8, lon), F32),
                pltpu.VMEM((4, lat, 128), F32),
                pltpu.VMEM((8, slots, 128), F32),
                pltpu.VMEM((count, cap, 128), F32),
                pltpu.VMEM((count, cap, 128), F32),
                dma((2, 4, 4)),
                dma((5,)),
                dma((5,)),
                dma((2, 2)),
                dma((6,)),
                dma((4,)),
                pltpu.SemaphoreType.REGULAR((2,)),
            ],
            compiler_params=pltpu.CompilerParams(
                collective_id=0, has_side_effects=True, vmem_limit_bytes=VMEM_LIMIT
            ),
        )(
            slab,
            speeds,
            source_matrix,
            pedersen,
            owners.reshape(1, blocks),
            tile_positions.reshape(1, blocks),
            jnp.asarray(wave),
            jnp.asarray(twiddle),
            jnp.asarray(table),
        )
        return pl.pallas_call(
            write_out,
            out_shape=tuple(jax.ShapeDtypeStruct(shape, F32) for shape in shapes),
            in_specs=[hbm] * 4,
            out_specs=(hbm,) * 4,
            scratch_shapes=[*(pltpu.VMEM(shape, F32) for shape in shapes), dma((2, 11))],
            compiler_params=pltpu.CompilerParams(vmem_limit_bytes=VMEM_LIMIT),
        )(*results)

    in_specs = (
        P(None, None, "blk", "inner"),
        P(None, None, "blk", "inner"),
        P(),
        P("blk", "inner"),
        P(("blk", "inner"), None),
        P(("blk", "inner")),
    )
    out_specs = (
        P(None, None, "blk", "inner"),
        P("blk", "inner"),
        P("blk", "inner"),
        P(("blk", "inner"), None),
    )
    return jax.shard_map(shards, mesh=mesh, in_specs=in_specs, out_specs=out_specs, check_vma=False)
```

```python
import functools
import math

import jax
import jax.numpy as jnp
import numpy as np
from jax import lax
from jax.experimental import pallas as pl
from jax.experimental.pallas import tpu as pltpu
from jax.sharding import PartitionSpec as P

F32 = jnp.float32
BF16 = jnp.bfloat16
I32 = jnp.int32
MESH = pl.DeviceIdType.MESH
BLOCK = 8
PAIRS = 8
SCREENING = 2.0
GAIN = 4096.0
VMEM_LIMIT = 60 * 1024 * 1024


def iota(shape, dim):
    return lax.broadcasted_iota(I32, shape, dim)


def split(value):
    high = value.astype(BF16)
    return high, (value - high.astype(F32)).astype(BF16)


def split3(value):
    high = value.astype(BF16)
    rest = value - high.astype(F32)
    middle = rest.astype(BF16)
    return high, middle, (rest - middle.astype(F32)).astype(BF16)


def dot(left, right, dims=((1,), (0,))):
    return lax.dot_general(left, right, (dims, ((), ())), preferred_element_type=F32)


def dot3(left, right, dims):
    lh, ll = left
    rh, rl = right
    return dot(lh, rh, dims) + dot(ll, rh, dims) + dot(lh, rl, dims)


def spectral_tables(blk_count, inner_count, lat_dev, lon_dev):
    orders = PAIRS * 2 * inner_count
    degrees = orders
    lon_total = lon_dev * inner_count
    first = np.arange(inner_count * PAIRS).reshape(inner_count, 1, PAIRS)
    order_of = np.concatenate([first, orders - 1 - first], axis=1).reshape(-1)
    cols = np.arange(lon_dev)
    phase = (order_of[:, None] * cols[None, :] % lon_total) * (2.0 * math.pi / lon_total)
    wave = np.stack([np.cos(phase), np.sin(phase)]).astype(np.float32)
    turn = (order_of[:, None] * (np.arange(inner_count) * lon_dev)[None, :] % lon_total) * (
        2.0 * math.pi / lon_total
    )
    twiddle = np.zeros((order_of.shape[0], 128), np.float32)
    twiddle[:, :inner_count] = np.cos(turn)
    twiddle[:, 32 : 32 + inner_count] = np.sin(turn)
    twiddle[:, 64] = order_of
    twiddle[:, 65] = np.where(order_of == 0, 1.0, 2.0)

    turns = -(-(degrees + 1) // 16)
    steps = turns * 16
    table = np.zeros((inner_count, turns + 1, PAIRS, 128), np.float32)

    def up(degree, order):
        return np.sqrt(
            np.float32(4.0 * degree * degree - 1.0) / np.float32(degree * degree - order * order)
        )

    counter = np.arange(1, orders, dtype=np.float64)
    log_start = 0.5 * np.log(0.5) + np.concatenate(
        [np.zeros(1), np.cumsum(0.5 * np.log((2.0 * counter + 1.0) / (2.0 * counter)))]
    )
    for pair in range(inner_count * PAIRS):
        place, lane = divmod(pair, PAIRS)
        low, partner = pair, orders - 1 - pair
        table[place, turns, lane, :4] = [low, log_start[low], partner, log_start[partner]]
        for step in range(degrees + 1):
            if step <= low:
                order, degree, kind = partner, partner + step, 3
            else:
                order, degree, kind = low, step - 1, 2
            turn_at, offset = divmod(step, 16)
            if degree == order:
                table[place, turn_at, lane, kind * 16 + offset] = 1.0
                continue
            ratio = up(degree, order)
            table[place, turn_at, lane, offset] = ratio
            if degree >= order + 2:
                table[place, turn_at, lane, 16 + offset] = ratio / up(degree - 1, order)
    return wave, twiddle, table, steps


def kernel(
    sizes,
    u_hbm,
    w_hbm,
    mix_ref,
    ped_hbm,
    owner_ref,
    tile_ref,
    wave_hbm,
    twiddle_hbm,
    table_hbm,
    out_ref,
    pot_ref,
    heat_ref,
    blocks_ref,
    u_ref,
    w_ref,
    ped_ref,
    wave_ref,
    twiddle_ref,
    ratios,
    coef,
    u1,
    first_send_x,
    first_send_y,
    first_recv_x,
    first_recv_y,
    rest_send_x,
    rest_send_y,
    rest_recv_x,
    rest_recv_y,
    face_send_x,
    face_send_y,
    face_recv_x,
    face_recv_y,
    last_send_x,
    last_send_y,
    last_recv_x,
    last_recv_y,
    turned,
    sel_t,
    label_ref,
    face_send,
    face_recv,
    forcing,
    base_ref,
    values_ref,
    spec_send,
    spec_recv,
    leg,
    mask_ref,
    coef_send,
    coef_recv,
    syn_all,
    rim_send,
    rim_recv,
    grids,
    wide,
    reply_send,
    reply_recv,
    edge_sems,
    send_sems,
    recv_sems,
    rim_sems,
    in_sems,
    ready,
):
    na, nb, steps = sizes
    count = na * nb
    lat, lon = ped_ref.shape
    rows_total, cols_total = lat * na, lon * nb
    cap = face_send.shape[1]
    slots = count * cap
    a, b = lax.axis_index("blk"), lax.axis_index("inner")
    me = a * nb + b
    orders = PAIRS * 2 * nb
    spec_rows = 2 * orders

    nx, nz = na // 2, min(4, nb)
    ny = nb // nz
    chip_x, core, chip_y, chip_z = a // 2, lax.rem(a, 2), b // nz, lax.rem(b, nz)
    peer_a = {
        (dx, dc): lax.rem(chip_x + dx, nx) * 2 + lax.rem(core + dc, 2)
        for dx in range(nx)
        for dc in range(2)
    }
    peer_b = {
        (dy, dz): lax.rem(chip_y + dy, ny) * nz + lax.rem(chip_z + dz, nz)
        for dy in range(ny)
        for dz in range(nz)
    }

    def hops(move):
        dx, dc, dy, dz = move
        return 2 * (min(dx, nx - dx) + min(dy, ny - dy) + min(dz, nz - dz)) + dc

    moves = sorted(
        [(dx, dc, dy, dz) for dx, dc in peer_a for dy, dz in peer_b if (dx, dc, dy, dz) != (0, 0, 0, 0)],
        key=hops,
        reverse=True,
    )
    blk_moves = [move for move in moves if move[2:] == (0, 0)]
    inner_moves = [move for move in moves if move[:2] == (0, 0)]

    def device(move):
        return peer_a[move[:2]], peer_b[move[2:]]

    def remote(src, dst, send_sem, recv_sem, target):
        pltpu.make_async_remote_copy(
            src_ref=src,
            dst_ref=dst,
            send_sem=send_sem,
            recv_sem=recv_sem,
            device_id=target,
            device_id_type=MESH,
        ).start()

    def take(ref, sem):
        pltpu.make_async_copy(ref, ref, sem).wait()

    def signal(sem, target):
        pl.semaphore_signal(sem, inc=1, device_id=target, device_id_type=MESH)

    up_a, down_a = lax.rem(a + 1, na), lax.rem(a + na - 1, na)
    up_b, down_b = lax.rem(b + 1, nb), lax.rem(b + nb - 1, nb)

    barrier = pltpu.get_barrier_semaphore()
    y_moves = [move for move in inner_moves if move[3] == 0]
    z_moves = [move for move in inner_moves if move[2] == 0]
    greeted = [device(move) for move in blk_moves + y_moves + z_moves]
    greeted += [(a, up_b), (a, down_b)]
    for target in greeted:
        signal(barrier, target)
    fetches = [
        pltpu.make_async_copy(src, dst, in_sems.at[at])
        for at, (src, dst) in enumerate(
            [
                (w_hbm, w_ref),
                (u_hbm.at[:, pl.ds(0, 2)], u_ref.at[:, pl.ds(0, 2)]),
                (twiddle_hbm, twiddle_ref),
                (wave_hbm, wave_ref),
                (table_hbm.at[b], ratios),
                (ped_hbm, ped_ref),
                (u_hbm.at[:, pl.ds(2, 2)], u_ref.at[:, pl.ds(2, 2)]),
            ]
        )
    ]
    for at in (0, 1, 6, 2, 3, 4, 5):
        fetches[at].start()

    row = iota((128, 128), 0)
    lane = iota((128, 128), 1)
    row8 = iota((8, 128), 0)
    fetches[0].wait()

    def make_coef(z, carry):
        wx, wy = 0.15 * w_ref[0, z], 0.15 * w_ref[1, z]
        coef[0, z] = jnp.where(row == 127, 0.0, 0.15 + wx)
        coef[1, z] = jnp.where(row == 0, 0.0, 0.15 - wx)
        coef[2, z] = jnp.where(lane == 127, 0.0, 0.15 + wy)
        coef[3, z] = jnp.where(lane == 0, 0.0, 0.15 - wy)
        below = 0.15 + 0.15 * w_ref[2, jnp.maximum(z - 1, 0)]
        above = 0.15 - 0.15 * w_ref[2, jnp.minimum(z + 1, 3)]
        coef[4, z] = jnp.where(z > 0, below, 0.0)
        coef[5, z] = jnp.where(z < 3, above, 0.0)
        coef[6, z] = jnp.where(lane == 0, 0.15 - wy, 0.15 + wy)
        return carry

    lax.fori_loop(0, 4, make_coef, 0)
    fetches[1].wait()
    fetches[6].wait()

    def pack(src, items, send_x, send_y):
        packed = jnp.zeros((128, 128), F32)
        for k, (v, z) in enumerate(items):
            last = (0.15 + 0.15 * w_ref[0, z, 120:128, :]) * src[v, z, 120:128, :]
            first = (0.15 - 0.15 * w_ref[0, z, 0:8, :]) * src[v, z, 0:8, :]
            send_x[0, k : k + 1, :] = last[7:8, :]
            send_x[1, k : k + 1, :] = first[0:1, :]
            rolled = pltpu.roll(coef[6, z] * src[v, z], 2 * k + 1, 1)
            packed = jnp.where((lane == 2 * k) | (lane == 2 * k + 1), rolled, packed)
        send_y[...] = packed.T[0 : send_y.shape[0], :]

    def send_edges(at, send_x, send_y, recv_x, recv_y):
        for side, target in ((0, (up_a, b)), (1, (down_a, b))):
            remote(
                send_x.at[side],
                recv_x.at[side],
                edge_sems.at[0, at, side],
                edge_sems.at[1, at, side],
                target,
            )
        for side, target in ((0, (a, up_b)), (1, (a, down_b))):
            remote(
                send_y,
                recv_y.at[side],
                edge_sems.at[0, at, 2 + side],
                edge_sems.at[1, at, 2 + side],
                target,
            )

    def wait_edges(at, recv_x, recv_y):
        for side in range(2):
            take(recv_x.at[side], edge_sems.at[1, at, side])
            take(recv_y.at[side], edge_sems.at[1, at, 2 + side])
        rows = recv_y.shape[1]
        odd = (iota((rows, 128), 0) & 1) == 1
        up = jnp.where(b > 0, recv_y[0], 0.0)
        down = jnp.where(b < nb - 1, recv_y[1], 0.0)
        mixed = jnp.where(odd, pltpu.roll(up, 1, 0), pltpu.roll(down, rows - 1, 0))
        if rows < 128:
            mixed = jnp.concatenate([mixed, jnp.zeros((128 - rows, 128), F32)], axis=0)
        turned[...] = mixed.T

    def drain_edges(at, send_x, send_y):
        for side in range(2):
            take(send_x.at[side], edge_sems.at[0, at, side])
            take(send_y, edge_sems.at[0, at, 2 + side])

    def mend(dst, recv_x, k, v, z):
        rolled = pltpu.roll(turned[...], 127 - 2 * k, 1)
        whole = dst[v, z] + jnp.where((lane == 0) | (lane == 127), rolled, 0.0)
        from_down = jnp.where(a > 0, recv_x[0, k : k + 1, :], 0.0)
        from_up = jnp.where(a < na - 1, recv_x[1, k : k + 1, :], 0.0)
        dst[v, z, 8:120, :] = whole[8:120]
        dst[v, z, 0:8, :] = whole[0:8] + jnp.where(row8 == 0, from_down, 0.0)
        dst[v, z, 120:128, :] = whole[120:128] + jnp.where(row8 == 7, from_up, 0.0)

    def advance(src, dst, v, z):
        u = src[v, z]
        total = mix_ref[v, 0] * src[0, z]
        for w in range(1, 8):
            total = total + mix_ref[v, w] * src[w, z]
        total = 0.3 * total + 0.1 * u
        total = total + pltpu.roll(coef[0, z] * u, 1, 0) + pltpu.roll(coef[1, z] * u, 127, 0)
        total = total + pltpu.roll(coef[2, z] * u, 1, 1) + pltpu.roll(coef[3, z] * u, 127, 1)
        if not (isinstance(z, int) and z == 0):
            total = total + coef[4, z] * src[v, z - 1 if isinstance(z, int) else jnp.maximum(z - 1, 0)]
        if not (isinstance(z, int) and z == 3):
            total = total + coef[5, z] * src[v, z + 1 if isinstance(z, int) else jnp.minimum(z + 1, 3)]
        dst[v, z] = total

    def advance_all(src, dst, vs, z):
        def one(v, carry):
            advance(src, dst, v, z)
            return carry

        lax.fori_loop(0, vs, one, 0)

    near = [(v, z) for z in (0, 1) for v in range(8)] + [(7, 2)]
    far = [(v, 2) for v in range(7)] + [(v, 3) for v in range(8)]
    faced = [(7, 0), (7, 1)]
    later = [(v, z) for z in range(4) for v in range(8) if (v, z) not in faced]
    first = (first_send_x, first_send_y, first_recv_x, first_recv_y)
    rest = (rest_send_x, rest_send_y, rest_recv_x, rest_recv_y)
    of_faces = (face_send_x, face_send_y, face_recv_x, face_recv_y)
    last = (last_send_x, last_send_y, last_recv_x, last_recv_y)

    pack(u_ref, near, first_send_x, first_send_y)
    pl.semaphore_wait(barrier, len(greeted))
    send_edges(0, *first)
    for move in y_moves:
        signal(ready.at[0], device(move))
    for z in (0, 1):
        advance_all(u_ref, u1, 8, z)
    advance(u_ref, u1, 7, 2)
    if y_moves:
        pl.semaphore_wait(ready.at[0], len(y_moves))
    for move in blk_moves:
        signal(ready.at[1], device(move))
    wait_edges(0, first_recv_x, first_recv_y)
    for k, (v, z) in enumerate(near):
        mend(u1, first_recv_x, k, v, z)

    pack(u1, faced, face_send_x, face_send_y)
    send_edges(1, *of_faces)
    for z in (0, 1):
        advance(u1, out_ref, 7, z)

    owner = jnp.broadcast_to(owner_ref[...].astype(F32), (128, 256)).T.astype(I32)
    owner_hot = jnp.where(iota((256, 128), 1) == owner, 1.0, 0.0)
    earlier = jnp.where(iota((256, 256), 0) > iota((256, 256), 1), 1.0, 0.0).astype(BF16)
    before = dot(earlier, owner_hot.astype(BF16))
    rank = jnp.sum(before * owner_hot, axis=1, keepdims=True)
    slot = owner.astype(F32) * float(cap) + rank
    slot_row = slot.T[0:1, :]
    sel = jnp.where(iota((slots, 256), 0).astype(F32) == slot_row, 1.0, 0.0).astype(BF16)
    flip = jnp.where(iota((256, 256), 0) == (iota((256, 256), 1) ^ 7), 1.0, 0.0).astype(BF16)
    sel_t[...] = dot(sel, flip).astype(BF16)
    tile_high, tile_low = split(jnp.broadcast_to(tile_ref[...].astype(F32), (128, 256)).T)
    label_ref[...] = dot(sel, tile_high) + dot(sel, tile_low)
    pack(u_ref, far, rest_send_x, rest_send_y)
    send_edges(2, *rest)

    wait_edges(1, face_recv_x, face_recv_y)
    for k, (v, z) in enumerate(faced):
        mend(out_ref, face_recv_x, k, v, z)
    current = out_ref[7, 1] - out_ref[7, 0]

    halves = [pltpu.roll(current, 64, 1).reshape(16, 8, 128), current.reshape(16, 8, 128)]
    group = iota((16, 8, 128), 2) // 8
    faces = []
    for half in range(2):
        face = jnp.zeros((16, 8, 128), F32)
        for r in range(8):
            spread = jnp.broadcast_to(halves[half][:, r : r + 1, :], (16, 8, 128))
            moved = pltpu.roll(spread, 8 * r + 8, 2, stride=8, stride_axis=1)
            face = jnp.where(group == r, moved, face)
        faces.append(face)
    faces = jnp.stack(faces, axis=1).reshape(256, 128)
    face_high, face_low = split(faces)
    routed = dot(sel_t[...], face_high) + dot(sel_t[...], face_low)
    lane_slot = iota((slots, 128), 1)
    routed = jnp.where(lane_slot < 64, routed, label_ref[...])
    face_send[...] = routed.reshape(count, cap, 128)

    def send_all(src, dst, at):
        for move in moves:
            peer_of_a, peer_of_b = device(move)
            remote(
                src.at[peer_of_a * nb + peer_of_b],
                dst.at[me],
                send_sems.at[at],
                recv_sems.at[at],
                (peer_of_a, peer_of_b),
            )
        dst[me] = src[me]

    pl.semaphore_wait(ready.at[1], len(blk_moves))
    send_all(face_send, face_recv, 0)

    advance_all(u_ref, u1, 7, 2)
    advance_all(u_ref, u1, 8, 3)
    wait_edges(2, rest_recv_x, rest_recv_y)
    for k, (v, z) in enumerate(far):
        mend(u1, rest_recv_x, k, v, z)
    pack(u1, later, last_send_x, last_send_y)
    send_edges(3, *last)

    fetches[2].wait()
    fetches[3].wait()

    def per_row(column):
        return jnp.sum(
            jnp.where(iota((orders, 128), 1) == column, twiddle_ref[...], 0.0),
            axis=1,
            keepdims=True,
        )

    def rows_of(even, odd):
        return jnp.concatenate([even, odd], axis=2).reshape(spec_rows, lon)

    def waves():
        cos_turn, sin_turn = per_row(b), per_row(b + 32)
        cos_wave, sin_wave = wave_ref[0], wave_ref[1]
        cosine = (cos_turn * cos_wave - sin_turn * sin_wave).reshape(nb, 2, 1, PAIRS, lon)
        sine = (sin_turn * cos_wave + cos_turn * sin_wave).reshape(nb, 2, 1, PAIRS, lon)
        return cosine, sine

    cosine, sine = waves()
    base_high, base_low = split(rows_of(cosine, sine) * (1.0 / cols_total))
    base_ref[0] = base_high
    base_ref[1] = base_low

    take(face_recv.at[pl.ds(0, count - 1)], recv_sems.at[0])
    got = face_recv[...].reshape(slots, 128)
    swapped = pltpu.roll(got, 64, 1)
    label = jnp.where(lane_slot < 64, swapped, got).astype(I32)
    face = jnp.where(lane_slot < 64, got, swapped)
    tile_row, tile_col = label >> 5, label & 31
    tile_row_t = tile_row.astype(F32).T.astype(I32)
    scatter = jnp.where(iota((32, slots), 0) == tile_row_t[0:32, :], 1.0, 0.0).astype(BF16)
    scatter = jnp.concatenate([scatter, scatter], axis=1)
    col_masks = [
        jnp.where((lane_slot >> 3) + 16 * half == tile_col, 1.0, 0.0).astype(BF16)
        for half in range(2)
    ]

    def spread_bit(value, width):
        moved = pltpu.roll(value, width, 1)
        bit = (lane_slot & width) == 0
        return [jnp.where(bit, value, moved), jnp.where(bit, moved, value)]

    lines = [face]
    for width in (32, 16, 8):
        lines = [part for line in lines for part in spread_bit(line, width)]
    for r in range(8):
        line_high, line_low = split(lines[r])
        right = jnp.concatenate(
            [
                jnp.concatenate([part * mask for mask in col_masks], axis=1)
                for part in (line_high, line_low)
            ],
            axis=0,
        )
        rows = dot(scatter, right)
        forcing[0, pl.ds(r, 32, stride=8), :] = rows[:, 0:128]
        forcing[1, pl.ds(r, 32, stride=8), :] = rows[:, 128:256]

    force = split(jnp.concatenate([forcing[0], forcing[1]], axis=1))
    spectrum = dot3((base_ref[0], base_ref[1]), force, ((1,), (1,)))
    spec_send[...] = spectrum.reshape(nb, 4 * PAIRS, lat)
    for move in inner_moves:
        peer = peer_b[move[2:]]
        remote(spec_send.at[peer], spec_recv.at[b], send_sems.at[1], recv_sems.at[1], (a, peer))
    spec_recv[b] = spec_send[b]

    fetches[4].wait()
    row_of_lane = a * lat + iota((PAIRS, lat), 1)
    x = -1.0 + (2.0 * row_of_lane.astype(F32) + 1.0) / rows_total
    log_sine = jnp.log(jnp.sqrt(1.0 - x * x))
    turns = steps // 16
    heads = ratios[turns]
    low_start = jnp.exp(heads[:, 1:2] + heads[:, 0:1] * log_sine)
    high_start = jnp.exp(heads[:, 3:4] + heads[:, 2:3] * log_sine)

    def build(turn, carry):
        previous, older = carry
        block = ratios[turn]
        made = []
        for offset in range(16):
            up = block[:, offset : offset + 1]
            down = block[:, 16 + offset : 17 + offset]
            begin_low = block[:, 32 + offset : 33 + offset]
            begin_high = block[:, 48 + offset : 49 + offset]
            present = (
                begin_low * low_start + begin_high * high_start + up * x * previous - down * older
            )
            made.append(present)
            older, previous = previous, present
        where = pl.ds(pl.multiple_of(turn * 128, 128), 128)
        for at, part in enumerate(split3(jnp.concatenate(made, axis=0))):
            leg[at, where, :] = part
        return previous, older

    empty = jnp.zeros((PAIRS, lat), F32)
    lax.fori_loop(0, turns, build, (empty, empty))

    width = steps * PAIRS
    at_step = iota((PAIRS, width), 1) // PAIRS
    at_pair = lax.rem(iota((PAIRS, width), 1), PAIRS)
    order_low = b * PAIRS + at_pair
    is_high = at_step <= order_low
    degree = jnp.where(is_high, orders - 1 - order_low + at_step, at_step - 1).astype(F32)
    scale = (2.0 / rows_total) * GAIN / (degree * (degree + 1.0) + SCREENING)
    scale = jnp.where(at_step <= orders, scale, 0.0)
    mine = at_pair == iota((PAIRS, width), 0)
    mask_ref[0] = jnp.where(mine & jnp.logical_not(is_high), scale, 0.0)
    mask_ref[1] = jnp.where(mine & is_high, scale, 0.0)

    order_col, weight_col = per_row(64), per_row(65)
    cosine, sine = waves()
    weight = weight_col.reshape(nb, 2, 1, PAIRS, 1)
    slope_weight = (weight_col * order_col).reshape(nb, 2, 1, PAIRS, 1)
    value_high, value_low = split(rows_of(cosine * weight, sine * weight))
    values_ref[0, :, 0:lon] = value_high
    values_ref[1, :, 0:lon] = value_low
    slope_high, slope_low = split(rows_of(-sine * slope_weight, cosine * slope_weight))
    values_ref[0, :, lon : 2 * lon] = slope_high
    values_ref[1, :, lon : 2 * lon] = slope_low

    take(spec_recv.at[pl.ds(0, nb - 1)], recv_sems.at[1])
    spec = spec_recv[0]
    for at in range(1, nb):
        spec = spec + spec_recv[at]
    spec_high, spec_low = split(spec)
    both = dot(jnp.concatenate([spec_high, spec_low], axis=0), leg[0], ((1,), (1,)))
    wide_sums = both[0:32] + both[32:64] + dot(spec_high, leg[1], ((1,), (1,)))
    for parity in range(2):
        low_rows = wide_sums[parity * 8 : parity * 8 + 8]
        high_rows = wide_sums[16 + parity * 8 : 24 + parity * 8]
        kept = low_rows * mask_ref[0] + high_rows * mask_ref[1]
        coef_send[parity : parity + 1, :] = jnp.sum(kept, axis=0, keepdims=True)
    for move in blk_moves:
        remote(
            coef_send,
            coef_recv.at[a],
            send_sems.at[2],
            recv_sems.at[2],
            (peer_a[move[:2]], b),
        )
    coef_recv[a] = coef_send[...]
    for z in (0, 1):
        advance_all(u1, out_ref, 7, z)
    take(coef_recv.at[pl.ds(0, na - 1)], recv_sems.at[2])
    solved = coef_recv[0]
    for at in range(1, na):
        solved = solved + coef_recv[at]
    expanded = []
    for kind in range(2):
        for parity in range(2):
            expanded.append(
                jnp.where(
                    mask_ref[kind] != 0.0,
                    jnp.broadcast_to(solved[parity : parity + 1, :], (PAIRS, width)),
                    0.0,
                )
            )
    solved_high, solved_low = split(jnp.concatenate(expanded, axis=0))
    solved_both = jnp.concatenate([solved_high, solved_low], axis=0)
    fine = dot(solved_high, leg[2])
    both = dot(solved_both, leg[0])
    middle = dot(solved_both, leg[1])
    syn_all[b] = both[0:32] + (both[32:64] + (middle[0:32] + (middle[32:64] + fine)))
    for move in inner_moves:
        remote(
            syn_all.at[b],
            syn_all.at[b],
            send_sems.at[3],
            recv_sems.at[3],
            (a, peer_b[move[2:]]),
        )
    for z in (2, 3):
        advance_all(u1, out_ref, 8, z)
    wait_edges(3, last_recv_x, last_recv_y)
    for k, (v, z) in enumerate(later):
        mend(out_ref, last_recv_x, k, v, z)
    take(syn_all.at[pl.ds(0, nb - 1)], recv_sems.at[3])

    syn_high, syn_middle, syn_low = split3(syn_all[...].reshape(spec_rows, lat).T)

    def potential_of(high, middle, low):
        rows = high.shape[0]
        coarse = dot(jnp.concatenate([high, middle, low], axis=0), values_ref[0, :, 0:lon])
        rest_of = dot(jnp.concatenate([high, middle], axis=0), values_ref[1, :, 0:lon])
        return coarse[0:rows] + (
            coarse[rows : 2 * rows] + (rest_of[0:rows] + (coarse[2 * rows :] + rest_of[rows:]))
        )

    def rims_of(part):
        return jnp.concatenate([part[0:16], part[lat - 16 :]], axis=0)

    rims = potential_of(rims_of(syn_high), rims_of(syn_middle), rims_of(syn_low))
    rim_send[0] = rims[0:8]
    rim_send[1] = rims[24:32]
    remote(rim_send.at[1], rim_recv.at[0], rim_sems.at[0, 0], rim_sems.at[1, 0], (up_a, b))
    remote(rim_send.at[0], rim_recv.at[1], rim_sems.at[0, 1], rim_sems.at[1, 1], (down_a, b))
    potential = potential_of(syn_high, syn_middle, syn_low)
    pot_ref[...] = potential
    turned_slopes = dot(
        jnp.concatenate([syn_high, syn_middle], axis=0), values_ref[0, :, lon : 2 * lon]
    )
    azimuthal = turned_slopes[0:lat] + (
        turned_slopes[lat:] + dot(syn_high, values_ref[1, :, lon : 2 * lon])
    )
    fetches[5].wait()
    grid_row = iota((lat, 1), 0)
    global_row = a * lat + grid_row
    x_col = -1.0 + (2.0 * global_row.astype(F32) + 1.0) / rows_total
    sine_col = jnp.sqrt(1.0 - x_col * x_col)
    eastward = azimuthal / sine_col
    take(rim_recv.at[0], rim_sems.at[1, 0])
    take(rim_recv.at[1], rim_sems.at[1, 1])
    above = jnp.where(grid_row == lat - 1, rim_recv[1, 0:1, :], pltpu.roll(potential, lat - 1, 0))
    below = jnp.where(grid_row == 0, rim_recv[0, 7:8, :], pltpu.roll(potential, 1, 0))
    inverse = rows_total / 2.0
    at_first, at_last = global_row == 0, global_row == rows_total - 1
    slope = (jnp.where(at_last, potential, above) - jnp.where(at_first, potential, below)) * (
        jnp.where(at_first | at_last, inverse, 0.5 * inverse)
    )
    polar = sine_col * slope
    heating = ped_ref[...] * (polar * polar + eastward * eastward)
    heat_ref[...] = heating

    grids[0] = potential[:, 0:128]
    grids[1] = potential[:, 128:256]
    grids[2] = heating[:, 0:128]
    grids[3] = heating[:, 128:256]
    pick = iota((slots, 128), 1)
    pick = jnp.where((pick < 96) & ((pick & 31) == tile_row), 1.0, 0.0).astype(BF16)
    bits = [(tile_col & (1 << at)) != 0 for at in range(5)]
    upper = lane_slot >= 64
    for r in range(8):
        rows = jnp.concatenate([grids[at, pl.ds(r, 32, stride=8), :] for at in range(4)], axis=1)
        high, middle, low = split3(rows)
        parts = jnp.concatenate([high, middle, low, jnp.zeros_like(low)], axis=0)
        picked = dot(pick, parts)
        pot = jnp.where(bits[4], picked[:, 128:256], picked[:, 0:128])
        heat = jnp.where(bits[4], picked[:, 384:512], picked[:, 256:384])
        wide[r] = jnp.where(
            upper,
            jnp.where(bits[3], heat, pltpu.roll(heat, 64, 1)),
            jnp.where(bits[3], pltpu.roll(pot, 64, 1), pot),
        )

    def join(first, second, at):
        width = 8 << at
        return jnp.where(
            (lane_slot & width) == 0,
            jnp.where(bits[at], pltpu.roll(first, 128 - width, 1), first),
            jnp.where(bits[at], second, pltpu.roll(second, width, 1)),
        )

    quads = [join(wide[r], wide[r + 4], 2) for r in range(4)]
    twos = [join(quads[r], quads[r + 2], 1) for r in range(2)]
    reply_send[...] = join(twos[0], twos[1], 0).reshape(count, cap, 128)
    send_all(reply_send, reply_recv, 4)
    chosen = jnp.where(iota((256, slots), 1).astype(F32) == slot[:, 0:1], 1.0, 0.0).astype(BF16)
    take(reply_recv.at[pl.ds(0, count - 1)], recv_sems.at[4])
    back_high, back_low = split(reply_recv[...].reshape(slots, 128))
    blocks_ref[...] = dot(chosen, back_high) + dot(chosen, back_low)

    for at, (sent_x, sent_y, _, _) in enumerate((first, of_faces, rest, last)):
        drain_edges(at, sent_x, sent_y)
    take(face_send.at[pl.ds(0, count - 1)], send_sems.at[0])
    take(spec_send.at[pl.ds(0, nb - 1)], send_sems.at[1])
    take(coef_recv.at[pl.ds(0, na - 1)], send_sems.at[2])
    take(syn_all.at[pl.ds(0, nb - 1)], send_sems.at[3])
    take(reply_send.at[pl.ds(0, count - 1)], send_sems.at[4])
    take(rim_send.at[0], rim_sems.at[0, 1])
    take(rim_send.at[1], rim_sems.at[0, 0])


def write_out(slab, potential, heating, blocks, *refs):
    pieces = [(slab.at[v], refs[0].at[v]) for v in range(8)]
    pieces += [(potential, refs[1]), (heating, refs[2]), (blocks, refs[3])]
    copies = [
        pltpu.make_async_copy(src, dst, refs[4].at[k]) for k, (src, dst) in enumerate(pieces)
    ]
    for copy in copies:
        copy.start()
    for copy in copies:
        copy.wait()


def solution(mesh):
    na, nb = mesh.shape["blk"], mesh.shape["inner"]
    count = na * nb

    def shards(slab, speeds, source_matrix, pedersen, owners, tile_positions):
        lat, lon = pedersen.shape
        blocks = owners.shape[0]
        cap = max(2, 2 * blocks // count)
        slots = count * cap
        orders = PAIRS * 2 * nb
        wave, twiddle, table, steps = spectral_tables(na, nb, lat, lon)
        width = steps * PAIRS
        vmem = pl.BlockSpec(memory_space=pltpu.VMEM)
        hbm = pl.BlockSpec(memory_space=pl.ANY)
        dma = pltpu.SemaphoreType.DMA
        shapes = (slab.shape, (lat, lon), (lat, lon), (blocks, 128))

        def edges(rows_x, rows_y):
            return [
                pltpu.VMEM((2, rows_x, 128), F32),
                pltpu.VMEM((rows_y, 128), F32),
                pltpu.VMEM((2, rows_x, 128), F32),
                pltpu.VMEM((2, rows_y, 128), F32),
            ]

        results = pl.pallas_call(
            functools.partial(kernel, (na, nb, steps)),
            out_shape=tuple(pltpu.VMEM(shape, F32) for shape in shapes),
            in_specs=[
                hbm,
                hbm,
                pl.BlockSpec(memory_space=pltpu.SMEM),
                hbm,
                vmem,
                vmem,
                hbm,
                hbm,
                hbm,
            ],
            out_specs=(vmem,) * 4,
            scratch_shapes=[
                pltpu.VMEM(slab.shape, F32),
                pltpu.VMEM(speeds.shape, F32),
                pltpu.VMEM((lat, lon), F32),
                pltpu.VMEM(wave.shape, F32),
                pltpu.VMEM(twiddle.shape, F32),
                pltpu.VMEM((steps // 16 + 1, PAIRS, 128), F32),
                pltpu.VMEM((7, 4, 128, 128), F32),
                pltpu.VMEM((8, 4, 128, 128), F32),
                *edges(24, 40),
                *edges(16, 32),
                *edges(8, 8),
                *edges(32, 64),
                pltpu.VMEM((128, 128), F32),
                pltpu.VMEM((slots, 256), BF16),
                pltpu.VMEM((slots, 128), F32),
                pltpu.VMEM((count, cap, 128), F32),
                pltpu.VMEM((count, cap, 128), F32),
                pltpu.VMEM((2, lat, 128), F32),
                pltpu.VMEM((2, 2 * orders, lon), BF16),
                pltpu.VMEM((2, 2 * orders, 2 * lon), BF16),
                pltpu.VMEM((nb, 4 * PAIRS, lat), F32),
                pltpu.VMEM((nb, 4 * PAIRS, lat), F32),
                pltpu.VMEM((3, width, lat), BF16),
                pltpu.VMEM((2, PAIRS, width), F32),
                pltpu.VMEM((2, width), F32),
                pltpu.VMEM((na, 2, width), F32),
                pltpu.VMEM((nb, 4 * PAIRS, lat), F32),
                pltpu.VMEM((2, 8, lon), F32),
                pltpu.VMEM((2, 8, lon), F32),
                pltpu.VMEM((4, lat, 128), F32),
                pltpu.VMEM((8, slots, 128), F32),
                pltpu.VMEM((count, cap, 128), F32),
                pltpu.VMEM((count, cap, 128), F32),
                dma((2, 4, 4)),
                dma((5,)),
                dma((5,)),
                dma((2, 2)),
                dma((7,)),
                pltpu.SemaphoreType.REGULAR((2,)),
            ],
            compiler_params=pltpu.CompilerParams(
                collective_id=0, has_side_effects=True, vmem_limit_bytes=VMEM_LIMIT
            ),
        )(
            slab,
            speeds,
            source_matrix,
            pedersen,
            owners.reshape(1, blocks),
            tile_positions.reshape(1, blocks),
            jnp.asarray(wave),
            jnp.asarray(twiddle),
            jnp.asarray(table),
        )
        return pl.pallas_call(
            write_out,
            out_shape=tuple(jax.ShapeDtypeStruct(shape, F32) for shape in shapes),
            in_specs=[vmem] * 4,
            out_specs=(hbm,) * 4,
            scratch_shapes=[dma((11,))],
            compiler_params=pltpu.CompilerParams(vmem_limit_bytes=16 * 1024 * 1024),
        )(*results)

    in_specs = (
        P(None, None, "blk", "inner"),
        P(None, None, "blk", "inner"),
        P(),
        P("blk", "inner"),
        P(("blk", "inner"), None),
        P(("blk", "inner")),
    )
    out_specs = (
        P(None, None, "blk", "inner"),
        P("blk", "inner"),
        P("blk", "inner"),
        P(("blk", "inner"), None),
    )
    return jax.shard_map(shards, mesh=mesh, in_specs=in_specs, out_specs=out_specs, check_vma=False)
```

```python
import functools
import math

import jax
import jax.numpy as jnp
import numpy as np
from jax import lax
from jax.experimental import pallas as pl
from jax.experimental.pallas import tpu as pltpu
from jax.sharding import PartitionSpec as P

F32 = jnp.float32
BF16 = jnp.bfloat16
I32 = jnp.int32
MESH = pl.DeviceIdType.MESH
BLOCK = 8
PAIRS = 8
SCREENING = 2.0
GAIN = 4096.0
VMEM_LIMIT = 60 * 1024 * 1024


def iota(shape, dim):
    return lax.broadcasted_iota(I32, shape, dim)


def split(value):
    high = value.astype(BF16)
    return high, (value - high.astype(F32)).astype(BF16)


def split3(value):
    high = value.astype(BF16)
    rest = value - high.astype(F32)
    middle = rest.astype(BF16)
    return high, middle, (rest - middle.astype(F32)).astype(BF16)


def dot(left, right, dims=((1,), (0,))):
    return lax.dot_general(left, right, (dims, ((), ())), preferred_element_type=F32)


def dot3(left, right, dims):
    lh, ll = left
    rh, rl = right
    return dot(lh, rh, dims) + dot(ll, rh, dims) + dot(lh, rl, dims)


def spectral_tables(blk_count, inner_count, lat_dev, lon_dev):
    orders = PAIRS * 2 * inner_count
    degrees = orders
    lon_total = lon_dev * inner_count
    first = np.arange(inner_count * PAIRS).reshape(inner_count, 1, PAIRS)
    order_of = np.concatenate([first, orders - 1 - first], axis=1).reshape(-1)
    cols = np.arange(lon_dev)
    phase = (order_of[:, None] * cols[None, :] % lon_total) * (2.0 * math.pi / lon_total)
    wave = np.stack([np.cos(phase), np.sin(phase)]).astype(np.float32)
    turn = (order_of[:, None] * (np.arange(inner_count) * lon_dev)[None, :] % lon_total) * (
        2.0 * math.pi / lon_total
    )
    twiddle = np.zeros((order_of.shape[0], 128), np.float32)
    twiddle[:, :inner_count] = np.cos(turn)
    twiddle[:, 32 : 32 + inner_count] = np.sin(turn)
    twiddle[:, 64] = order_of
    twiddle[:, 65] = np.where(order_of == 0, 1.0, 2.0)

    turns = -(-(degrees + 1) // 16)
    steps = turns * 16
    table = np.zeros((inner_count, turns + 1, PAIRS, 128), np.float32)

    def up(degree, order):
        return np.sqrt(
            np.float32(4.0 * degree * degree - 1.0) / np.float32(degree * degree - order * order)
        )

    counter = np.arange(1, orders, dtype=np.float64)
    log_start = 0.5 * np.log(0.5) + np.concatenate(
        [np.zeros(1), np.cumsum(0.5 * np.log((2.0 * counter + 1.0) / (2.0 * counter)))]
    )
    for pair in range(inner_count * PAIRS):
        place, lane = divmod(pair, PAIRS)
        low, partner = pair, orders - 1 - pair
        table[place, turns, lane, :4] = [low, log_start[low], partner, log_start[partner]]
        for step in range(degrees + 1):
            if step <= low:
                order, degree, kind = partner, partner + step, 3
            else:
                order, degree, kind = low, step - 1, 2
            turn_at, offset = divmod(step, 16)
            if degree == order:
                table[place, turn_at, lane, kind * 16 + offset] = 1.0
                continue
            ratio = up(degree, order)
            table[place, turn_at, lane, offset] = ratio
            if degree >= order + 2:
                table[place, turn_at, lane, 16 + offset] = ratio / up(degree - 1, order)
    return wave, twiddle, table, steps


def kernel(
    sizes,
    u_hbm,
    w_hbm,
    mix_ref,
    ped_hbm,
    owner_ref,
    tile_ref,
    wave_hbm,
    twiddle_hbm,
    table_hbm,
    out_ref,
    pot_ref,
    heat_ref,
    blocks_ref,
    u_ref,
    w_ref,
    ped_ref,
    wave_ref,
    twiddle_ref,
    ratios,
    coef,
    u1,
    first_send_x,
    first_send_y,
    first_recv_x,
    first_recv_y,
    rest_send_x,
    rest_send_y,
    rest_recv_x,
    rest_recv_y,
    face_send_x,
    face_send_y,
    face_recv_x,
    face_recv_y,
    ring_x,
    corner_send,
    corner_recv,
    last_send_x,
    last_send_y,
    last_recv_x,
    last_recv_y,
    turned,
    sel_t,
    label_ref,
    face_send,
    face_recv,
    forcing,
    base_ref,
    values_ref,
    spec_send,
    spec_recv,
    leg,
    mask_ref,
    coef_send,
    coef_recv,
    syn_all,
    rim_send,
    rim_recv,
    grids,
    wide,
    reply_send,
    reply_recv,
    edge_sems,
    send_sems,
    recv_sems,
    rim_sems,
    corner_sems,
    in_sems,
    ready,
):
    na, nb, steps = sizes
    count = na * nb
    lat, lon = ped_ref.shape
    rows_total, cols_total = lat * na, lon * nb
    cap = face_send.shape[1]
    slots = count * cap
    a, b = lax.axis_index("blk"), lax.axis_index("inner")
    me = a * nb + b
    orders = PAIRS * 2 * nb
    spec_rows = 2 * orders

    nx, nz = na // 2, min(4, nb)
    ny = nb // nz
    chip_x, core, chip_y, chip_z = a // 2, lax.rem(a, 2), b // nz, lax.rem(b, nz)
    peer_a = {
        (dx, dc): lax.rem(chip_x + dx, nx) * 2 + lax.rem(core + dc, 2)
        for dx in range(nx)
        for dc in range(2)
    }
    peer_b = {
        (dy, dz): lax.rem(chip_y + dy, ny) * nz + lax.rem(chip_z + dz, nz)
        for dy in range(ny)
        for dz in range(nz)
    }

    def hops(move):
        dx, dc, dy, dz = move
        return 2 * (min(dx, nx - dx) + min(dy, ny - dy) + min(dz, nz - dz)) + dc

    moves = sorted(
        [(dx, dc, dy, dz) for dx, dc in peer_a for dy, dz in peer_b if (dx, dc, dy, dz) != (0, 0, 0, 0)],
        key=hops,
        reverse=True,
    )
    blk_moves = [move for move in moves if move[2:] == (0, 0)]
    inner_moves = [move for move in moves if move[:2] == (0, 0)]

    def device(move):
        return peer_a[move[:2]], peer_b[move[2:]]

    def remote(src, dst, send_sem, recv_sem, target):
        pltpu.make_async_remote_copy(
            src_ref=src,
            dst_ref=dst,
            send_sem=send_sem,
            recv_sem=recv_sem,
            device_id=target,
            device_id_type=MESH,
        ).start()

    def take(ref, sem):
        pltpu.make_async_copy(ref, ref, sem).wait()

    def signal(sem, target):
        pl.semaphore_signal(sem, inc=1, device_id=target, device_id_type=MESH)

    up_a, down_a = lax.rem(a + 1, na), lax.rem(a + na - 1, na)
    up_b, down_b = lax.rem(b + 1, nb), lax.rem(b + nb - 1, nb)

    barrier = pltpu.get_barrier_semaphore()
    y_moves = [move for move in inner_moves if move[3] == 0]
    z_moves = [move for move in inner_moves if move[2] == 0]
    greeted = [device(move) for move in blk_moves + y_moves + z_moves]
    greeted += [(a, up_b), (a, down_b)]
    corners = [(up_a, up_b), (up_a, down_b), (down_a, up_b), (down_a, down_b)]
    greeted += corners
    for target in greeted:
        signal(barrier, target)
    fetches = [
        pltpu.make_async_copy(src, dst, in_sems.at[at])
        for at, (src, dst) in enumerate(
            [
                (w_hbm, w_ref),
                (u_hbm.at[:, pl.ds(0, 2)], u_ref.at[:, pl.ds(0, 2)]),
                (twiddle_hbm, twiddle_ref),
                (wave_hbm, wave_ref),
                (table_hbm.at[b], ratios),
                (ped_hbm, ped_ref),
                (u_hbm.at[:, pl.ds(2, 2)], u_ref.at[:, pl.ds(2, 2)]),
            ]
        )
    ]
    for at in (0, 1, 6, 2, 3, 4, 5):
        fetches[at].start()

    row = iota((128, 128), 0)
    lane = iota((128, 128), 1)
    row8 = iota((8, 128), 0)
    fetches[0].wait()

    def make_coef(z, carry):
        wx, wy = 0.15 * w_ref[0, z], 0.15 * w_ref[1, z]
        coef[0, z] = jnp.where(row == 127, 0.0, 0.15 + wx)
        coef[1, z] = jnp.where(row == 0, 0.0, 0.15 - wx)
        coef[2, z] = jnp.where(lane == 127, 0.0, 0.15 + wy)
        coef[3, z] = jnp.where(lane == 0, 0.0, 0.15 - wy)
        below = 0.15 + 0.15 * w_ref[2, jnp.maximum(z - 1, 0)]
        above = 0.15 - 0.15 * w_ref[2, jnp.minimum(z + 1, 3)]
        coef[4, z] = jnp.where(z > 0, below, 0.0)
        coef[5, z] = jnp.where(z < 3, above, 0.0)
        coef[6, z] = jnp.where(lane == 0, 0.15 - wy, 0.15 + wy)
        return carry

    lax.fori_loop(0, 4, make_coef, 0)
    fetches[1].wait()
    fetches[6].wait()

    def pack(src, items, send_x, send_y):
        packed = jnp.zeros((128, 128), F32)
        for k, (v, z) in enumerate(items):
            last = (0.15 + 0.15 * w_ref[0, z, 120:128, :]) * src[v, z, 120:128, :]
            first = (0.15 - 0.15 * w_ref[0, z, 0:8, :]) * src[v, z, 0:8, :]
            send_x[0, k : k + 1, :] = last[7:8, :]
            send_x[1, k : k + 1, :] = first[0:1, :]
            rolled = pltpu.roll(coef[6, z] * src[v, z], 2 * k + 1, 1)
            packed = jnp.where((lane == 2 * k) | (lane == 2 * k + 1), rolled, packed)
        send_y[...] = packed.T[0 : send_y.shape[0], :]

    def send_edges(at, send_x, send_y, recv_x, recv_y):
        for side, target in ((0, (up_a, b)), (1, (down_a, b))):
            remote(
                send_x.at[side],
                recv_x.at[side],
                edge_sems.at[0, at, side],
                edge_sems.at[1, at, side],
                target,
            )
        for side, target in ((0, (a, up_b)), (1, (a, down_b))):
            remote(
                send_y,
                recv_y.at[side],
                edge_sems.at[0, at, 2 + side],
                edge_sems.at[1, at, 2 + side],
                target,
            )

    def wait_edges(at, recv_x, recv_y):
        for side in range(2):
            take(recv_x.at[side], edge_sems.at[1, at, side])
            take(recv_y.at[side], edge_sems.at[1, at, 2 + side])
        rows = recv_y.shape[1]
        odd = (iota((rows, 128), 0) & 1) == 1
        up = jnp.where(b > 0, recv_y[0], 0.0)
        down = jnp.where(b < nb - 1, recv_y[1], 0.0)
        mixed = jnp.where(odd, pltpu.roll(up, 1, 0), pltpu.roll(down, rows - 1, 0))
        if rows < 128:
            mixed = jnp.concatenate([mixed, jnp.zeros((128 - rows, 128), F32)], axis=0)
        turned[...] = mixed.T

    def drain_edges(at, send_x, send_y):
        for side in range(2):
            take(send_x.at[side], edge_sems.at[0, at, side])
            take(send_y, edge_sems.at[0, at, 2 + side])

    def mend(dst, recv_x, k, v, z):
        rolled = pltpu.roll(turned[...], 127 - 2 * k, 1)
        whole = dst[v, z] + jnp.where((lane == 0) | (lane == 127), rolled, 0.0)
        from_down = jnp.where(a > 0, recv_x[0, k : k + 1, :], 0.0)
        from_up = jnp.where(a < na - 1, recv_x[1, k : k + 1, :], 0.0)
        dst[v, z, 8:120, :] = whole[8:120]
        dst[v, z, 0:8, :] = whole[0:8] + jnp.where(row8 == 0, from_down, 0.0)
        dst[v, z, 120:128, :] = whole[120:128] + jnp.where(row8 == 7, from_up, 0.0)

    def advance(src, dst, v, z):
        u = src[v, z]
        total = mix_ref[v, 0] * src[0, z]
        for w in range(1, 8):
            total = total + mix_ref[v, w] * src[w, z]
        total = 0.3 * total + 0.1 * u
        total = total + pltpu.roll(coef[0, z] * u, 1, 0) + pltpu.roll(coef[1, z] * u, 127, 0)
        total = total + pltpu.roll(coef[2, z] * u, 1, 1) + pltpu.roll(coef[3, z] * u, 127, 1)
        if not (isinstance(z, int) and z == 0):
            total = total + coef[4, z] * src[v, z - 1 if isinstance(z, int) else jnp.maximum(z - 1, 0)]
        if not (isinstance(z, int) and z == 3):
            total = total + coef[5, z] * src[v, z + 1 if isinstance(z, int) else jnp.minimum(z + 1, 3)]
        dst[v, z] = total

    def advance_all(src, dst, vs, z):
        def one(v, carry):
            advance(src, dst, v, z)
            return carry

        lax.fori_loop(0, vs, one, 0)

    near = [(v, z) for z in (0, 1) for v in range(8)] + [(7, 2)]
    far = [(v, 2) for v in range(7)] + [(v, 3) for v in range(8)]
    faced = [(7, 0), (7, 1)]
    later = [(v, z) for z in range(4) for v in range(8) if (v, z) not in faced]
    first = (first_send_x, first_send_y, first_recv_x, first_recv_y)
    rest = (rest_send_x, rest_send_y, rest_recv_x, rest_recv_y)
    of_faces = (face_send_x, face_send_y, face_recv_x, face_recv_y)
    last = (last_send_x, last_send_y, last_recv_x, last_recv_y)

    pack(u_ref, near, first_send_x, first_send_y)
    at_0, at_1 = near.index((7, 0)), near.index((7, 1))
    for side in range(2):
        for z, k in enumerate((at_0, at_1)):
            corner_send[2 * side + z : 2 * side + z + 1, :] = first_send_x[side, k : k + 1, :]
            corner_send[4 + 2 * side + z : 5 + 2 * side + z, :] = first_send_y[
                2 * k + side : 2 * k + side + 1, :
            ]
    pl.semaphore_wait(barrier, len(greeted))
    send_edges(0, *first)
    for at, target in enumerate(corners):
        remote(corner_send, corner_recv.at[at], corner_sems.at[0, at], corner_sems.at[1, at], target)
    for move in y_moves:
        signal(ready.at[0], device(move))

    for z in (0, 1):
        advance(u_ref, u1, 7, z)
    columns = jnp.zeros((128, 128), F32)
    for z in (0, 1):
        upper = 0.15 + 0.15 * w_ref[0, z, 120:128, :]
        lower = 0.15 - 0.15 * w_ref[0, z, 0:8, :]
        face_send_x[0, z : z + 1, :] = (upper * u1[7, z, 120:128, :])[7:8, :]
        face_send_x[0, 2 + z : 3 + z, :] = upper[7:8, :]
        face_send_x[1, z : z + 1, :] = (lower * u1[7, z, 0:8, :])[0:1, :]
        face_send_x[1, 2 + z : 3 + z, :] = lower[0:1, :]
        factor = coef[6, z]
        scaled = factor * u1[7, z]
        columns = jnp.where(lane == z, pltpu.roll(scaled, 1 + z, 1), columns)
        columns = jnp.where(lane == 2 + z, pltpu.roll(factor, 3 + z, 1), columns)
        columns = jnp.where(lane == 4 + z, pltpu.roll(scaled, 4 + z, 1), columns)
        columns = jnp.where(lane == 6 + z, pltpu.roll(factor, 6 + z, 1), columns)
    face_send_y[...] = columns.T[0:8, :]
    send_edges(1, *of_faces)
    for z in (0, 1):
        advance_all(u_ref, u1, 7, z)
    advance(u_ref, u1, 7, 2)
    if y_moves:
        pl.semaphore_wait(ready.at[0], len(y_moves))
    for move in blk_moves:
        signal(ready.at[1], device(move))

    owner = jnp.broadcast_to(owner_ref[...].astype(F32), (128, 256)).T.astype(I32)
    owner_hot = jnp.where(iota((256, 128), 1) == owner, 1.0, 0.0)
    earlier = jnp.where(iota((256, 256), 0) > iota((256, 256), 1), 1.0, 0.0).astype(BF16)
    before = dot(earlier, owner_hot.astype(BF16))
    rank = jnp.sum(before * owner_hot, axis=1, keepdims=True)
    slot = owner.astype(F32) * float(cap) + rank
    slot_row = slot.T[0:1, :]
    sel = jnp.where(iota((slots, 256), 0).astype(F32) == slot_row, 1.0, 0.0).astype(BF16)
    flip = jnp.where(iota((256, 256), 0) == (iota((256, 256), 1) ^ 7), 1.0, 0.0).astype(BF16)
    sel_t[...] = dot(sel, flip).astype(BF16)
    tile_high, tile_low = split(jnp.broadcast_to(tile_ref[...].astype(F32), (128, 256)).T)
    label_ref[...] = dot(sel, tile_high) + dot(sel, tile_low)
    pack(u_ref, far, rest_send_x, rest_send_y)
    send_edges(2, *rest)

    wait_edges(0, first_recv_x, first_recv_y)
    for k, (v, z) in enumerate(near):
        mend(u1, first_recv_x, k, v, z)
    for z in (0, 1):
        advance(u1, out_ref, 7, z)

    for side in range(2):
        take(face_recv_x.at[side], edge_sems.at[1, 1, side])
        take(face_recv_y.at[side], edge_sems.at[1, 1, 2 + side])
    for at in range(4):
        take(corner_recv.at[at], corner_sems.at[1, at])
    own = corner_send[...]
    low_low = jnp.where((a > 0) & (b > 0), corner_recv[0], 0.0)
    low_high = jnp.where((a > 0) & (b < nb - 1), corner_recv[1], 0.0)
    high_low = jnp.where((a < na - 1) & (b > 0), corner_recv[2], 0.0)
    high_high = jnp.where((a < na - 1) & (b < nb - 1), corner_recv[3], 0.0)
    low_low, high_high = pltpu.roll(low_low, 1, 1), pltpu.roll(high_high, 127, 1)
    lane2 = iota((2, 128), 1)

    def beyond(came, rows, first_rows, last_rows):
        brought = rows + jnp.where(lane2 == 0, first_rows, 0.0)
        brought = brought + jnp.where(lane2 == 127, last_rows, 0.0)
        return came[0:2] + came[2:4] * brought

    from_left = beyond(face_recv_y[0, 0:4], own[6:8], low_low[0:2], high_low[2:4])
    from_right = beyond(face_recv_y[1, 4:8], own[4:6], low_high[0:2], high_high[2:4])
    from_left = jnp.where(b > 0, from_left, 0.0)
    from_right = jnp.where(b < nb - 1, from_right, 0.0)
    ring_x[0, 0:2, :] = beyond(face_recv_x[0, 0:4], own[2:4], low_low[4:6], low_high[6:8])
    ring_x[1, 0:2, :] = beyond(face_recv_x[1, 0:4], own[0:2], high_low[4:6], high_high[6:8])
    beside = [from_right[0:1], from_left[0:1], from_right[1:2], from_left[1:2]]
    turned[...] = jnp.concatenate(beside + [jnp.zeros((124, 128), F32)], axis=0).T
    for k, (v, z) in enumerate(faced):
        mend(out_ref, ring_x, k, v, z)
    current = out_ref[7, 1] - out_ref[7, 0]

    halves = [pltpu.roll(current, 64, 1).reshape(16, 8, 128), current.reshape(16, 8, 128)]
    group = iota((16, 8, 128), 2) // 8
    faces = []
    for half in range(2):
        face = jnp.zeros((16, 8, 128), F32)
        for r in range(8):
            spread = jnp.broadcast_to(halves[half][:, r : r + 1, :], (16, 8, 128))
            moved = pltpu.roll(spread, 8 * r + 8, 2, stride=8, stride_axis=1)
            face = jnp.where(group == r, moved, face)
        faces.append(face)
    faces = jnp.stack(faces, axis=1).reshape(256, 128)
    face_high, face_low = split(faces)
    routed = dot(sel_t[...], face_high) + dot(sel_t[...], face_low)
    lane_slot = iota((slots, 128), 1)
    routed = jnp.where(lane_slot < 64, routed, label_ref[...])
    face_send[...] = routed.reshape(count, cap, 128)

    def send_all(src, dst, at):
        for move in moves:
            peer_of_a, peer_of_b = device(move)
            remote(
                src.at[peer_of_a * nb + peer_of_b],
                dst.at[me],
                send_sems.at[at],
                recv_sems.at[at],
                (peer_of_a, peer_of_b),
            )
        dst[me] = src[me]

    pl.semaphore_wait(ready.at[1], len(blk_moves))
    send_all(face_send, face_recv, 0)

    advance_all(u_ref, u1, 7, 2)
    advance_all(u_ref, u1, 8, 3)
    wait_edges(2, rest_recv_x, rest_recv_y)
    for k, (v, z) in enumerate(far):
        mend(u1, rest_recv_x, k, v, z)
    pack(u1, later, last_send_x, last_send_y)
    send_edges(3, *last)

    fetches[2].wait()
    fetches[3].wait()

    def per_row(column):
        return jnp.sum(
            jnp.where(iota((orders, 128), 1) == column, twiddle_ref[...], 0.0),
            axis=1,
            keepdims=True,
        )

    def rows_of(even, odd):
        return jnp.concatenate([even, odd], axis=2).reshape(spec_rows, lon)

    def waves():
        cos_turn, sin_turn = per_row(b), per_row(b + 32)
        cos_wave, sin_wave = wave_ref[0], wave_ref[1]
        cosine = (cos_turn * cos_wave - sin_turn * sin_wave).reshape(nb, 2, 1, PAIRS, lon)
        sine = (sin_turn * cos_wave + cos_turn * sin_wave).reshape(nb, 2, 1, PAIRS, lon)
        return cosine, sine

    cosine, sine = waves()
    base_high, base_low = split(rows_of(cosine, sine) * (1.0 / cols_total))
    base_ref[0] = base_high
    base_ref[1] = base_low

    take(face_recv.at[pl.ds(0, count - 1)], recv_sems.at[0])
    got = face_recv[...].reshape(slots, 128)
    swapped = pltpu.roll(got, 64, 1)
    label = jnp.where(lane_slot < 64, swapped, got).astype(I32)
    face = jnp.where(lane_slot < 64, got, swapped)
    tile_row, tile_col = label >> 5, label & 31
    tile_row_t = tile_row.astype(F32).T.astype(I32)
    scatter = jnp.where(iota((32, slots), 0) == tile_row_t[0:32, :], 1.0, 0.0).astype(BF16)
    scatter = jnp.concatenate([scatter, scatter], axis=1)
    col_masks = [
        jnp.where((lane_slot >> 3) + 16 * half == tile_col, 1.0, 0.0).astype(BF16)
        for half in range(2)
    ]

    def spread_bit(value, width):
        moved = pltpu.roll(value, width, 1)
        bit = (lane_slot & width) == 0
        return [jnp.where(bit, value, moved), jnp.where(bit, moved, value)]

    lines = [face]
    for width in (32, 16, 8):
        lines = [part for line in lines for part in spread_bit(line, width)]
    for r in range(8):
        line_high, line_low = split(lines[r])
        right = jnp.concatenate(
            [
                jnp.concatenate([part * mask for mask in col_masks], axis=1)
                for part in (line_high, line_low)
            ],
            axis=0,
        )
        rows = dot(scatter, right)
        forcing[0, pl.ds(r, 32, stride=8), :] = rows[:, 0:128]
        forcing[1, pl.ds(r, 32, stride=8), :] = rows[:, 128:256]

    force = split(jnp.concatenate([forcing[0], forcing[1]], axis=1))
    spectrum = dot3((base_ref[0], base_ref[1]), force, ((1,), (1,)))
    spec_send[...] = spectrum.reshape(nb, 4 * PAIRS, lat)
    for move in inner_moves:
        peer = peer_b[move[2:]]
        remote(spec_send.at[peer], spec_recv.at[b], send_sems.at[1], recv_sems.at[1], (a, peer))
    spec_recv[b] = spec_send[b]

    fetches[4].wait()
    row_of_lane = a * lat + iota((PAIRS, lat), 1)
    x = -1.0 + (2.0 * row_of_lane.astype(F32) + 1.0) / rows_total
    log_sine = jnp.log(jnp.sqrt(1.0 - x * x))
    turns = steps // 16
    heads = ratios[turns]
    low_start = jnp.exp(heads[:, 1:2] + heads[:, 0:1] * log_sine)
    high_start = jnp.exp(heads[:, 3:4] + heads[:, 2:3] * log_sine)

    def build(turn, carry):
        previous, older = carry
        block = ratios[turn]
        made = []
        for offset in range(16):
            up = block[:, offset : offset + 1]
            down = block[:, 16 + offset : 17 + offset]
            begin_low = block[:, 32 + offset : 33 + offset]
            begin_high = block[:, 48 + offset : 49 + offset]
            present = (
                begin_low * low_start + begin_high * high_start + up * x * previous - down * older
            )
            made.append(present)
            older, previous = previous, present
        where = pl.ds(pl.multiple_of(turn * 128, 128), 128)
        for at, part in enumerate(split3(jnp.concatenate(made, axis=0))):
            leg[at, where, :] = part
        return previous, older

    empty = jnp.zeros((PAIRS, lat), F32)
    lax.fori_loop(0, turns, build, (empty, empty))

    width = steps * PAIRS
    at_step = iota((PAIRS, width), 1) // PAIRS
    at_pair = lax.rem(iota((PAIRS, width), 1), PAIRS)
    order_low = b * PAIRS + at_pair
    is_high = at_step <= order_low
    degree = jnp.where(is_high, orders - 1 - order_low + at_step, at_step - 1).astype(F32)
    scale = (2.0 / rows_total) * GAIN / (degree * (degree + 1.0) + SCREENING)
    scale = jnp.where(at_step <= orders, scale, 0.0)
    mine = at_pair == iota((PAIRS, width), 0)
    mask_ref[0] = jnp.where(mine & jnp.logical_not(is_high), scale, 0.0)
    mask_ref[1] = jnp.where(mine & is_high, scale, 0.0)

    order_col, weight_col = per_row(64), per_row(65)
    cosine, sine = waves()
    weight = weight_col.reshape(nb, 2, 1, PAIRS, 1)
    slope_weight = (weight_col * order_col).reshape(nb, 2, 1, PAIRS, 1)
    value_high, value_low = split(rows_of(cosine * weight, sine * weight))
    values_ref[0, :, 0:lon] = value_high
    values_ref[1, :, 0:lon] = value_low
    slope_high, slope_low = split(rows_of(-sine * slope_weight, cosine * slope_weight))
    values_ref[0, :, lon : 2 * lon] = slope_high
    values_ref[1, :, lon : 2 * lon] = slope_low

    take(spec_recv.at[pl.ds(0, nb - 1)], recv_sems.at[1])
    spec = spec_recv[0]
    for at in range(1, nb):
        spec = spec + spec_recv[at]
    spec_high, spec_low = split(spec)
    both = dot(jnp.concatenate([spec_high, spec_low], axis=0), leg[0], ((1,), (1,)))
    wide_sums = both[0:32] + both[32:64] + dot(spec_high, leg[1], ((1,), (1,)))
    for parity in range(2):
        low_rows = wide_sums[parity * 8 : parity * 8 + 8]
        high_rows = wide_sums[16 + parity * 8 : 24 + parity * 8]
        kept = low_rows * mask_ref[0] + high_rows * mask_ref[1]
        coef_send[parity : parity + 1, :] = jnp.sum(kept, axis=0, keepdims=True)
    for move in blk_moves:
        remote(
            coef_send,
            coef_recv.at[a],
            send_sems.at[2],
            recv_sems.at[2],
            (peer_a[move[:2]], b),
        )
    coef_recv[a] = coef_send[...]
    for z in (0, 1):
        advance_all(u1, out_ref, 7, z)
    take(coef_recv.at[pl.ds(0, na - 1)], recv_sems.at[2])
    solved = coef_recv[0]
    for at in range(1, na):
        solved = solved + coef_recv[at]
    expanded = []
    for kind in range(2):
        for parity in range(2):
            expanded.append(
                jnp.where(
                    mask_ref[kind] != 0.0,
                    jnp.broadcast_to(solved[parity : parity + 1, :], (PAIRS, width)),
                    0.0,
                )
            )
    solved_high, solved_low = split(jnp.concatenate(expanded, axis=0))
    solved_both = jnp.concatenate([solved_high, solved_low], axis=0)
    fine = dot(solved_high, leg[2])
    both = dot(solved_both, leg[0])
    middle = dot(solved_both, leg[1])
    syn_all[b] = both[0:32] + (both[32:64] + (middle[0:32] + (middle[32:64] + fine)))
    for move in inner_moves:
        remote(
            syn_all.at[b],
            syn_all.at[b],
            send_sems.at[3],
            recv_sems.at[3],
            (a, peer_b[move[2:]]),
        )
    for z in (2, 3):
        advance_all(u1, out_ref, 8, z)
    wait_edges(3, last_recv_x, last_recv_y)
    for k, (v, z) in enumerate(later):
        mend(out_ref, last_recv_x, k, v, z)
    take(syn_all.at[pl.ds(0, nb - 1)], recv_sems.at[3])

    syn_high, syn_middle, syn_low = split3(syn_all[...].reshape(spec_rows, lat).T)

    def potential_of(high, middle, low):
        rows = high.shape[0]
        coarse = dot(jnp.concatenate([high, middle, low], axis=0), values_ref[0, :, 0:lon])
        rest_of = dot(jnp.concatenate([high, middle], axis=0), values_ref[1, :, 0:lon])
        return coarse[0:rows] + (
            coarse[rows : 2 * rows] + (rest_of[0:rows] + (coarse[2 * rows :] + rest_of[rows:]))
        )

    def rims_of(part):
        return jnp.concatenate([part[0:16], part[lat - 16 :]], axis=0)

    rims = potential_of(rims_of(syn_high), rims_of(syn_middle), rims_of(syn_low))
    rim_send[0] = rims[0:8]
    rim_send[1] = rims[24:32]
    remote(rim_send.at[1], rim_recv.at[0], rim_sems.at[0, 0], rim_sems.at[1, 0], (up_a, b))
    remote(rim_send.at[0], rim_recv.at[1], rim_sems.at[0, 1], rim_sems.at[1, 1], (down_a, b))
    potential = potential_of(syn_high, syn_middle, syn_low)
    pot_ref[...] = potential
    turned_slopes = dot(
        jnp.concatenate([syn_high, syn_middle], axis=0), values_ref[0, :, lon : 2 * lon]
    )
    azimuthal = turned_slopes[0:lat] + (
        turned_slopes[lat:] + dot(syn_high, values_ref[1, :, lon : 2 * lon])
    )
    fetches[5].wait()
    grid_row = iota((lat, 1), 0)
    global_row = a * lat + grid_row
    x_col = -1.0 + (2.0 * global_row.astype(F32) + 1.0) / rows_total
    sine_col = jnp.sqrt(1.0 - x_col * x_col)
    eastward = azimuthal / sine_col
    inverse = rows_total / 2.0

    def heat_of(first_row, last_row, above, below):
        part = slice(first_row, last_row)
        at_first, at_last = global_row[part] == 0, global_row[part] == rows_total - 1
        here = potential[part]
        slope = (jnp.where(at_last, here, above) - jnp.where(at_first, here, below)) * (
            jnp.where(at_first | at_last, inverse, 0.5 * inverse)
        )
        polar = sine_col[part] * slope
        return ped_ref[part, :] * (polar * polar + eastward[part] * eastward[part])

    above, below = pltpu.roll(potential, lat - 1, 0), pltpu.roll(potential, 1, 0)
    heating = heat_of(0, lat, above, below)
    heat_ref[...] = heating

    grids[0] = potential[:, 0:128]
    grids[1] = potential[:, 128:256]
    grids[2] = heating[:, 0:128]
    grids[3] = heating[:, 128:256]
    pick = iota((slots, 128), 1)
    pick = jnp.where((pick < 96) & ((pick & 31) == tile_row), 1.0, 0.0).astype(BF16)
    bits = [(tile_col & (1 << at)) != 0 for at in range(5)]
    upper = lane_slot >= 64

    def pick_row(r):
        rows = jnp.concatenate([grids[at, pl.ds(r, 32, stride=8), :] for at in range(4)], axis=1)
        high, middle, low = split3(rows)
        parts = jnp.concatenate([high, middle, low, jnp.zeros_like(low)], axis=0)
        picked = dot(pick, parts)
        pot = jnp.where(bits[4], picked[:, 128:256], picked[:, 0:128])
        heat = jnp.where(bits[4], picked[:, 384:512], picked[:, 256:384])
        wide[r] = jnp.where(
            upper,
            jnp.where(bits[3], heat, pltpu.roll(heat, 64, 1)),
            jnp.where(bits[3], pltpu.roll(pot, 64, 1), pot),
        )

    for r in range(1, 7):
        pick_row(r)
    take(rim_recv.at[0], rim_sems.at[1, 0])
    take(rim_recv.at[1], rim_sems.at[1, 1])
    edge8 = iota((8, lon), 0)
    top = heat_of(0, 8, above[0:8], jnp.where(edge8 == 0, rim_recv[0, 7:8, :], below[0:8]))
    bottom = heat_of(
        lat - 8, lat, jnp.where(edge8 == 7, rim_recv[1, 0:1, :], above[lat - 8 :]), below[lat - 8 :]
    )
    for first_row, part in ((0, top), (lat - 8, bottom)):
        heat_ref[first_row : first_row + 8, :] = part
        grids[2, first_row : first_row + 8, :] = part[:, 0:128]
        grids[3, first_row : first_row + 8, :] = part[:, 128:256]
    for r in (0, 7):
        pick_row(r)

    def join(first, second, at):
        width = 8 << at
        return jnp.where(
            (lane_slot & width) == 0,
            jnp.where(bits[at], pltpu.roll(first, 128 - width, 1), first),
            jnp.where(bits[at], second, pltpu.roll(second, width, 1)),
        )

    quads = [join(wide[r], wide[r + 4], 2) for r in range(4)]
    twos = [join(quads[r], quads[r + 2], 1) for r in range(2)]
    reply_send[...] = join(twos[0], twos[1], 0).reshape(count, cap, 128)
    send_all(reply_send, reply_recv, 4)
    chosen = jnp.where(iota((256, slots), 1).astype(F32) == slot[:, 0:1], 1.0, 0.0).astype(BF16)
    take(reply_recv.at[pl.ds(0, count - 1)], recv_sems.at[4])
    back_high, back_low = split(reply_recv[...].reshape(slots, 128))
    blocks_ref[...] = dot(chosen, back_high) + dot(chosen, back_low)

    for at, (sent_x, sent_y, _, _) in enumerate((first, of_faces, rest, last)):
        drain_edges(at, sent_x, sent_y)
    take(face_send.at[pl.ds(0, count - 1)], send_sems.at[0])
    take(spec_send.at[pl.ds(0, nb - 1)], send_sems.at[1])
    take(coef_recv.at[pl.ds(0, na - 1)], send_sems.at[2])
    take(syn_all.at[pl.ds(0, nb - 1)], send_sems.at[3])
    take(reply_send.at[pl.ds(0, count - 1)], send_sems.at[4])
    for at in range(4):
        take(corner_send, corner_sems.at[0, at])
    take(rim_send.at[0], rim_sems.at[0, 1])
    take(rim_send.at[1], rim_sems.at[0, 0])


def write_out(slab, potential, heating, blocks, *refs):
    pieces = [(slab.at[v], refs[0].at[v]) for v in range(8)]
    pieces += [(potential, refs[1]), (heating, refs[2]), (blocks, refs[3])]
    copies = [
        pltpu.make_async_copy(src, dst, refs[4].at[k]) for k, (src, dst) in enumerate(pieces)
    ]
    for copy in copies:
        copy.start()
    for copy in copies:
        copy.wait()


def solution(mesh):
    na, nb = mesh.shape["blk"], mesh.shape["inner"]
    count = na * nb

    def shards(slab, speeds, source_matrix, pedersen, owners, tile_positions):
        lat, lon = pedersen.shape
        blocks = owners.shape[0]
        cap = max(2, 2 * blocks // count)
        slots = count * cap
        orders = PAIRS * 2 * nb
        wave, twiddle, table, steps = spectral_tables(na, nb, lat, lon)
        width = steps * PAIRS
        vmem = pl.BlockSpec(memory_space=pltpu.VMEM)
        hbm = pl.BlockSpec(memory_space=pl.ANY)
        dma = pltpu.SemaphoreType.DMA
        shapes = (slab.shape, (lat, lon), (lat, lon), (blocks, 128))

        def edges(rows_x, rows_y):
            return [
                pltpu.VMEM((2, rows_x, 128), F32),
                pltpu.VMEM((rows_y, 128), F32),
                pltpu.VMEM((2, rows_x, 128), F32),
                pltpu.VMEM((2, rows_y, 128), F32),
            ]

        results = pl.pallas_call(
            functools.partial(kernel, (na, nb, steps)),
            out_shape=tuple(pltpu.VMEM(shape, F32) for shape in shapes),
            in_specs=[
                hbm,
                hbm,
                pl.BlockSpec(memory_space=pltpu.SMEM),
                hbm,
                vmem,
                vmem,
                hbm,
                hbm,
                hbm,
            ],
            out_specs=(vmem,) * 4,
            scratch_shapes=[
                pltpu.VMEM(slab.shape, F32),
                pltpu.VMEM(speeds.shape, F32),
                pltpu.VMEM((lat, lon), F32),
                pltpu.VMEM(wave.shape, F32),
                pltpu.VMEM(twiddle.shape, F32),
                pltpu.VMEM((steps // 16 + 1, PAIRS, 128), F32),
                pltpu.VMEM((7, 4, 128, 128), F32),
                pltpu.VMEM((8, 4, 128, 128), F32),
                *edges(24, 40),
                *edges(16, 32),
                *edges(8, 8),
                pltpu.VMEM((2, 8, 128), F32),
                pltpu.VMEM((8, 128), F32),
                pltpu.VMEM((4, 8, 128), F32),
                *edges(32, 64),
                pltpu.VMEM((128, 128), F32),
                pltpu.VMEM((slots, 256), BF16),
                pltpu.VMEM((slots, 128), F32),
                pltpu.VMEM((count, cap, 128), F32),
                pltpu.VMEM((count, cap, 128), F32),
                pltpu.VMEM((2, lat, 128), F32),
                pltpu.VMEM((2, 2 * orders, lon), BF16),
                pltpu.VMEM((2, 2 * orders, 2 * lon), BF16),
                pltpu.VMEM((nb, 4 * PAIRS, lat), F32),
                pltpu.VMEM((nb, 4 * PAIRS, lat), F32),
                pltpu.VMEM((3, width, lat), BF16),
                pltpu.VMEM((2, PAIRS, width), F32),
                pltpu.VMEM((2, width), F32),
                pltpu.VMEM((na, 2, width), F32),
                pltpu.VMEM((nb, 4 * PAIRS, lat), F32),
                pltpu.VMEM((2, 8, lon), F32),
                pltpu.VMEM((2, 8, lon), F32),
                pltpu.VMEM((4, lat, 128), F32),
                pltpu.VMEM((8, slots, 128), F32),
                pltpu.VMEM((count, cap, 128), F32),
                pltpu.VMEM((count, cap, 128), F32),
                dma((2, 4, 4)),
                dma((5,)),
                dma((5,)),
                dma((2, 2)),
                dma((2, 4)),
                dma((7,)),
                pltpu.SemaphoreType.REGULAR((2,)),
            ],
            compiler_params=pltpu.CompilerParams(
                collective_id=0, has_side_effects=True, vmem_limit_bytes=VMEM_LIMIT
            ),
        )(
            slab,
            speeds,
            source_matrix,
            pedersen,
            owners.reshape(1, blocks),
            tile_positions.reshape(1, blocks),
            jnp.asarray(wave),
            jnp.asarray(twiddle),
            jnp.asarray(table),
        )
        return pl.pallas_call(
            write_out,
            out_shape=tuple(jax.ShapeDtypeStruct(shape, F32) for shape in shapes),
            in_specs=[vmem] * 4,
            out_specs=(hbm,) * 4,
            scratch_shapes=[dma((11,))],
            compiler_params=pltpu.CompilerParams(vmem_limit_bytes=16 * 1024 * 1024),
        )(*results)

    in_specs = (
        P(None, None, "blk", "inner"),
        P(None, None, "blk", "inner"),
        P(),
        P("blk", "inner"),
        P(("blk", "inner"), None),
        P(("blk", "inner")),
    )
    out_specs = (
        P(None, None, "blk", "inner"),
        P("blk", "inner"),
        P("blk", "inner"),
        P(("blk", "inner"), None),
    )
    return jax.shard_map(shards, mesh=mesh, in_specs=in_specs, out_specs=out_specs, check_vma=False)
```

```python
import functools
import math

import jax
import jax.numpy as jnp
import numpy as np
from jax import lax
from jax.experimental import pallas as pl
from jax.experimental.pallas import tpu as pltpu
from jax.sharding import PartitionSpec as P

F32 = jnp.float32
BF16 = jnp.bfloat16
I32 = jnp.int32
MESH = pl.DeviceIdType.MESH
BLOCK = 8
PAIRS = 8
SCREENING = 2.0
GAIN = 4096.0
VMEM_LIMIT = 60 * 1024 * 1024


def iota(shape, dim):
    return lax.broadcasted_iota(I32, shape, dim)


def split(value):
    high = value.astype(BF16)
    return high, (value - high.astype(F32)).astype(BF16)


def split3(value):
    high = value.astype(BF16)
    rest = value - high.astype(F32)
    middle = rest.astype(BF16)
    return high, middle, (rest - middle.astype(F32)).astype(BF16)


def dot(left, right, dims=((1,), (0,))):
    return lax.dot_general(left, right, (dims, ((), ())), preferred_element_type=F32)


def dot3(left, right, dims):
    lh, ll = left
    rh, rl = right
    return dot(lh, rh, dims) + dot(ll, rh, dims) + dot(lh, rl, dims)


def spectral_tables(blk_count, inner_count, lat_dev, lon_dev):
    orders = PAIRS * 2 * inner_count
    degrees = orders
    lon_total = lon_dev * inner_count
    first = np.arange(inner_count * PAIRS).reshape(inner_count, 1, PAIRS)
    order_of = np.concatenate([first, orders - 1 - first], axis=1).reshape(-1)
    cols = np.arange(lon_dev)
    phase = (order_of[:, None] * cols[None, :] % lon_total) * (2.0 * math.pi / lon_total)
    wave = np.stack([np.cos(phase), np.sin(phase)]).astype(np.float32)
    turn = (order_of[:, None] * (np.arange(inner_count) * lon_dev)[None, :] % lon_total) * (
        2.0 * math.pi / lon_total
    )
    twiddle = np.zeros((order_of.shape[0], 128), np.float32)
    twiddle[:, :inner_count] = np.cos(turn)
    twiddle[:, 32 : 32 + inner_count] = np.sin(turn)
    twiddle[:, 64] = order_of
    twiddle[:, 65] = np.where(order_of == 0, 1.0, 2.0)

    turns = -(-(degrees + 1) // 16)
    steps = turns * 16
    table = np.zeros((inner_count, turns + 1, PAIRS, 128), np.float32)

    def up(degree, order):
        return np.sqrt(
            np.float32(4.0 * degree * degree - 1.0) / np.float32(degree * degree - order * order)
        )

    counter = np.arange(1, orders, dtype=np.float64)
    log_start = 0.5 * np.log(0.5) + np.concatenate(
        [np.zeros(1), np.cumsum(0.5 * np.log((2.0 * counter + 1.0) / (2.0 * counter)))]
    )
    for pair in range(inner_count * PAIRS):
        place, lane = divmod(pair, PAIRS)
        low, partner = pair, orders - 1 - pair
        table[place, turns, lane, :4] = [low, log_start[low], partner, log_start[partner]]
        for step in range(degrees + 1):
            if step <= low:
                order, degree, kind = partner, partner + step, 3
            else:
                order, degree, kind = low, step - 1, 2
            turn_at, offset = divmod(step, 16)
            if degree == order:
                table[place, turn_at, lane, kind * 16 + offset] = 1.0
                continue
            ratio = up(degree, order)
            table[place, turn_at, lane, offset] = ratio
            if degree >= order + 2:
                table[place, turn_at, lane, 16 + offset] = ratio / up(degree - 1, order)
    return wave, twiddle, table, steps


def kernel(
    sizes,
    u_hbm,
    w_hbm,
    mix_ref,
    ped_hbm,
    owner_ref,
    tile_ref,
    wave_hbm,
    twiddle_hbm,
    table_hbm,
    out_ref,
    pot_ref,
    heat_ref,
    blocks_ref,
    u_ref,
    w_ref,
    ped_ref,
    wave_ref,
    twiddle_ref,
    ratios,
    coef,
    u1,
    q_ref,
    source_ref,
    first_send_x,
    first_send_y,
    first_recv_x,
    first_recv_y,
    rest_send_x,
    rest_send_y,
    rest_recv_x,
    rest_recv_y,
    face_send_x,
    face_send_y,
    face_recv_x,
    face_recv_y,
    ring_x,
    corner_send,
    corner_recv,
    last_send_x,
    last_send_y,
    last_recv_x,
    last_recv_y,
    turned,
    sel_t,
    label_ref,
    face_send,
    face_recv,
    forcing,
    base_ref,
    values_ref,
    spec_send,
    spec_recv,
    leg,
    mask_ref,
    coef_send,
    coef_recv,
    syn_all,
    rim_send,
    rim_recv,
    grids,
    wide,
    reply_send,
    reply_recv,
    edge_sems,
    send_sems,
    recv_sems,
    rim_sems,
    corner_sems,
    in_sems,
    ready,
):
    na, nb, steps = sizes
    count = na * nb
    lat, lon = ped_ref.shape
    rows_total, cols_total = lat * na, lon * nb
    cap = face_send.shape[1]
    slots = count * cap
    a, b = lax.axis_index("blk"), lax.axis_index("inner")
    me = a * nb + b
    orders = PAIRS * 2 * nb
    spec_rows = 2 * orders

    nx, nz = na // 2, min(4, nb)
    ny = nb // nz
    chip_x, core, chip_y, chip_z = a // 2, lax.rem(a, 2), b // nz, lax.rem(b, nz)
    peer_a = {
        (dx, dc): lax.rem(chip_x + dx, nx) * 2 + lax.rem(core + dc, 2)
        for dx in range(nx)
        for dc in range(2)
    }
    peer_b = {
        (dy, dz): lax.rem(chip_y + dy, ny) * nz + lax.rem(chip_z + dz, nz)
        for dy in range(ny)
        for dz in range(nz)
    }

    def hops(move):
        dx, dc, dy, dz = move
        return 2 * (min(dx, nx - dx) + min(dy, ny - dy) + min(dz, nz - dz)) + dc

    moves = sorted(
        [(dx, dc, dy, dz) for dx, dc in peer_a for dy, dz in peer_b if (dx, dc, dy, dz) != (0, 0, 0, 0)],
        key=hops,
        reverse=True,
    )
    blk_moves = [move for move in moves if move[2:] == (0, 0)]
    inner_moves = [move for move in moves if move[:2] == (0, 0)]

    def device(move):
        return peer_a[move[:2]], peer_b[move[2:]]

    def remote(src, dst, send_sem, recv_sem, target):
        pltpu.make_async_remote_copy(
            src_ref=src,
            dst_ref=dst,
            send_sem=send_sem,
            recv_sem=recv_sem,
            device_id=target,
            device_id_type=MESH,
        ).start()

    def take(ref, sem):
        pltpu.make_async_copy(ref, ref, sem).wait()

    def signal(sem, target):
        pl.semaphore_signal(sem, inc=1, device_id=target, device_id_type=MESH)

    up_a, down_a = lax.rem(a + 1, na), lax.rem(a + na - 1, na)
    up_b, down_b = lax.rem(b + 1, nb), lax.rem(b + nb - 1, nb)

    fetches = [
        pltpu.make_async_copy(src, dst, in_sems.at[at])
        for at, (src, dst) in enumerate(
            [
                (w_hbm, w_ref),
                (u_hbm.at[7], u_ref.at[7]),
                (u_hbm.at[pl.ds(0, 7), pl.ds(0, 3)], u_ref.at[pl.ds(0, 7), pl.ds(0, 3)]),
                (u_hbm.at[pl.ds(0, 7), pl.ds(3, 1)], u_ref.at[pl.ds(0, 7), pl.ds(3, 1)]),
                (twiddle_hbm, twiddle_ref),
                (wave_hbm, wave_ref),
                (table_hbm.at[b], ratios),
                (ped_hbm, ped_ref),
            ]
        )
    ]
    for fetch in fetches:
        fetch.start()
    barrier = pltpu.get_barrier_semaphore()
    y_moves = [move for move in inner_moves if move[3] == 0]
    z_moves = [move for move in inner_moves if move[2] == 0]
    greeted = [device(move) for move in blk_moves + y_moves + z_moves]
    greeted += [(a, up_b), (a, down_b)]
    corners = [(up_a, up_b), (up_a, down_b), (down_a, up_b), (down_a, down_b)]
    greeted += corners
    for target in greeted:
        signal(barrier, target)

    row = iota((128, 128), 0)
    lane = iota((128, 128), 1)
    row8 = iota((8, 128), 0)
    fetches[0].wait()

    def make_coef(z, carry):
        wx, wy = 0.15 * w_ref[0, z], 0.15 * w_ref[1, z]
        coef[0, z] = jnp.where(row == 127, 0.0, 0.15 + wx)
        coef[1, z] = jnp.where(row == 0, 0.0, 0.15 - wx)
        coef[2, z] = jnp.where(lane == 127, 0.0, 0.15 + wy)
        coef[3, z] = jnp.where(lane == 0, 0.0, 0.15 - wy)
        below = 0.15 + 0.15 * w_ref[2, jnp.maximum(z - 1, 0)]
        above = 0.15 - 0.15 * w_ref[2, jnp.minimum(z + 1, 3)]
        coef[4, z] = jnp.where(z > 0, below, 0.0)
        coef[5, z] = jnp.where(z < 3, above, 0.0)
        coef[6, z] = jnp.where(lane == 0, 0.15 - wy, 0.15 + wy)
        return carry

    lax.fori_loop(0, 4, make_coef, 0)

    def weighted(weights, z):
        total = weights[0] * u_ref[0, z]
        for w in range(1, 8):
            total = total + weights[w] * u_ref[w, z]
        return total

    source = [mix_ref[7, w] for w in range(8)]
    second = []
    for w in range(8):
        total = source[0] * mix_ref[0, w]
        for k in range(1, 8):
            total = total + source[k] * mix_ref[k, w]
        second.append(total)
    fetches[1].wait()
    fetches[2].wait()
    for z in range(3):
        q_ref[z] = weighted(source, z)

    def pack(src, items, send_x, send_y):
        packed = jnp.zeros((128, 128), F32)
        for k, (v, z) in enumerate(items):
            cells = q_ref.at[z] if v == 8 else src.at[v, z]
            last = (0.15 + 0.15 * w_ref[0, z, 120:128, :]) * cells[120:128, :]
            first = (0.15 - 0.15 * w_ref[0, z, 0:8, :]) * cells[0:8, :]
            send_x[0, k : k + 1, :] = last[7:8, :]
            send_x[1, k : k + 1, :] = first[0:1, :]
            rolled = pltpu.roll(coef[6, z] * cells[...], 2 * k + 1, 1)
            packed = jnp.where((lane == 2 * k) | (lane == 2 * k + 1), rolled, packed)
        send_y[...] = packed.T[0 : send_y.shape[0], :]

    def send_edges(at, send_x, send_y, recv_x, recv_y):
        for side, target in ((0, (up_a, b)), (1, (down_a, b))):
            remote(
                send_x.at[side],
                recv_x.at[side],
                edge_sems.at[0, at, side],
                edge_sems.at[1, at, side],
                target,
            )
        for side, target in ((0, (a, up_b)), (1, (a, down_b))):
            remote(
                send_y,
                recv_y.at[side],
                edge_sems.at[0, at, 2 + side],
                edge_sems.at[1, at, 2 + side],
                target,
            )

    def wait_edges(at, recv_x, recv_y):
        for side in range(2):
            take(recv_x.at[side], edge_sems.at[1, at, side])
            take(recv_y.at[side], edge_sems.at[1, at, 2 + side])
        rows = recv_y.shape[1]
        odd = (iota((rows, 128), 0) & 1) == 1
        up = jnp.where(b > 0, recv_y[0], 0.0)
        down = jnp.where(b < nb - 1, recv_y[1], 0.0)
        mixed = jnp.where(odd, pltpu.roll(up, 1, 0), pltpu.roll(down, rows - 1, 0))
        if rows < 128:
            mixed = jnp.concatenate([mixed, jnp.zeros((128 - rows, 128), F32)], axis=0)
        turned[...] = mixed.T

    def drain_edges(at, send_x, send_y):
        for side in range(2):
            take(send_x.at[side], edge_sems.at[0, at, side])
            take(send_y, edge_sems.at[0, at, 2 + side])

    def mend(cells, recv_x, k):
        rolled = pltpu.roll(turned[...], 127 - 2 * k, 1)
        whole = cells[...] + jnp.where((lane == 0) | (lane == 127), rolled, 0.0)
        from_down = jnp.where(a > 0, recv_x[0, k : k + 1, :], 0.0)
        from_up = jnp.where(a < na - 1, recv_x[1, k : k + 1, :], 0.0)
        cells[8:120, :] = whole[8:120]
        cells[0:8, :] = whole[0:8] + jnp.where(row8 == 0, from_down, 0.0)
        cells[120:128, :] = whole[120:128] + jnp.where(row8 == 7, from_up, 0.0)

    def transport(field, z):
        u = field(z)
        total = pltpu.roll(coef[0, z] * u, 1, 0) + pltpu.roll(coef[1, z] * u, 127, 0)
        total = total + pltpu.roll(coef[2, z] * u, 1, 1) + pltpu.roll(coef[3, z] * u, 127, 1)
        if z > 0:
            total = total + coef[4, z] * field(z - 1)
        if z < 3:
            total = total + coef[5, z] * field(z + 1)
        return total + 0.1 * u

    def advance(src, dst, v, z):
        u = src[v, z]
        total = mix_ref[v, 0] * src[0, z]
        for w in range(1, 8):
            total = total + mix_ref[v, w] * src[w, z]
        total = 0.3 * total + 0.1 * u
        total = total + pltpu.roll(coef[0, z] * u, 1, 0) + pltpu.roll(coef[1, z] * u, 127, 0)
        total = total + pltpu.roll(coef[2, z] * u, 1, 1) + pltpu.roll(coef[3, z] * u, 127, 1)
        if not (isinstance(z, int) and z == 0):
            total = total + coef[4, z] * src[v, z - 1 if isinstance(z, int) else jnp.maximum(z - 1, 0)]
        if not (isinstance(z, int) and z == 3):
            total = total + coef[5, z] * src[v, z + 1 if isinstance(z, int) else jnp.minimum(z + 1, 3)]
        dst[v, z] = total

    def advance_all(src, dst, vs, z):
        def one(v, carry):
            advance(src, dst, v, z)
            return carry

        lax.fori_loop(0, vs, one, 0)

    near = [(7, 0), (7, 1), (7, 2), (8, 0), (8, 1)]
    far = [(v, z) for z in range(4) for v in range(7)] + [(7, 3)]
    faced = [(7, 0), (7, 1)]
    later = [(v, z) for z in range(4) for v in range(8) if (v, z) not in faced]
    first = (first_send_x, first_send_y, first_recv_x, first_recv_y)
    rest = (rest_send_x, rest_send_y, rest_recv_x, rest_recv_y)
    of_faces = (face_send_x, face_send_y, face_recv_x, face_recv_y)
    last = (last_send_x, last_send_y, last_recv_x, last_recv_y)

    pack(u_ref, near, first_send_x, first_send_y)
    at_0, at_1 = near.index((7, 0)), near.index((7, 1))
    for side in range(2):
        for z, k in enumerate((at_0, at_1)):
            corner_send[2 * side + z : 2 * side + z + 1, :] = first_send_x[side, k : k + 1, :]
            corner_send[4 + 2 * side + z : 5 + 2 * side + z, :] = first_send_y[
                2 * k + side : 2 * k + side + 1, :
            ]
    pl.semaphore_wait(barrier, len(greeted))
    send_edges(0, *first)
    for at, target in enumerate(corners):
        remote(corner_send, corner_recv.at[at], corner_sems.at[0, at], corner_sems.at[1, at], target)
    for move in y_moves:
        signal(ready.at[0], device(move))

    for z in (0, 1):
        u1[7, z] = transport(lambda at: u_ref[7, at], z) + 0.3 * q_ref[z]
    columns = jnp.zeros((128, 128), F32)
    for z in (0, 1):
        upper = 0.15 + 0.15 * w_ref[0, z, 120:128, :]
        lower = 0.15 - 0.15 * w_ref[0, z, 0:8, :]
        face_send_x[0, z : z + 1, :] = (upper * u1[7, z, 120:128, :])[7:8, :]
        face_send_x[0, 2 + z : 3 + z, :] = upper[7:8, :]
        face_send_x[1, z : z + 1, :] = (lower * u1[7, z, 0:8, :])[0:1, :]
        face_send_x[1, 2 + z : 3 + z, :] = lower[0:1, :]
        factor = coef[6, z]
        scaled = factor * u1[7, z]
        columns = jnp.where(lane == z, pltpu.roll(scaled, 1 + z, 1), columns)
        columns = jnp.where(lane == 2 + z, pltpu.roll(factor, 3 + z, 1), columns)
        columns = jnp.where(lane == 4 + z, pltpu.roll(scaled, 4 + z, 1), columns)
        columns = jnp.where(lane == 6 + z, pltpu.roll(factor, 6 + z, 1), columns)
    face_send_y[...] = columns.T[0:8, :]
    send_edges(1, *of_faces)
    u1[7, 2] = transport(lambda at: u_ref[7, at], 2) + 0.3 * q_ref[2]
    for z in (0, 1):
        source_ref[z] = transport(lambda at: q_ref[at], z) + 0.3 * weighted(second, z)
    if y_moves:
        pl.semaphore_wait(ready.at[0], len(y_moves))
    for move in blk_moves:
        signal(ready.at[1], device(move))

    owner = jnp.broadcast_to(owner_ref[...].astype(F32), (128, 256)).T.astype(I32)
    owner_hot = jnp.where(iota((256, 128), 1) == owner, 1.0, 0.0)
    earlier = jnp.where(iota((256, 256), 0) > iota((256, 256), 1), 1.0, 0.0).astype(BF16)
    before = dot(earlier, owner_hot.astype(BF16))
    rank = jnp.sum(before * owner_hot, axis=1, keepdims=True)
    slot = owner.astype(F32) * float(cap) + rank
    slot_row = slot.T[0:1, :]
    sel = jnp.where(iota((slots, 256), 0).astype(F32) == slot_row, 1.0, 0.0).astype(BF16)
    flip = jnp.where(iota((256, 256), 0) == (iota((256, 256), 1) ^ 7), 1.0, 0.0).astype(BF16)
    sel_t[...] = dot(sel, flip).astype(BF16)
    tile_high, tile_low = split(jnp.broadcast_to(tile_ref[...].astype(F32), (128, 256)).T)
    label_ref[...] = dot(sel, tile_high) + dot(sel, tile_low)

    wait_edges(0, first_recv_x, first_recv_y)
    for k, (v, z) in enumerate(near):
        mend(source_ref.at[z] if v == 8 else u1.at[v, z], first_recv_x, k)
    for z in (0, 1):
        out_ref[7, z] = transport(lambda at: u1[7, at], z) + 0.3 * source_ref[z]

    for side in range(2):
        take(face_recv_x.at[side], edge_sems.at[1, 1, side])
        take(face_recv_y.at[side], edge_sems.at[1, 1, 2 + side])
    for at in range(4):
        take(corner_recv.at[at], corner_sems.at[1, at])
    own = corner_send[...]
    low_low = jnp.where((a > 0) & (b > 0), corner_recv[0], 0.0)
    low_high = jnp.where((a > 0) & (b < nb - 1), corner_recv[1], 0.0)
    high_low = jnp.where((a < na - 1) & (b > 0), corner_recv[2], 0.0)
    high_high = jnp.where((a < na - 1) & (b < nb - 1), corner_recv[3], 0.0)
    low_low, high_high = pltpu.roll(low_low, 1, 1), pltpu.roll(high_high, 127, 1)
    lane2 = iota((2, 128), 1)

    def beyond(came, rows, first_rows, last_rows):
        brought = rows + jnp.where(lane2 == 0, first_rows, 0.0)
        brought = brought + jnp.where(lane2 == 127, last_rows, 0.0)
        return came[0:2] + came[2:4] * brought

    from_left = beyond(face_recv_y[0, 0:4], own[6:8], low_low[0:2], high_low[2:4])
    from_right = beyond(face_recv_y[1, 4:8], own[4:6], low_high[0:2], high_high[2:4])
    from_left = jnp.where(b > 0, from_left, 0.0)
    from_right = jnp.where(b < nb - 1, from_right, 0.0)
    ring_x[0, 0:2, :] = beyond(face_recv_x[0, 0:4], own[2:4], low_low[4:6], low_high[6:8])
    ring_x[1, 0:2, :] = beyond(face_recv_x[1, 0:4], own[0:2], high_low[4:6], high_high[6:8])
    beside = [from_right[0:1], from_left[0:1], from_right[1:2], from_left[1:2]]
    turned[...] = jnp.concatenate(beside + [jnp.zeros((124, 128), F32)], axis=0).T
    for k, (v, z) in enumerate(faced):
        mend(out_ref.at[v, z], ring_x, k)
    current = out_ref[7, 1] - out_ref[7, 0]

    halves = [pltpu.roll(current, 64, 1).reshape(16, 8, 128), current.reshape(16, 8, 128)]
    group = iota((16, 8, 128), 2) // 8
    faces = []
    for half in range(2):
        face = jnp.zeros((16, 8, 128), F32)
        for r in range(8):
            spread = jnp.broadcast_to(halves[half][:, r : r + 1, :], (16, 8, 128))
            moved = pltpu.roll(spread, 8 * r + 8, 2, stride=8, stride_axis=1)
            face = jnp.where(group == r, moved, face)
        faces.append(face)
    faces = jnp.stack(faces, axis=1).reshape(256, 128)
    face_high, face_low = split(faces)
    routed = dot(sel_t[...], face_high) + dot(sel_t[...], face_low)
    lane_slot = iota((slots, 128), 1)
    routed = jnp.where(lane_slot < 64, routed, label_ref[...])
    face_send[...] = routed.reshape(count, cap, 128)

    def send_all(src, dst, at):
        for move in moves:
            peer_of_a, peer_of_b = device(move)
            remote(
                src.at[peer_of_a * nb + peer_of_b],
                dst.at[me],
                send_sems.at[at],
                recv_sems.at[at],
                (peer_of_a, peer_of_b),
            )
        dst[me] = src[me]

    pl.semaphore_wait(ready.at[1], len(blk_moves))
    send_all(face_send, face_recv, 0)

    fetches[3].wait()
    pack(u_ref, far, rest_send_x, rest_send_y)
    send_edges(2, *rest)

    fetches[4].wait()
    fetches[5].wait()

    def per_row(column):
        return jnp.sum(
            jnp.where(iota((orders, 128), 1) == column, twiddle_ref[...], 0.0),
            axis=1,
            keepdims=True,
        )

    def rows_of(even, odd):
        return jnp.concatenate([even, odd], axis=2).reshape(spec_rows, lon)

    def waves():
        cos_turn, sin_turn = per_row(b), per_row(b + 32)
        cos_wave, sin_wave = wave_ref[0], wave_ref[1]
        cosine = (cos_turn * cos_wave - sin_turn * sin_wave).reshape(nb, 2, 1, PAIRS, lon)
        sine = (sin_turn * cos_wave + cos_turn * sin_wave).reshape(nb, 2, 1, PAIRS, lon)
        return cosine, sine

    cosine, sine = waves()
    base_high, base_low = split(rows_of(cosine, sine) * (1.0 / cols_total))
    base_ref[0] = base_high
    base_ref[1] = base_low

    for z in range(3):
        advance_all(u_ref, u1, 7, z)

    take(face_recv.at[pl.ds(0, count - 1)], recv_sems.at[0])
    got = face_recv[...].reshape(slots, 128)
    swapped = pltpu.roll(got, 64, 1)
    label = jnp.where(lane_slot < 64, swapped, got).astype(I32)
    face = jnp.where(lane_slot < 64, got, swapped)
    tile_row, tile_col = label >> 5, label & 31
    tile_row_t = tile_row.astype(F32).T.astype(I32)
    scatter = jnp.where(iota((32, slots), 0) == tile_row_t[0:32, :], 1.0, 0.0).astype(BF16)
    scatter = jnp.concatenate([scatter, scatter], axis=1)
    col_masks = [
        jnp.where((lane_slot >> 3) + 16 * half == tile_col, 1.0, 0.0).astype(BF16)
        for half in range(2)
    ]

    def spread_bit(value, width):
        moved = pltpu.roll(value, width, 1)
        bit = (lane_slot & width) == 0
        return [jnp.where(bit, value, moved), jnp.where(bit, moved, value)]

    lines = [face]
    for width in (32, 16, 8):
        lines = [part for line in lines for part in spread_bit(line, width)]
    for r in range(8):
        line_high, line_low = split(lines[r])
        right = jnp.concatenate(
            [
                jnp.concatenate([part * mask for mask in col_masks], axis=1)
                for part in (line_high, line_low)
            ],
            axis=0,
        )
        rows = dot(scatter, right)
        forcing[0, pl.ds(r, 32, stride=8), :] = rows[:, 0:128]
        forcing[1, pl.ds(r, 32, stride=8), :] = rows[:, 128:256]

    force = split(jnp.concatenate([forcing[0], forcing[1]], axis=1))
    spectrum = dot3((base_ref[0], base_ref[1]), force, ((1,), (1,)))
    spec_send[...] = spectrum.reshape(nb, 4 * PAIRS, lat)
    for move in inner_moves:
        peer = peer_b[move[2:]]
        remote(spec_send.at[peer], spec_recv.at[b], send_sems.at[1], recv_sems.at[1], (a, peer))
    spec_recv[b] = spec_send[b]

    fetches[6].wait()
    row_of_lane = a * lat + iota((PAIRS, lat), 1)
    x = -1.0 + (2.0 * row_of_lane.astype(F32) + 1.0) / rows_total
    log_sine = jnp.log(jnp.sqrt(1.0 - x * x))
    turns = steps // 16
    heads = ratios[turns]
    low_start = jnp.exp(heads[:, 1:2] + heads[:, 0:1] * log_sine)
    high_start = jnp.exp(heads[:, 3:4] + heads[:, 2:3] * log_sine)

    def build(turn, carry):
        previous, older = carry
        block = ratios[turn]
        made = []
        for offset in range(16):
            up = block[:, offset : offset + 1]
            down = block[:, 16 + offset : 17 + offset]
            begin_low = block[:, 32 + offset : 33 + offset]
            begin_high = block[:, 48 + offset : 49 + offset]
            present = (
                begin_low * low_start + begin_high * high_start + up * x * previous - down * older
            )
            made.append(present)
            older, previous = previous, present
        where = pl.ds(pl.multiple_of(turn * 128, 128), 128)
        for at, part in enumerate(split3(jnp.concatenate(made, axis=0))):
            leg[at, where, :] = part
        return previous, older

    empty = jnp.zeros((PAIRS, lat), F32)
    lax.fori_loop(0, turns, build, (empty, empty))

    width = steps * PAIRS
    at_step = iota((PAIRS, width), 1) // PAIRS
    at_pair = lax.rem(iota((PAIRS, width), 1), PAIRS)
    order_low = b * PAIRS + at_pair
    is_high = at_step <= order_low
    degree = jnp.where(is_high, orders - 1 - order_low + at_step, at_step - 1).astype(F32)
    scale = (2.0 / rows_total) * GAIN / (degree * (degree + 1.0) + SCREENING)
    scale = jnp.where(at_step <= orders, scale, 0.0)
    mine = at_pair == iota((PAIRS, width), 0)
    mask_ref[0] = jnp.where(mine & jnp.logical_not(is_high), scale, 0.0)
    mask_ref[1] = jnp.where(mine & is_high, scale, 0.0)

    advance_all(u_ref, u1, 8, 3)
    wait_edges(2, rest_recv_x, rest_recv_y)
    for k, (v, z) in enumerate(far):
        mend(u1.at[v, z], rest_recv_x, k)
    pack(u1, later, last_send_x, last_send_y)
    send_edges(3, *last)

    take(spec_recv.at[pl.ds(0, nb - 1)], recv_sems.at[1])
    spec = spec_recv[0]
    for at in range(1, nb):
        spec = spec + spec_recv[at]
    spec_high, spec_low = split(spec)
    both = dot(jnp.concatenate([spec_high, spec_low], axis=0), leg[0], ((1,), (1,)))
    wide_sums = both[0:32] + both[32:64] + dot(spec_high, leg[1], ((1,), (1,)))
    for parity in range(2):
        low_rows = wide_sums[parity * 8 : parity * 8 + 8]
        high_rows = wide_sums[16 + parity * 8 : 24 + parity * 8]
        kept = low_rows * mask_ref[0] + high_rows * mask_ref[1]
        coef_send[parity : parity + 1, :] = jnp.sum(kept, axis=0, keepdims=True)
    for move in blk_moves:
        remote(
            coef_send,
            coef_recv.at[a],
            send_sems.at[2],
            recv_sems.at[2],
            (peer_a[move[:2]], b),
        )
    coef_recv[a] = coef_send[...]
    for z in (0, 1):
        advance_all(u1, out_ref, 7, z)
    take(coef_recv.at[pl.ds(0, na - 1)], recv_sems.at[2])
    solved = coef_recv[0]
    for at in range(1, na):
        solved = solved + coef_recv[at]
    expanded = []
    for kind in range(2):
        for parity in range(2):
            expanded.append(
                jnp.where(
                    mask_ref[kind] != 0.0,
                    jnp.broadcast_to(solved[parity : parity + 1, :], (PAIRS, width)),
                    0.0,
                )
            )
    solved_high, solved_low = split(jnp.concatenate(expanded, axis=0))
    solved_both = jnp.concatenate([solved_high, solved_low], axis=0)
    fine = dot(solved_high, leg[2])
    both = dot(solved_both, leg[0])
    middle = dot(solved_both, leg[1])
    syn_all[b] = both[0:32] + (both[32:64] + (middle[0:32] + (middle[32:64] + fine)))
    for move in inner_moves:
        remote(
            syn_all.at[b],
            syn_all.at[b],
            send_sems.at[3],
            recv_sems.at[3],
            (a, peer_b[move[2:]]),
        )
    order_col, weight_col = per_row(64), per_row(65)
    cosine, sine = waves()
    weight = weight_col.reshape(nb, 2, 1, PAIRS, 1)
    slope_weight = (weight_col * order_col).reshape(nb, 2, 1, PAIRS, 1)
    value_high, value_low = split(rows_of(cosine * weight, sine * weight))
    values_ref[0, :, 0:lon] = value_high
    values_ref[1, :, 0:lon] = value_low
    slope_high, slope_low = split(rows_of(-sine * slope_weight, cosine * slope_weight))
    values_ref[0, :, lon : 2 * lon] = slope_high
    values_ref[1, :, lon : 2 * lon] = slope_low

    for z in (2, 3):
        advance_all(u1, out_ref, 8, z)
    wait_edges(3, last_recv_x, last_recv_y)
    for k, (v, z) in enumerate(later):
        mend(out_ref.at[v, z], last_recv_x, k)
    take(syn_all.at[pl.ds(0, nb - 1)], recv_sems.at[3])

    syn_high, syn_middle, syn_low = split3(syn_all[...].reshape(spec_rows, lat).T)

    def potential_of(high, middle, low):
        rows = high.shape[0]
        coarse = dot(jnp.concatenate([high, middle, low], axis=0), values_ref[0, :, 0:lon])
        rest_of = dot(jnp.concatenate([high, middle], axis=0), values_ref[1, :, 0:lon])
        return coarse[0:rows] + (
            coarse[rows : 2 * rows] + (rest_of[0:rows] + (coarse[2 * rows :] + rest_of[rows:]))
        )

    def rims_of(part):
        return jnp.concatenate([part[0:16], part[lat - 16 :]], axis=0)

    rims = potential_of(rims_of(syn_high), rims_of(syn_middle), rims_of(syn_low))
    rim_send[0] = rims[0:8]
    rim_send[1] = rims[24:32]
    remote(rim_send.at[1], rim_recv.at[0], rim_sems.at[0, 0], rim_sems.at[1, 0], (up_a, b))
    remote(rim_send.at[0], rim_recv.at[1], rim_sems.at[0, 1], rim_sems.at[1, 1], (down_a, b))
    potential = potential_of(syn_high, syn_middle, syn_low)
    pot_ref[...] = potential
    turned_slopes = dot(
        jnp.concatenate([syn_high, syn_middle], axis=0), values_ref[0, :, lon : 2 * lon]
    )
    azimuthal = turned_slopes[0:lat] + (
        turned_slopes[lat:] + dot(syn_high, values_ref[1, :, lon : 2 * lon])
    )
    fetches[7].wait()
    grid_row = iota((lat, 1), 0)
    global_row = a * lat + grid_row
    x_col = -1.0 + (2.0 * global_row.astype(F32) + 1.0) / rows_total
    sine_col = jnp.sqrt(1.0 - x_col * x_col)
    eastward = azimuthal / sine_col
    inverse = rows_total / 2.0

    def heat_of(first_row, last_row, above, below):
        part = slice(first_row, last_row)
        at_first, at_last = global_row[part] == 0, global_row[part] == rows_total - 1
        here = potential[part]
        slope = (jnp.where(at_last, here, above) - jnp.where(at_first, here, below)) * (
            jnp.where(at_first | at_last, inverse, 0.5 * inverse)
        )
        polar = sine_col[part] * slope
        return ped_ref[part, :] * (polar * polar + eastward[part] * eastward[part])

    above, below = pltpu.roll(potential, lat - 1, 0), pltpu.roll(potential, 1, 0)
    heating = heat_of(0, lat, above, below)
    heat_ref[...] = heating

    grids[0] = potential[:, 0:128]
    grids[1] = potential[:, 128:256]
    grids[2] = heating[:, 0:128]
    grids[3] = heating[:, 128:256]
    pick = iota((slots, 128), 1)
    pick = jnp.where((pick < 96) & ((pick & 31) == tile_row), 1.0, 0.0).astype(BF16)
    bits = [(tile_col & (1 << at)) != 0 for at in range(5)]
    upper = lane_slot >= 64

    def pick_row(r):
        rows = jnp.concatenate([grids[at, pl.ds(r, 32, stride=8), :] for at in range(4)], axis=1)
        high, middle, low = split3(rows)
        parts = jnp.concatenate([high, middle, low, jnp.zeros_like(low)], axis=0)
        picked = dot(pick, parts)
        pot = jnp.where(bits[4], picked[:, 128:256], picked[:, 0:128])
        heat = jnp.where(bits[4], picked[:, 384:512], picked[:, 256:384])
        wide[r] = jnp.where(
            upper,
            jnp.where(bits[3], heat, pltpu.roll(heat, 64, 1)),
            jnp.where(bits[3], pltpu.roll(pot, 64, 1), pot),
        )

    for r in range(1, 7):
        pick_row(r)
    take(rim_recv.at[0], rim_sems.at[1, 0])
    take(rim_recv.at[1], rim_sems.at[1, 1])
    edge8 = iota((8, lon), 0)
    top = heat_of(0, 8, above[0:8], jnp.where(edge8 == 0, rim_recv[0, 7:8, :], below[0:8]))
    bottom = heat_of(
        lat - 8, lat, jnp.where(edge8 == 7, rim_recv[1, 0:1, :], above[lat - 8 :]), below[lat - 8 :]
    )
    for first_row, part in ((0, top), (lat - 8, bottom)):
        heat_ref[first_row : first_row + 8, :] = part
        grids[2, first_row : first_row + 8, :] = part[:, 0:128]
        grids[3, first_row : first_row + 8, :] = part[:, 128:256]
    for r in (0, 7):
        pick_row(r)

    def join(first, second, at):
        width = 8 << at
        return jnp.where(
            (lane_slot & width) == 0,
            jnp.where(bits[at], pltpu.roll(first, 128 - width, 1), first),
            jnp.where(bits[at], second, pltpu.roll(second, width, 1)),
        )

    quads = [join(wide[r], wide[r + 4], 2) for r in range(4)]
    twos = [join(quads[r], quads[r + 2], 1) for r in range(2)]
    reply_send[...] = join(twos[0], twos[1], 0).reshape(count, cap, 128)
    send_all(reply_send, reply_recv, 4)
    chosen = jnp.where(iota((256, slots), 1).astype(F32) == slot[:, 0:1], 1.0, 0.0).astype(BF16)
    take(reply_recv.at[pl.ds(0, count - 1)], recv_sems.at[4])
    back_high, back_low = split(reply_recv[...].reshape(slots, 128))
    blocks_ref[...] = dot(chosen, back_high) + dot(chosen, back_low)

    for at, (sent_x, sent_y, _, _) in enumerate((first, of_faces, rest, last)):
        drain_edges(at, sent_x, sent_y)
    take(face_send.at[pl.ds(0, count - 1)], send_sems.at[0])
    take(spec_send.at[pl.ds(0, nb - 1)], send_sems.at[1])
    take(coef_recv.at[pl.ds(0, na - 1)], send_sems.at[2])
    take(syn_all.at[pl.ds(0, nb - 1)], send_sems.at[3])
    take(reply_send.at[pl.ds(0, count - 1)], send_sems.at[4])
    for at in range(4):
        take(corner_send, corner_sems.at[0, at])
    take(rim_send.at[0], rim_sems.at[0, 1])
    take(rim_send.at[1], rim_sems.at[0, 0])


def write_out(slab, potential, heating, blocks, *refs):
    pieces = [(slab.at[v], refs[0].at[v]) for v in range(8)]
    pieces += [(potential, refs[1]), (heating, refs[2]), (blocks, refs[3])]
    copies = [
        pltpu.make_async_copy(src, dst, refs[4].at[k]) for k, (src, dst) in enumerate(pieces)
    ]
    for copy in copies:
        copy.start()
    for copy in copies:
        copy.wait()


def solution(mesh):
    na, nb = mesh.shape["blk"], mesh.shape["inner"]
    count = na * nb

    def shards(slab, speeds, source_matrix, pedersen, owners, tile_positions):
        lat, lon = pedersen.shape
        blocks = owners.shape[0]
        cap = max(2, 2 * blocks // count)
        slots = count * cap
        orders = PAIRS * 2 * nb
        wave, twiddle, table, steps = spectral_tables(na, nb, lat, lon)
        width = steps * PAIRS
        vmem = pl.BlockSpec(memory_space=pltpu.VMEM)
        hbm = pl.BlockSpec(memory_space=pl.ANY)
        dma = pltpu.SemaphoreType.DMA
        shapes = (slab.shape, (lat, lon), (lat, lon), (blocks, 128))

        def edges(rows_x, rows_y):
            return [
                pltpu.VMEM((2, rows_x, 128), F32),
                pltpu.VMEM((rows_y, 128), F32),
                pltpu.VMEM((2, rows_x, 128), F32),
                pltpu.VMEM((2, rows_y, 128), F32),
            ]

        results = pl.pallas_call(
            functools.partial(kernel, (na, nb, steps)),
            out_shape=tuple(pltpu.VMEM(shape, F32) for shape in shapes),
            in_specs=[
                hbm,
                hbm,
                pl.BlockSpec(memory_space=pltpu.SMEM),
                hbm,
                vmem,
                vmem,
                hbm,
                hbm,
                hbm,
            ],
            out_specs=(vmem,) * 4,
            scratch_shapes=[
                pltpu.VMEM(slab.shape, F32),
                pltpu.VMEM(speeds.shape, F32),
                pltpu.VMEM((lat, lon), F32),
                pltpu.VMEM(wave.shape, F32),
                pltpu.VMEM(twiddle.shape, F32),
                pltpu.VMEM((steps // 16 + 1, PAIRS, 128), F32),
                pltpu.VMEM((7, 4, 128, 128), F32),
                pltpu.VMEM((8, 4, 128, 128), F32),
                pltpu.VMEM((3, 128, 128), F32),
                pltpu.VMEM((2, 128, 128), F32),
                *edges(8, 16),
                *edges(32, 64),
                *edges(8, 8),
                pltpu.VMEM((2, 8, 128), F32),
                pltpu.VMEM((8, 128), F32),
                pltpu.VMEM((4, 8, 128), F32),
                *edges(32, 64),
                pltpu.VMEM((128, 128), F32),
                pltpu.VMEM((slots, 256), BF16),
                pltpu.VMEM((slots, 128), F32),
                pltpu.VMEM((count, cap, 128), F32),
                pltpu.VMEM((count, cap, 128), F32),
                pltpu.VMEM((2, lat, 128), F32),
                pltpu.VMEM((2, 2 * orders, lon), BF16),
                pltpu.VMEM((2, 2 * orders, 2 * lon), BF16),
                pltpu.VMEM((nb, 4 * PAIRS, lat), F32),
                pltpu.VMEM((nb, 4 * PAIRS, lat), F32),
                pltpu.VMEM((3, width, lat), BF16),
                pltpu.VMEM((2, PAIRS, width), F32),
                pltpu.VMEM((2, width), F32),
                pltpu.VMEM((na, 2, width), F32),
                pltpu.VMEM((nb, 4 * PAIRS, lat), F32),
                pltpu.VMEM((2, 8, lon), F32),
                pltpu.VMEM((2, 8, lon), F32),
                pltpu.VMEM((4, lat, 128), F32),
                pltpu.VMEM((8, slots, 128), F32),
                pltpu.VMEM((count, cap, 128), F32),
                pltpu.VMEM((count, cap, 128), F32),
                dma((2, 4, 4)),
                dma((5,)),
                dma((5,)),
                dma((2, 2)),
                dma((2, 4)),
                dma((8,)),
                pltpu.SemaphoreType.REGULAR((2,)),
            ],
            compiler_params=pltpu.CompilerParams(
                collective_id=0, has_side_effects=True, vmem_limit_bytes=VMEM_LIMIT
            ),
        )(
            slab,
            speeds,
            source_matrix,
            pedersen,
            owners.reshape(1, blocks),
            tile_positions.reshape(1, blocks),
            jnp.asarray(wave),
            jnp.asarray(twiddle),
            jnp.asarray(table),
        )
        return pl.pallas_call(
            write_out,
            out_shape=tuple(jax.ShapeDtypeStruct(shape, F32) for shape in shapes),
            in_specs=[vmem] * 4,
            out_specs=(hbm,) * 4,
            scratch_shapes=[dma((11,))],
            compiler_params=pltpu.CompilerParams(vmem_limit_bytes=16 * 1024 * 1024),
        )(*results)

    in_specs = (
        P(None, None, "blk", "inner"),
        P(None, None, "blk", "inner"),
        P(),
        P("blk", "inner"),
        P(("blk", "inner"), None),
        P(("blk", "inner")),
    )
    out_specs = (
        P(None, None, "blk", "inner"),
        P("blk", "inner"),
        P("blk", "inner"),
        P(("blk", "inner"), None),
    )
    return jax.shard_map(shards, mesh=mesh, in_specs=in_specs, out_specs=out_specs, check_vma=False)
```

```python
import functools
import math

import jax
import jax.numpy as jnp
import numpy as np
from jax import lax
from jax.experimental import pallas as pl
from jax.experimental.pallas import tpu as pltpu
from jax.sharding import PartitionSpec as P

F32 = jnp.float32
BF16 = jnp.bfloat16
I32 = jnp.int32
MESH = pl.DeviceIdType.MESH
BLOCK = 8
PAIRS = 8
SCREENING = 2.0
GAIN = 4096.0
VMEM_LIMIT = 60 * 1024 * 1024


def iota(shape, dim):
    return lax.broadcasted_iota(I32, shape, dim)


def split(value):
    high = value.astype(BF16)
    return high, (value - high.astype(F32)).astype(BF16)


def split3(value):
    high = value.astype(BF16)
    rest = value - high.astype(F32)
    middle = rest.astype(BF16)
    return high, middle, (rest - middle.astype(F32)).astype(BF16)


def dot(left, right, dims=((1,), (0,))):
    return lax.dot_general(left, right, (dims, ((), ())), preferred_element_type=F32)


def dot3(left, right, dims):
    lh, ll = left
    rh, rl = right
    return dot(lh, rh, dims) + dot(ll, rh, dims) + dot(lh, rl, dims)


def spectral_tables(blk_count, inner_count, lat_dev, lon_dev):
    orders = PAIRS * 2 * inner_count
    degrees = orders
    lon_total = lon_dev * inner_count
    first = np.arange(inner_count * PAIRS).reshape(inner_count, 1, PAIRS)
    order_of = np.concatenate([first, orders - 1 - first], axis=1).reshape(-1)
    cols = np.arange(lon_dev)
    phase = (order_of[:, None] * cols[None, :] % lon_total) * (2.0 * math.pi / lon_total)
    wave = np.stack([np.cos(phase), np.sin(phase)]).astype(np.float32)
    turn = (order_of[:, None] * (np.arange(inner_count) * lon_dev)[None, :] % lon_total) * (
        2.0 * math.pi / lon_total
    )
    twiddle = np.zeros((order_of.shape[0], 128), np.float32)
    twiddle[:, :inner_count] = np.cos(turn)
    twiddle[:, 32 : 32 + inner_count] = np.sin(turn)
    twiddle[:, 64] = order_of
    twiddle[:, 65] = np.where(order_of == 0, 1.0, 2.0)

    turns = -(-(degrees + 1) // 16)
    steps = turns * 16
    table = np.zeros((inner_count, turns + 1, PAIRS, 128), np.float32)

    def up(degree, order):
        return np.sqrt(
            np.float32(4.0 * degree * degree - 1.0) / np.float32(degree * degree - order * order)
        )

    counter = np.arange(1, orders, dtype=np.float64)
    log_start = 0.5 * np.log(0.5) + np.concatenate(
        [np.zeros(1), np.cumsum(0.5 * np.log((2.0 * counter + 1.0) / (2.0 * counter)))]
    )
    for pair in range(inner_count * PAIRS):
        place, lane = divmod(pair, PAIRS)
        low, partner = pair, orders - 1 - pair
        table[place, turns, lane, :4] = [low, log_start[low], partner, log_start[partner]]
        for step in range(degrees + 1):
            if step <= low:
                order, degree, kind = partner, partner + step, 3
            else:
                order, degree, kind = low, step - 1, 2
            turn_at, offset = divmod(step, 16)
            if degree == order:
                table[place, turn_at, lane, kind * 16 + offset] = 1.0
                continue
            ratio = up(degree, order)
            table[place, turn_at, lane, offset] = ratio
            if degree >= order + 2:
                table[place, turn_at, lane, 16 + offset] = ratio / up(degree - 1, order)
    return wave, twiddle, table, steps


def kernel(
    sizes,
    u_hbm,
    w_hbm,
    mix_ref,
    ped_hbm,
    owner_ref,
    tile_ref,
    wave_hbm,
    twiddle_hbm,
    table_hbm,
    out_ref,
    pot_ref,
    heat_ref,
    blocks_ref,
    u_ref,
    w_ref,
    ped_ref,
    wave_ref,
    twiddle_ref,
    ratios,
    coef,
    u1,
    q_ref,
    source_ref,
    first_send_x,
    first_send_y,
    first_recv_x,
    first_recv_y,
    rest_send_x,
    rest_send_y,
    rest_recv_x,
    rest_recv_y,
    face_send_x,
    face_send_y,
    face_recv_x,
    face_recv_y,
    ring_x,
    corner_send,
    corner_recv,
    last_send_x,
    last_send_y,
    last_recv_x,
    last_recv_y,
    turned,
    sel_t,
    label_ref,
    face_send,
    face_recv,
    forcing,
    base_ref,
    values_ref,
    spec_send,
    spec_recv,
    leg,
    mask_ref,
    coef_send,
    coef_recv,
    syn_all,
    rim_send,
    rim_recv,
    grids,
    wide,
    reply_send,
    reply_recv,
    edge_sems,
    send_sems,
    recv_sems,
    rim_sems,
    corner_sems,
    in_sems,
    ready,
):
    na, nb, steps = sizes
    count = na * nb
    lat, lon = ped_ref.shape
    rows_total, cols_total = lat * na, lon * nb
    cap = face_send.shape[1]
    slots = count * cap
    a, b = lax.axis_index("blk"), lax.axis_index("inner")
    me = a * nb + b
    orders = PAIRS * 2 * nb
    spec_rows = 2 * orders

    nx, nz = na // 2, min(4, nb)
    ny = nb // nz
    chip_x, core, chip_y, chip_z = a // 2, lax.rem(a, 2), b // nz, lax.rem(b, nz)
    peer_a = {
        (dx, dc): lax.rem(chip_x + dx, nx) * 2 + lax.rem(core + dc, 2)
        for dx in range(nx)
        for dc in range(2)
    }
    peer_b = {
        (dy, dz): lax.rem(chip_y + dy, ny) * nz + lax.rem(chip_z + dz, nz)
        for dy in range(ny)
        for dz in range(nz)
    }

    def hops(move):
        dx, dc, dy, dz = move
        return 2 * (min(dx, nx - dx) + min(dy, ny - dy) + min(dz, nz - dz)) + dc

    moves = sorted(
        [(dx, dc, dy, dz) for dx, dc in peer_a for dy, dz in peer_b if (dx, dc, dy, dz) != (0, 0, 0, 0)],
        key=hops,
        reverse=True,
    )
    blk_moves = [move for move in moves if move[2:] == (0, 0)]
    inner_moves = [move for move in moves if move[:2] == (0, 0)]

    def device(move):
        return peer_a[move[:2]], peer_b[move[2:]]

    def remote(src, dst, send_sem, recv_sem, target):
        pltpu.make_async_remote_copy(
            src_ref=src,
            dst_ref=dst,
            send_sem=send_sem,
            recv_sem=recv_sem,
            device_id=target,
            device_id_type=MESH,
        ).start()

    def take(ref, sem):
        pltpu.make_async_copy(ref, ref, sem).wait()

    def signal(sem, target):
        pl.semaphore_signal(sem, inc=1, device_id=target, device_id_type=MESH)

    up_a, down_a = lax.rem(a + 1, na), lax.rem(a + na - 1, na)
    up_b, down_b = lax.rem(b + 1, nb), lax.rem(b + nb - 1, nb)

    fetches = [
        pltpu.make_async_copy(src, dst, in_sems.at[at])
        for at, (src, dst) in enumerate(
            [
                (w_hbm, w_ref),
                (u_hbm.at[7], u_ref.at[7]),
                (u_hbm.at[pl.ds(0, 7), pl.ds(0, 3)], u_ref.at[pl.ds(0, 7), pl.ds(0, 3)]),
                (u_hbm.at[pl.ds(0, 7), pl.ds(3, 1)], u_ref.at[pl.ds(0, 7), pl.ds(3, 1)]),
                (twiddle_hbm, twiddle_ref),
                (wave_hbm, wave_ref),
                (table_hbm.at[b], ratios),
                (ped_hbm, ped_ref),
            ]
        )
    ]
    for fetch in fetches:
        fetch.start()
    barrier = pltpu.get_barrier_semaphore()
    y_moves = [move for move in inner_moves if move[3] == 0]
    z_moves = [move for move in inner_moves if move[2] == 0]
    greeted = [device(move) for move in blk_moves + y_moves + z_moves]
    greeted += [(a, up_b), (a, down_b)]
    corners = [(up_a, up_b), (up_a, down_b), (down_a, up_b), (down_a, down_b)]
    greeted += corners
    for target in greeted:
        signal(barrier, target)

    row = iota((128, 128), 0)
    lane = iota((128, 128), 1)
    row8 = iota((8, 128), 0)
    fetches[0].wait()

    def make_coef(z, carry):
        wx, wy = 0.15 * w_ref[0, z], 0.15 * w_ref[1, z]
        coef[0, z] = jnp.where(row == 127, 0.0, 0.15 + wx)
        coef[1, z] = jnp.where(row == 0, 0.0, 0.15 - wx)
        coef[2, z] = jnp.where(lane == 127, 0.0, 0.15 + wy)
        coef[3, z] = jnp.where(lane == 0, 0.0, 0.15 - wy)
        below = 0.15 + 0.15 * w_ref[2, jnp.maximum(z - 1, 0)]
        above = 0.15 - 0.15 * w_ref[2, jnp.minimum(z + 1, 3)]
        coef[4, z] = jnp.where(z > 0, below, 0.0)
        coef[5, z] = jnp.where(z < 3, above, 0.0)
        coef[6, z] = jnp.where(lane == 0, 0.15 - wy, 0.15 + wy)
        return carry

    lax.fori_loop(0, 4, make_coef, 0)

    def weighted(weights, z):
        total = weights[0] * u_ref[0, z]
        for w in range(1, 8):
            total = total + weights[w] * u_ref[w, z]
        return total

    source = [mix_ref[7, w] for w in range(8)]
    second = []
    for w in range(8):
        total = source[0] * mix_ref[0, w]
        for k in range(1, 8):
            total = total + source[k] * mix_ref[k, w]
        second.append(total)
    fetches[1].wait()
    fetches[2].wait()
    for z in range(3):
        q_ref[z] = weighted(source, z)

    def pack(src, items, send_x, send_y):
        packed = jnp.zeros((128, 128), F32)
        for k, (v, z) in enumerate(items):
            cells = q_ref.at[z] if v == 8 else src.at[v, z]
            last = (0.15 + 0.15 * w_ref[0, z, 120:128, :]) * cells[120:128, :]
            first = (0.15 - 0.15 * w_ref[0, z, 0:8, :]) * cells[0:8, :]
            send_x[0, k : k + 1, :] = last[7:8, :]
            send_x[1, k : k + 1, :] = first[0:1, :]
            rolled = pltpu.roll(coef[6, z] * cells[...], 2 * k + 1, 1)
            packed = jnp.where((lane == 2 * k) | (lane == 2 * k + 1), rolled, packed)
        send_y[...] = packed.T[0 : send_y.shape[0], :]

    def send_edges(at, send_x, send_y, recv_x, recv_y):
        for side, target in ((0, (up_a, b)), (1, (down_a, b))):
            remote(
                send_x.at[side],
                recv_x.at[side],
                edge_sems.at[0, at, side],
                edge_sems.at[1, at, side],
                target,
            )
        for side, target in ((0, (a, up_b)), (1, (a, down_b))):
            remote(
                send_y,
                recv_y.at[side],
                edge_sems.at[0, at, 2 + side],
                edge_sems.at[1, at, 2 + side],
                target,
            )

    def wait_edges(at, recv_x, recv_y):
        for side in range(2):
            take(recv_x.at[side], edge_sems.at[1, at, side])
            take(recv_y.at[side], edge_sems.at[1, at, 2 + side])
        rows = recv_y.shape[1]
        odd = (iota((rows, 128), 0) & 1) == 1
        up = jnp.where(b > 0, recv_y[0], 0.0)
        down = jnp.where(b < nb - 1, recv_y[1], 0.0)
        mixed = jnp.where(odd, pltpu.roll(up, 1, 0), pltpu.roll(down, rows - 1, 0))
        if rows < 128:
            mixed = jnp.concatenate([mixed, jnp.zeros((128 - rows, 128), F32)], axis=0)
        turned[...] = mixed.T

    def drain_edges(at, send_x, send_y):
        for side in range(2):
            take(send_x.at[side], edge_sems.at[0, at, side])
            take(send_y, edge_sems.at[0, at, 2 + side])

    def mend(cells, recv_x, k):
        rolled = pltpu.roll(turned[...], 127 - 2 * k, 1)
        whole = cells[...] + jnp.where((lane == 0) | (lane == 127), rolled, 0.0)
        from_down = jnp.where(a > 0, recv_x[0, k : k + 1, :], 0.0)
        from_up = jnp.where(a < na - 1, recv_x[1, k : k + 1, :], 0.0)
        cells[8:120, :] = whole[8:120]
        cells[0:8, :] = whole[0:8] + jnp.where(row8 == 0, from_down, 0.0)
        cells[120:128, :] = whole[120:128] + jnp.where(row8 == 7, from_up, 0.0)

    def transport(field, z):
        u = field(z)
        total = pltpu.roll(coef[0, z] * u, 1, 0) + pltpu.roll(coef[1, z] * u, 127, 0)
        total = total + pltpu.roll(coef[2, z] * u, 1, 1) + pltpu.roll(coef[3, z] * u, 127, 1)
        if z > 0:
            total = total + coef[4, z] * field(z - 1)
        if z < 3:
            total = total + coef[5, z] * field(z + 1)
        return total + 0.1 * u

    def advance(src, dst, v, z):
        u = src[v, z]
        total = mix_ref[v, 0] * src[0, z]
        for w in range(1, 8):
            total = total + mix_ref[v, w] * src[w, z]
        total = 0.3 * total + 0.1 * u
        total = total + pltpu.roll(coef[0, z] * u, 1, 0) + pltpu.roll(coef[1, z] * u, 127, 0)
        total = total + pltpu.roll(coef[2, z] * u, 1, 1) + pltpu.roll(coef[3, z] * u, 127, 1)
        if not (isinstance(z, int) and z == 0):
            total = total + coef[4, z] * src[v, z - 1 if isinstance(z, int) else jnp.maximum(z - 1, 0)]
        if not (isinstance(z, int) and z == 3):
            total = total + coef[5, z] * src[v, z + 1 if isinstance(z, int) else jnp.minimum(z + 1, 3)]
        dst[v, z] = total

    def advance_all(src, dst, vs, z):
        def one(v, carry):
            advance(src, dst, v, z)
            return carry

        lax.fori_loop(0, vs, one, 0)

    near = [(7, 0), (7, 1), (7, 2), (8, 0), (8, 1)]
    far = [(v, z) for z in range(4) for v in range(7)] + [(7, 3)]
    faced = [(7, 0), (7, 1)]
    later = [(v, z) for z in range(4) for v in range(8) if (v, z) not in faced]
    first = (first_send_x, first_send_y, first_recv_x, first_recv_y)
    rest = (rest_send_x, rest_send_y, rest_recv_x, rest_recv_y)
    of_faces = (face_send_x, face_send_y, face_recv_x, face_recv_y)
    last = (last_send_x, last_send_y, last_recv_x, last_recv_y)

    pack(u_ref, near, first_send_x, first_send_y)
    at_0, at_1 = near.index((7, 0)), near.index((7, 1))
    for side in range(2):
        for z, k in enumerate((at_0, at_1)):
            corner_send[2 * side + z : 2 * side + z + 1, :] = first_send_x[side, k : k + 1, :]
            corner_send[4 + 2 * side + z : 5 + 2 * side + z, :] = first_send_y[
                2 * k + side : 2 * k + side + 1, :
            ]
    for z in (0, 1):
        u1[7, z] = transport(lambda at: u_ref[7, at], z) + 0.3 * q_ref[z]
    columns = jnp.zeros((128, 128), F32)
    for z in (0, 1):
        upper = 0.15 + 0.15 * w_ref[0, z, 120:128, :]
        lower = 0.15 - 0.15 * w_ref[0, z, 0:8, :]
        face_send_x[0, z : z + 1, :] = (upper * u1[7, z, 120:128, :])[7:8, :]
        face_send_x[0, 2 + z : 3 + z, :] = upper[7:8, :]
        face_send_x[1, z : z + 1, :] = (lower * u1[7, z, 0:8, :])[0:1, :]
        face_send_x[1, 2 + z : 3 + z, :] = lower[0:1, :]
        factor = coef[6, z]
        scaled = factor * u1[7, z]
        columns = jnp.where(lane == z, pltpu.roll(scaled, 1 + z, 1), columns)
        columns = jnp.where(lane == 2 + z, pltpu.roll(factor, 3 + z, 1), columns)
        columns = jnp.where(lane == 4 + z, pltpu.roll(scaled, 4 + z, 1), columns)
        columns = jnp.where(lane == 6 + z, pltpu.roll(factor, 6 + z, 1), columns)
    face_send_y[...] = columns.T[0:8, :]
    pl.semaphore_wait(barrier, len(greeted))
    send_edges(1, *of_faces)
    send_edges(0, *first)
    for at, target in enumerate(corners):
        remote(corner_send, corner_recv.at[at], corner_sems.at[0, at], corner_sems.at[1, at], target)
    for move in y_moves:
        signal(ready.at[0], device(move))
    u1[7, 2] = transport(lambda at: u_ref[7, at], 2) + 0.3 * q_ref[2]
    for z in (0, 1):
        source_ref[z] = transport(lambda at: q_ref[at], z) + 0.3 * weighted(second, z)
    if y_moves:
        pl.semaphore_wait(ready.at[0], len(y_moves))
    for move in blk_moves:
        signal(ready.at[1], device(move))

    owner = jnp.broadcast_to(owner_ref[...].astype(F32), (128, 256)).T.astype(I32)
    owner_hot = jnp.where(iota((256, 128), 1) == owner, 1.0, 0.0)
    earlier = jnp.where(iota((256, 256), 0) > iota((256, 256), 1), 1.0, 0.0).astype(BF16)
    before = dot(earlier, owner_hot.astype(BF16))
    rank = jnp.sum(before * owner_hot, axis=1, keepdims=True)
    slot = owner.astype(F32) * float(cap) + rank
    slot_row = slot.T[0:1, :]
    sel = jnp.where(iota((slots, 256), 0).astype(F32) == slot_row, 1.0, 0.0).astype(BF16)
    flip = jnp.where(iota((256, 256), 0) == (iota((256, 256), 1) ^ 7), 1.0, 0.0).astype(BF16)
    sel_t[...] = dot(sel, flip).astype(BF16)
    tile_high, tile_low = split(jnp.broadcast_to(tile_ref[...].astype(F32), (128, 256)).T)
    label_ref[...] = dot(sel, tile_high) + dot(sel, tile_low)

    wait_edges(0, first_recv_x, first_recv_y)
    for k, (v, z) in enumerate(near):
        mend(source_ref.at[z] if v == 8 else u1.at[v, z], first_recv_x, k)
    for z in (0, 1):
        out_ref[7, z] = transport(lambda at: u1[7, at], z) + 0.3 * source_ref[z]

    for side in range(2):
        take(face_recv_x.at[side], edge_sems.at[1, 1, side])
        take(face_recv_y.at[side], edge_sems.at[1, 1, 2 + side])
    for at in range(4):
        take(corner_recv.at[at], corner_sems.at[1, at])
    own = corner_send[...]
    low_low = jnp.where((a > 0) & (b > 0), corner_recv[0], 0.0)
    low_high = jnp.where((a > 0) & (b < nb - 1), corner_recv[1], 0.0)
    high_low = jnp.where((a < na - 1) & (b > 0), corner_recv[2], 0.0)
    high_high = jnp.where((a < na - 1) & (b < nb - 1), corner_recv[3], 0.0)
    low_low, high_high = pltpu.roll(low_low, 1, 1), pltpu.roll(high_high, 127, 1)
    lane2 = iota((2, 128), 1)

    def beyond(came, rows, first_rows, last_rows):
        brought = rows + jnp.where(lane2 == 0, first_rows, 0.0)
        brought = brought + jnp.where(lane2 == 127, last_rows, 0.0)
        return came[0:2] + came[2:4] * brought

    from_left = beyond(face_recv_y[0, 0:4], own[6:8], low_low[0:2], high_low[2:4])
    from_right = beyond(face_recv_y[1, 4:8], own[4:6], low_high[0:2], high_high[2:4])
    from_left = jnp.where(b > 0, from_left, 0.0)
    from_right = jnp.where(b < nb - 1, from_right, 0.0)
    ring_x[0, 0:2, :] = beyond(face_recv_x[0, 0:4], own[2:4], low_low[4:6], low_high[6:8])
    ring_x[1, 0:2, :] = beyond(face_recv_x[1, 0:4], own[0:2], high_low[4:6], high_high[6:8])
    beside = [from_right[0:1], from_left[0:1], from_right[1:2], from_left[1:2]]
    turned[...] = jnp.concatenate(beside + [jnp.zeros((124, 128), F32)], axis=0).T
    for k, (v, z) in enumerate(faced):
        mend(out_ref.at[v, z], ring_x, k)
    current = out_ref[7, 1] - out_ref[7, 0]

    halves = [pltpu.roll(current, 64, 1).reshape(16, 8, 128), current.reshape(16, 8, 128)]
    group = iota((16, 8, 128), 2) // 8
    faces = []
    for half in range(2):
        face = jnp.zeros((16, 8, 128), F32)
        for r in range(8):
            spread = jnp.broadcast_to(halves[half][:, r : r + 1, :], (16, 8, 128))
            moved = pltpu.roll(spread, 8 * r + 8, 2, stride=8, stride_axis=1)
            face = jnp.where(group == r, moved, face)
        faces.append(face)
    faces = jnp.stack(faces, axis=1).reshape(256, 128)
    face_high, face_low = split(faces)
    routed = dot(sel_t[...], face_high) + dot(sel_t[...], face_low)
    lane_slot = iota((slots, 128), 1)
    routed = jnp.where(lane_slot < 64, routed, label_ref[...])
    face_send[...] = routed.reshape(count, cap, 128)

    def send_all(src, dst, at):
        for move in moves:
            peer_of_a, peer_of_b = device(move)
            remote(
                src.at[peer_of_a * nb + peer_of_b],
                dst.at[me],
                send_sems.at[at],
                recv_sems.at[at],
                (peer_of_a, peer_of_b),
            )
        dst[me] = src[me]

    pl.semaphore_wait(ready.at[1], len(blk_moves))
    send_all(face_send, face_recv, 0)

    fetches[3].wait()
    pack(u_ref, far, rest_send_x, rest_send_y)
    send_edges(2, *rest)

    fetches[4].wait()
    fetches[5].wait()

    def per_row(column):
        return jnp.sum(
            jnp.where(iota((orders, 128), 1) == column, twiddle_ref[...], 0.0),
            axis=1,
            keepdims=True,
        )

    def rows_of(even, odd):
        return jnp.concatenate([even, odd], axis=2).reshape(spec_rows, lon)

    def waves():
        cos_turn, sin_turn = per_row(b), per_row(b + 32)
        cos_wave, sin_wave = wave_ref[0], wave_ref[1]
        cosine = (cos_turn * cos_wave - sin_turn * sin_wave).reshape(nb, 2, 1, PAIRS, lon)
        sine = (sin_turn * cos_wave + cos_turn * sin_wave).reshape(nb, 2, 1, PAIRS, lon)
        return cosine, sine

    cosine, sine = waves()
    base_high, base_low = split(rows_of(cosine, sine) * (1.0 / cols_total))
    base_ref[0] = base_high
    base_ref[1] = base_low

    for z in range(3):
        advance_all(u_ref, u1, 7, z)

    take(face_recv.at[pl.ds(0, count - 1)], recv_sems.at[0])
    got = face_recv[...].reshape(slots, 128)
    swapped = pltpu.roll(got, 64, 1)
    label = jnp.where(lane_slot < 64, swapped, got).astype(I32)
    face = jnp.where(lane_slot < 64, got, swapped)
    tile_row, tile_col = label >> 5, label & 31
    tile_row_t = tile_row.astype(F32).T.astype(I32)
    scatter = jnp.where(iota((32, slots), 0) == tile_row_t[0:32, :], 1.0, 0.0).astype(BF16)
    scatter = jnp.concatenate([scatter, scatter], axis=1)
    col_masks = [
        jnp.where((lane_slot >> 3) + 16 * half == tile_col, 1.0, 0.0).astype(BF16)
        for half in range(2)
    ]

    def spread_bit(value, width):
        moved = pltpu.roll(value, width, 1)
        bit = (lane_slot & width) == 0
        return [jnp.where(bit, value, moved), jnp.where(bit, moved, value)]

    lines = [face]
    for width in (32, 16, 8):
        lines = [part for line in lines for part in spread_bit(line, width)]
    for r in range(8):
        line_high, line_low = split(lines[r])
        right = jnp.concatenate(
            [
                jnp.concatenate([part * mask for mask in col_masks], axis=1)
                for part in (line_high, line_low)
            ],
            axis=0,
        )
        rows = dot(scatter, right)
        forcing[0, pl.ds(r, 32, stride=8), :] = rows[:, 0:128]
        forcing[1, pl.ds(r, 32, stride=8), :] = rows[:, 128:256]

    middle_row = lat // 2
    for half in range(2):
        rows = slice(half * middle_row, (half + 1) * middle_row)
        force = split(jnp.concatenate([forcing[0, rows], forcing[1, rows]], axis=1))
        spectrum = dot3((base_ref[0], base_ref[1]), force, ((1,), (1,)))
        spec_send[half] = spectrum.reshape(nb, 4 * PAIRS, middle_row)
        for move in inner_moves:
            peer = peer_b[move[2:]]
            remote(
                spec_send.at[half, peer],
                spec_recv.at[half, b],
                send_sems.at[1 + 4 * half],
                recv_sems.at[1 + 4 * half],
                (a, peer),
            )
        spec_recv[half, b] = spec_send[half, b]

    fetches[6].wait()
    row_of_lane = a * lat + iota((PAIRS, lat), 1)
    x = -1.0 + (2.0 * row_of_lane.astype(F32) + 1.0) / rows_total
    log_sine = jnp.log(jnp.sqrt(1.0 - x * x))
    turns = steps // 16
    heads = ratios[turns]
    low_start = jnp.exp(heads[:, 1:2] + heads[:, 0:1] * log_sine)
    high_start = jnp.exp(heads[:, 3:4] + heads[:, 2:3] * log_sine)

    def build(turn, carry):
        previous, older = carry
        block = ratios[turn]
        made = []
        for offset in range(16):
            up = block[:, offset : offset + 1]
            down = block[:, 16 + offset : 17 + offset]
            begin_low = block[:, 32 + offset : 33 + offset]
            begin_high = block[:, 48 + offset : 49 + offset]
            present = (
                begin_low * low_start + begin_high * high_start + up * x * previous - down * older
            )
            made.append(present)
            older, previous = previous, present
        where = pl.ds(pl.multiple_of(turn * 128, 128), 128)
        for at, part in enumerate(split3(jnp.concatenate(made, axis=0))):
            leg[at, where, :] = part
        return previous, older

    empty = jnp.zeros((PAIRS, lat), F32)
    lax.fori_loop(0, turns, build, (empty, empty))

    width = steps * PAIRS
    at_step = iota((PAIRS, width), 1) // PAIRS
    at_pair = lax.rem(iota((PAIRS, width), 1), PAIRS)
    order_low = b * PAIRS + at_pair
    is_high = at_step <= order_low
    degree = jnp.where(is_high, orders - 1 - order_low + at_step, at_step - 1).astype(F32)
    scale = (2.0 / rows_total) * GAIN / (degree * (degree + 1.0) + SCREENING)
    scale = jnp.where(at_step <= orders, scale, 0.0)
    mine = at_pair == iota((PAIRS, width), 0)
    mask_ref[0] = jnp.where(mine & jnp.logical_not(is_high), scale, 0.0)
    mask_ref[1] = jnp.where(mine & is_high, scale, 0.0)

    advance_all(u_ref, u1, 8, 3)
    wait_edges(2, rest_recv_x, rest_recv_y)
    for k, (v, z) in enumerate(far):
        mend(u1.at[v, z], rest_recv_x, k)
    pack(u1, later, last_send_x, last_send_y)
    send_edges(3, *last)

    wide_sums = None
    for half in range(2):
        take(spec_recv.at[half, pl.ds(0, nb - 1)], recv_sems.at[1 + 4 * half])
        spec = spec_recv[half, 0]
        for at in range(1, nb):
            spec = spec + spec_recv[half, at]
        spec_high, spec_low = split(spec)
        cols = slice(half * middle_row, (half + 1) * middle_row)
        both = dot(jnp.concatenate([spec_high, spec_low], axis=0), leg[0, :, cols], ((1,), (1,)))
        part = both[0:32] + both[32:64] + dot(spec_high, leg[1, :, cols], ((1,), (1,)))
        wide_sums = part if wide_sums is None else wide_sums + part
    for parity in range(2):
        low_rows = wide_sums[parity * 8 : parity * 8 + 8]
        high_rows = wide_sums[16 + parity * 8 : 24 + parity * 8]
        kept = low_rows * mask_ref[0] + high_rows * mask_ref[1]
        coef_send[parity : parity + 1, :] = jnp.sum(kept, axis=0, keepdims=True)
    for move in blk_moves:
        remote(
            coef_send,
            coef_recv.at[a],
            send_sems.at[2],
            recv_sems.at[2],
            (peer_a[move[:2]], b),
        )
    coef_recv[a] = coef_send[...]
    for z in (0, 1):
        advance_all(u1, out_ref, 7, z)
    take(coef_recv.at[pl.ds(0, na - 1)], recv_sems.at[2])
    solved = coef_recv[0]
    for at in range(1, na):
        solved = solved + coef_recv[at]
    expanded = []
    for kind in range(2):
        for parity in range(2):
            expanded.append(
                jnp.where(
                    mask_ref[kind] != 0.0,
                    jnp.broadcast_to(solved[parity : parity + 1, :], (PAIRS, width)),
                    0.0,
                )
            )
    solved_high, solved_low = split(jnp.concatenate(expanded, axis=0))
    solved_both = jnp.concatenate([solved_high, solved_low], axis=0)
    fine = dot(solved_high, leg[2])
    both = dot(solved_both, leg[0])
    middle = dot(solved_both, leg[1])
    syn = both[0:32] + (both[32:64] + (middle[0:32] + (middle[32:64] + fine)))
    for half in range(2):
        syn_all[half, b] = syn[:, half * middle_row : (half + 1) * middle_row]
    for half in range(2):
        for move in inner_moves:
            remote(
                syn_all.at[half, b],
                syn_all.at[half, b],
                send_sems.at[3 + 3 * half],
                recv_sems.at[3 + 3 * half],
                (a, peer_b[move[2:]]),
            )
    order_col, weight_col = per_row(64), per_row(65)
    cosine, sine = waves()
    weight = weight_col.reshape(nb, 2, 1, PAIRS, 1)
    slope_weight = (weight_col * order_col).reshape(nb, 2, 1, PAIRS, 1)
    value_high, value_low = split(rows_of(cosine * weight, sine * weight))
    values_ref[0, :, 0:lon] = value_high
    values_ref[1, :, 0:lon] = value_low
    slope_high, slope_low = split(rows_of(-sine * slope_weight, cosine * slope_weight))
    values_ref[0, :, lon : 2 * lon] = slope_high
    values_ref[1, :, lon : 2 * lon] = slope_low

    for z in (2, 3):
        advance_all(u1, out_ref, 8, z)
    wait_edges(3, last_recv_x, last_recv_y)
    for k, (v, z) in enumerate(later):
        mend(out_ref.at[v, z], last_recv_x, k)

    def potential_of(high, middle, low):
        rows = high.shape[0]
        coarse = dot(jnp.concatenate([high, middle, low], axis=0), values_ref[0, :, 0:lon])
        rest_of = dot(jnp.concatenate([high, middle], axis=0), values_ref[1, :, 0:lon])
        return coarse[0:rows] + (
            coarse[rows : 2 * rows] + (rest_of[0:rows] + (coarse[2 * rows :] + rest_of[rows:]))
        )

    potentials, slopes = [], []
    for half, target in enumerate(((down_a, b), (up_a, b))):
        take(syn_all.at[half, pl.ds(0, nb - 1)], recv_sems.at[3 + 3 * half])
        parts = split3(syn_all[half].reshape(spec_rows, middle_row).T)
        rims = potential_of(*(part[0:16] if half == 0 else part[middle_row - 16 :] for part in parts))
        rim_send[half] = rims[0:8] if half == 0 else rims[8:16]
        remote(
            rim_send.at[half],
            rim_recv.at[1 - half],
            rim_sems.at[0, half],
            rim_sems.at[1, 1 - half],
            target,
        )
        potentials.append(potential_of(*parts))
        coarse = dot(jnp.concatenate(parts[0:2], axis=0), values_ref[0, :, lon : 2 * lon])
        finer = dot(parts[0], values_ref[1, :, lon : 2 * lon])
        slopes.append(coarse[0:middle_row] + (coarse[middle_row:] + finer))
    potential = jnp.concatenate(potentials, axis=0)
    azimuthal = jnp.concatenate(slopes, axis=0)
    pot_ref[...] = potential
    fetches[7].wait()
    grid_row = iota((lat, 1), 0)
    global_row = a * lat + grid_row
    x_col = -1.0 + (2.0 * global_row.astype(F32) + 1.0) / rows_total
    sine_col = jnp.sqrt(1.0 - x_col * x_col)
    eastward = azimuthal / sine_col
    inverse = rows_total / 2.0

    def heat_of(first_row, last_row, above, below):
        part = slice(first_row, last_row)
        at_first, at_last = global_row[part] == 0, global_row[part] == rows_total - 1
        here = potential[part]
        slope = (jnp.where(at_last, here, above) - jnp.where(at_first, here, below)) * (
            jnp.where(at_first | at_last, inverse, 0.5 * inverse)
        )
        polar = sine_col[part] * slope
        return ped_ref[part, :] * (polar * polar + eastward[part] * eastward[part])

    above, below = pltpu.roll(potential, lat - 1, 0), pltpu.roll(potential, 1, 0)
    heating = heat_of(0, lat, above, below)
    heat_ref[...] = heating

    grids[0] = potential[:, 0:128]
    grids[1] = potential[:, 128:256]
    grids[2] = heating[:, 0:128]
    grids[3] = heating[:, 128:256]
    pick = iota((slots, 128), 1)
    pick = jnp.where((pick < 96) & ((pick & 31) == tile_row), 1.0, 0.0).astype(BF16)
    bits = [(tile_col & (1 << at)) != 0 for at in range(5)]
    upper = lane_slot >= 64

    def pick_row(r):
        rows = jnp.concatenate([grids[at, pl.ds(r, 32, stride=8), :] for at in range(4)], axis=1)
        high, middle, low = split3(rows)
        parts = jnp.concatenate([high, middle, low, jnp.zeros_like(low)], axis=0)
        picked = dot(pick, parts)
        pot = jnp.where(bits[4], picked[:, 128:256], picked[:, 0:128])
        heat = jnp.where(bits[4], picked[:, 384:512], picked[:, 256:384])
        wide[r] = jnp.where(
            upper,
            jnp.where(bits[3], heat, pltpu.roll(heat, 64, 1)),
            jnp.where(bits[3], pltpu.roll(pot, 64, 1), pot),
        )

    for r in range(1, 7):
        pick_row(r)
    take(rim_recv.at[0], rim_sems.at[1, 0])
    take(rim_recv.at[1], rim_sems.at[1, 1])
    edge8 = iota((8, lon), 0)
    top = heat_of(0, 8, above[0:8], jnp.where(edge8 == 0, rim_recv[0, 7:8, :], below[0:8]))
    bottom = heat_of(
        lat - 8, lat, jnp.where(edge8 == 7, rim_recv[1, 0:1, :], above[lat - 8 :]), below[lat - 8 :]
    )
    for first_row, part in ((0, top), (lat - 8, bottom)):
        heat_ref[first_row : first_row + 8, :] = part
        grids[2, first_row : first_row + 8, :] = part[:, 0:128]
        grids[3, first_row : first_row + 8, :] = part[:, 128:256]
    for r in (0, 7):
        pick_row(r)

    def join(first, second, at):
        width = 8 << at
        return jnp.where(
            (lane_slot & width) == 0,
            jnp.where(bits[at], pltpu.roll(first, 128 - width, 1), first),
            jnp.where(bits[at], second, pltpu.roll(second, width, 1)),
        )

    quads = [join(wide[r], wide[r + 4], 2) for r in range(4)]
    twos = [join(quads[r], quads[r + 2], 1) for r in range(2)]
    reply_send[...] = join(twos[0], twos[1], 0).reshape(count, cap, 128)
    send_all(reply_send, reply_recv, 4)
    chosen = jnp.where(iota((256, slots), 1).astype(F32) == slot[:, 0:1], 1.0, 0.0).astype(BF16)
    take(reply_recv.at[pl.ds(0, count - 1)], recv_sems.at[4])
    back_high, back_low = split(reply_recv[...].reshape(slots, 128))
    blocks_ref[...] = dot(chosen, back_high) + dot(chosen, back_low)

    for at, (sent_x, sent_y, _, _) in enumerate((first, of_faces, rest, last)):
        drain_edges(at, sent_x, sent_y)
    take(face_send.at[pl.ds(0, count - 1)], send_sems.at[0])
    for half in range(2):
        take(spec_send.at[half, pl.ds(0, nb - 1)], send_sems.at[1 + 4 * half])
        take(syn_all.at[half, pl.ds(0, nb - 1)], send_sems.at[3 + 3 * half])
    take(coef_recv.at[pl.ds(0, na - 1)], send_sems.at[2])
    take(reply_send.at[pl.ds(0, count - 1)], send_sems.at[4])
    for at in range(4):
        take(corner_send, corner_sems.at[0, at])
    take(rim_send.at[0], rim_sems.at[0, 0])
    take(rim_send.at[1], rim_sems.at[0, 1])


def write_out(slab, potential, heating, blocks, *refs):
    pieces = [(slab.at[v], refs[0].at[v]) for v in range(8)]
    pieces += [(potential, refs[1]), (heating, refs[2]), (blocks, refs[3])]
    copies = [
        pltpu.make_async_copy(src, dst, refs[4].at[k]) for k, (src, dst) in enumerate(pieces)
    ]
    for copy in copies:
        copy.start()
    for copy in copies:
        copy.wait()


def solution(mesh):
    na, nb = mesh.shape["blk"], mesh.shape["inner"]
    count = na * nb

    def shards(slab, speeds, source_matrix, pedersen, owners, tile_positions):
        lat, lon = pedersen.shape
        blocks = owners.shape[0]
        cap = max(2, 2 * blocks // count)
        slots = count * cap
        orders = PAIRS * 2 * nb
        wave, twiddle, table, steps = spectral_tables(na, nb, lat, lon)
        width = steps * PAIRS
        vmem = pl.BlockSpec(memory_space=pltpu.VMEM)
        hbm = pl.BlockSpec(memory_space=pl.ANY)
        dma = pltpu.SemaphoreType.DMA
        shapes = (slab.shape, (lat, lon), (lat, lon), (blocks, 128))

        def edges(rows_x, rows_y):
            return [
                pltpu.VMEM((2, rows_x, 128), F32),
                pltpu.VMEM((rows_y, 128), F32),
                pltpu.VMEM((2, rows_x, 128), F32),
                pltpu.VMEM((2, rows_y, 128), F32),
            ]

        results = pl.pallas_call(
            functools.partial(kernel, (na, nb, steps)),
            out_shape=tuple(pltpu.VMEM(shape, F32) for shape in shapes),
            in_specs=[
                hbm,
                hbm,
                pl.BlockSpec(memory_space=pltpu.SMEM),
                hbm,
                vmem,
                vmem,
                hbm,
                hbm,
                hbm,
            ],
            out_specs=(vmem,) * 4,
            scratch_shapes=[
                pltpu.VMEM(slab.shape, F32),
                pltpu.VMEM(speeds.shape, F32),
                pltpu.VMEM((lat, lon), F32),
                pltpu.VMEM(wave.shape, F32),
                pltpu.VMEM(twiddle.shape, F32),
                pltpu.VMEM((steps // 16 + 1, PAIRS, 128), F32),
                pltpu.VMEM((7, 4, 128, 128), F32),
                pltpu.VMEM((8, 4, 128, 128), F32),
                pltpu.VMEM((3, 128, 128), F32),
                pltpu.VMEM((2, 128, 128), F32),
                *edges(8, 16),
                *edges(32, 64),
                *edges(8, 8),
                pltpu.VMEM((2, 8, 128), F32),
                pltpu.VMEM((8, 128), F32),
                pltpu.VMEM((4, 8, 128), F32),
                *edges(32, 64),
                pltpu.VMEM((128, 128), F32),
                pltpu.VMEM((slots, 256), BF16),
                pltpu.VMEM((slots, 128), F32),
                pltpu.VMEM((count, cap, 128), F32),
                pltpu.VMEM((count, cap, 128), F32),
                pltpu.VMEM((2, lat, 128), F32),
                pltpu.VMEM((2, 2 * orders, lon), BF16),
                pltpu.VMEM((2, 2 * orders, 2 * lon), BF16),
                pltpu.VMEM((2, nb, 4 * PAIRS, lat // 2), F32),
                pltpu.VMEM((2, nb, 4 * PAIRS, lat // 2), F32),
                pltpu.VMEM((3, width, lat), BF16),
                pltpu.VMEM((2, PAIRS, width), F32),
                pltpu.VMEM((2, width), F32),
                pltpu.VMEM((na, 2, width), F32),
                pltpu.VMEM((2, nb, 4 * PAIRS, lat // 2), F32),
                pltpu.VMEM((2, 8, lon), F32),
                pltpu.VMEM((2, 8, lon), F32),
                pltpu.VMEM((4, lat, 128), F32),
                pltpu.VMEM((8, slots, 128), F32),
                pltpu.VMEM((count, cap, 128), F32),
                pltpu.VMEM((count, cap, 128), F32),
                dma((2, 4, 4)),
                dma((7,)),
                dma((7,)),
                dma((2, 2)),
                dma((2, 4)),
                dma((8,)),
                pltpu.SemaphoreType.REGULAR((2,)),
            ],
            compiler_params=pltpu.CompilerParams(
                collective_id=0, has_side_effects=True, vmem_limit_bytes=VMEM_LIMIT
            ),
        )(
            slab,
            speeds,
            source_matrix,
            pedersen,
            owners.reshape(1, blocks),
            tile_positions.reshape(1, blocks),
            jnp.asarray(wave),
            jnp.asarray(twiddle),
            jnp.asarray(table),
        )
        return pl.pallas_call(
            write_out,
            out_shape=tuple(jax.ShapeDtypeStruct(shape, F32) for shape in shapes),
            in_specs=[vmem] * 4,
            out_specs=(hbm,) * 4,
            scratch_shapes=[dma((11,))],
            compiler_params=pltpu.CompilerParams(vmem_limit_bytes=16 * 1024 * 1024),
        )(*results)

    in_specs = (
        P(None, None, "blk", "inner"),
        P(None, None, "blk", "inner"),
        P(),
        P("blk", "inner"),
        P(("blk", "inner"), None),
        P(("blk", "inner")),
    )
    out_specs = (
        P(None, None, "blk", "inner"),
        P("blk", "inner"),
        P("blk", "inner"),
        P(("blk", "inner"), None),
    )
    return jax.shard_map(shards, mesh=mesh, in_specs=in_specs, out_specs=out_specs, check_vma=False)
```

```python
import functools
import math

import jax
import jax.numpy as jnp
import numpy as np
from jax import lax
from jax.experimental import pallas as pl
from jax.experimental.pallas import tpu as pltpu
from jax.sharding import PartitionSpec as P

F32 = jnp.float32
BF16 = jnp.bfloat16
I32 = jnp.int32
MESH = pl.DeviceIdType.MESH
BLOCK = 8
PAIRS = 8
SCREENING = 2.0
GAIN = 4096.0
VMEM_LIMIT = 60 * 1024 * 1024


def iota(shape, dim):
    return lax.broadcasted_iota(I32, shape, dim)


def split(value):
    high = value.astype(BF16)
    return high, (value - high.astype(F32)).astype(BF16)


def split3(value):
    high = value.astype(BF16)
    rest = value - high.astype(F32)
    middle = rest.astype(BF16)
    return high, middle, (rest - middle.astype(F32)).astype(BF16)


def dot(left, right, dims=((1,), (0,))):
    return lax.dot_general(left, right, (dims, ((), ())), preferred_element_type=F32)


def dot3(left, right, dims):
    lh, ll = left
    rh, rl = right
    return dot(lh, rh, dims) + dot(ll, rh, dims) + dot(lh, rl, dims)


def spectral_tables(blk_count, inner_count, lat_dev, lon_dev):
    orders = PAIRS * 2 * inner_count
    degrees = orders
    lon_total = lon_dev * inner_count
    first = np.arange(inner_count * PAIRS).reshape(inner_count, 1, PAIRS)
    order_of = np.concatenate([first, orders - 1 - first], axis=1).reshape(-1)
    cols = np.arange(lon_dev)
    phase = (order_of[:, None] * cols[None, :] % lon_total) * (2.0 * math.pi / lon_total)
    wave = np.stack([np.cos(phase), np.sin(phase)]).astype(np.float32)
    turn = (order_of[:, None] * (np.arange(inner_count) * lon_dev)[None, :] % lon_total) * (
        2.0 * math.pi / lon_total
    )
    twiddle = np.zeros((order_of.shape[0], 128), np.float32)
    twiddle[:, :inner_count] = np.cos(turn)
    twiddle[:, 32 : 32 + inner_count] = np.sin(turn)
    twiddle[:, 64] = order_of
    twiddle[:, 65] = np.where(order_of == 0, 1.0, 2.0)

    turns = -(-(degrees + 1) // 16)
    steps = turns * 16
    table = np.zeros((inner_count, turns + 1, PAIRS, 128), np.float32)

    def up(degree, order):
        return np.sqrt(
            np.float32(4.0 * degree * degree - 1.0) / np.float32(degree * degree - order * order)
        )

    counter = np.arange(1, orders, dtype=np.float64)
    log_start = 0.5 * np.log(0.5) + np.concatenate(
        [np.zeros(1), np.cumsum(0.5 * np.log((2.0 * counter + 1.0) / (2.0 * counter)))]
    )
    for pair in range(inner_count * PAIRS):
        place, lane = divmod(pair, PAIRS)
        low, partner = pair, orders - 1 - pair
        table[place, turns, lane, :4] = [low, log_start[low], partner, log_start[partner]]
        for step in range(degrees + 1):
            if step <= low:
                order, degree, kind = partner, partner + step, 3
            else:
                order, degree, kind = low, step - 1, 2
            turn_at, offset = divmod(step, 16)
            if degree == order:
                table[place, turn_at, lane, kind * 16 + offset] = 1.0
                continue
            ratio = up(degree, order)
            table[place, turn_at, lane, offset] = ratio
            if degree >= order + 2:
                table[place, turn_at, lane, 16 + offset] = ratio / up(degree - 1, order)
    return wave, twiddle, table, steps


def kernel(
    sizes,
    u_hbm,
    w_hbm,
    mix_ref,
    ped_hbm,
    owner_ref,
    tile_ref,
    wave_hbm,
    twiddle_hbm,
    table_hbm,
    out_ref,
    pot_ref,
    heat_ref,
    blocks_ref,
    u_ref,
    w_ref,
    ped_ref,
    wave_ref,
    twiddle_ref,
    ratios,
    coef,
    u1,
    q_ref,
    source_ref,
    first_send_x,
    first_send_y,
    first_recv_x,
    first_recv_y,
    rest_send_x,
    rest_send_y,
    rest_recv_x,
    rest_recv_y,
    face_send_x,
    face_send_y,
    face_recv_x,
    face_recv_y,
    ring_x,
    corner_send,
    corner_recv,
    last_send_x,
    last_send_y,
    last_recv_x,
    last_recv_y,
    turned,
    sel_t,
    label_ref,
    face_send,
    face_recv,
    forcing,
    base_ref,
    values_ref,
    spec_send,
    spec_recv,
    leg,
    mask_ref,
    coef_send,
    coef_recv,
    syn_all,
    rim_send,
    rim_recv,
    grids,
    wide,
    reply_send,
    reply_recv,
    edge_sems,
    send_sems,
    recv_sems,
    rim_sems,
    corner_sems,
    in_sems,
    ready,
):
    na, nb, steps = sizes
    count = na * nb
    lat, lon = ped_ref.shape
    rows_total, cols_total = lat * na, lon * nb
    cap = face_send.shape[1]
    slots = count * cap
    a, b = lax.axis_index("blk"), lax.axis_index("inner")
    me = a * nb + b
    orders = PAIRS * 2 * nb
    spec_rows = 2 * orders

    nx, nz = na // 2, min(4, nb)
    ny = nb // nz
    chip_x, core, chip_y, chip_z = a // 2, lax.rem(a, 2), b // nz, lax.rem(b, nz)
    peer_a = {
        (dx, dc): lax.rem(chip_x + dx, nx) * 2 + lax.rem(core + dc, 2)
        for dx in range(nx)
        for dc in range(2)
    }
    peer_b = {
        (dy, dz): lax.rem(chip_y + dy, ny) * nz + lax.rem(chip_z + dz, nz)
        for dy in range(ny)
        for dz in range(nz)
    }

    def hops(move):
        dx, dc, dy, dz = move
        return 2 * (min(dx, nx - dx) + min(dy, ny - dy) + min(dz, nz - dz)) + dc

    moves = sorted(
        [(dx, dc, dy, dz) for dx, dc in peer_a for dy, dz in peer_b if (dx, dc, dy, dz) != (0, 0, 0, 0)],
        key=hops,
        reverse=True,
    )
    blk_moves = [move for move in moves if move[2:] == (0, 0)]
    inner_moves = [move for move in moves if move[:2] == (0, 0)]

    def device(move):
        return peer_a[move[:2]], peer_b[move[2:]]

    def remote(src, dst, send_sem, recv_sem, target):
        pltpu.make_async_remote_copy(
            src_ref=src,
            dst_ref=dst,
            send_sem=send_sem,
            recv_sem=recv_sem,
            device_id=target,
            device_id_type=MESH,
        ).start()

    def take(ref, sem):
        pltpu.make_async_copy(ref, ref, sem).wait()

    def signal(sem, target):
        pl.semaphore_signal(sem, inc=1, device_id=target, device_id_type=MESH)

    up_a, down_a = lax.rem(a + 1, na), lax.rem(a + na - 1, na)
    up_b, down_b = lax.rem(b + 1, nb), lax.rem(b + nb - 1, nb)

    fetches = [
        pltpu.make_async_copy(src, dst, in_sems.at[at])
        for at, (src, dst) in enumerate(
            [
                (w_hbm, w_ref),
                (u_hbm.at[7], u_ref.at[7]),
                (u_hbm.at[pl.ds(0, 7), pl.ds(0, 3)], u_ref.at[pl.ds(0, 7), pl.ds(0, 3)]),
                (u_hbm.at[pl.ds(0, 7), pl.ds(3, 1)], u_ref.at[pl.ds(0, 7), pl.ds(3, 1)]),
                (twiddle_hbm, twiddle_ref),
                (wave_hbm, wave_ref),
                (table_hbm.at[b], ratios),
                (ped_hbm, ped_ref),
            ]
        )
    ]
    for fetch in fetches:
        fetch.start()
    barrier = pltpu.get_barrier_semaphore()
    y_moves = [move for move in inner_moves if move[3] == 0]
    z_moves = [move for move in inner_moves if move[2] == 0]
    greeted = [device(move) for move in blk_moves + y_moves + z_moves]
    greeted += [(a, up_b), (a, down_b)]
    corners = [(up_a, up_b), (up_a, down_b), (down_a, up_b), (down_a, down_b)]
    greeted += corners
    for target in greeted:
        signal(barrier, target)

    row = iota((128, 128), 0)
    lane = iota((128, 128), 1)
    row8 = iota((8, 128), 0)
    fetches[0].wait()

    def make_coef(z, carry):
        wx, wy = 0.15 * w_ref[0, z], 0.15 * w_ref[1, z]
        coef[0, z] = jnp.where(row == 127, 0.0, 0.15 + wx)
        coef[1, z] = jnp.where(row == 0, 0.0, 0.15 - wx)
        coef[2, z] = jnp.where(lane == 127, 0.0, 0.15 + wy)
        coef[3, z] = jnp.where(lane == 0, 0.0, 0.15 - wy)
        below = 0.15 + 0.15 * w_ref[2, jnp.maximum(z - 1, 0)]
        above = 0.15 - 0.15 * w_ref[2, jnp.minimum(z + 1, 3)]
        coef[4, z] = jnp.where(z > 0, below, 0.0)
        coef[5, z] = jnp.where(z < 3, above, 0.0)
        coef[6, z] = jnp.where(lane == 0, 0.15 - wy, 0.15 + wy)
        return carry

    lax.fori_loop(0, 4, make_coef, 0)

    def weighted(weights, z):
        total = weights[0] * u_ref[0, z]
        for w in range(1, 8):
            total = total + weights[w] * u_ref[w, z]
        return total

    source = [mix_ref[7, w] for w in range(8)]
    second = []
    for w in range(8):
        total = source[0] * mix_ref[0, w]
        for k in range(1, 8):
            total = total + source[k] * mix_ref[k, w]
        second.append(total)
    fetches[1].wait()
    fetches[2].wait()
    for z in range(3):
        q_ref[z] = weighted(source, z)

    def pack(src, items, send_x, send_y):
        packed = jnp.zeros((128, 128), F32)
        for k, (v, z) in enumerate(items):
            cells = q_ref.at[z] if v == 8 else src.at[v, z]
            last = (0.15 + 0.15 * w_ref[0, z, 120:128, :]) * cells[120:128, :]
            first = (0.15 - 0.15 * w_ref[0, z, 0:8, :]) * cells[0:8, :]
            send_x[0, k : k + 1, :] = last[7:8, :]
            send_x[1, k : k + 1, :] = first[0:1, :]
            rolled = pltpu.roll(coef[6, z] * cells[...], 2 * k + 1, 1)
            packed = jnp.where((lane == 2 * k) | (lane == 2 * k + 1), rolled, packed)
        send_y[...] = packed.T[0 : send_y.shape[0], :]

    def send_edges(at, send_x, send_y, recv_x, recv_y):
        for side, target in ((0, (up_a, b)), (1, (down_a, b))):
            remote(
                send_x.at[side],
                recv_x.at[side],
                edge_sems.at[0, at, side],
                edge_sems.at[1, at, side],
                target,
            )
        for side, target in ((0, (a, up_b)), (1, (a, down_b))):
            remote(
                send_y,
                recv_y.at[side],
                edge_sems.at[0, at, 2 + side],
                edge_sems.at[1, at, 2 + side],
                target,
            )

    def wait_edges(at, recv_x, recv_y):
        for side in range(2):
            take(recv_x.at[side], edge_sems.at[1, at, side])
            take(recv_y.at[side], edge_sems.at[1, at, 2 + side])
        rows = recv_y.shape[1]
        odd = (iota((rows, 128), 0) & 1) == 1
        up = jnp.where(b > 0, recv_y[0], 0.0)
        down = jnp.where(b < nb - 1, recv_y[1], 0.0)
        mixed = jnp.where(odd, pltpu.roll(up, 1, 0), pltpu.roll(down, rows - 1, 0))
        if rows < 128:
            mixed = jnp.concatenate([mixed, jnp.zeros((128 - rows, 128), F32)], axis=0)
        turned[...] = mixed.T

    def drain_edges(at, send_x, send_y):
        for side in range(2):
            take(send_x.at[side], edge_sems.at[0, at, side])
            take(send_y, edge_sems.at[0, at, 2 + side])

    def mend(cells, recv_x, k):
        rolled = pltpu.roll(turned[...], 127 - 2 * k, 1)
        whole = cells[...] + jnp.where((lane == 0) | (lane == 127), rolled, 0.0)
        from_down = jnp.where(a > 0, recv_x[0, k : k + 1, :], 0.0)
        from_up = jnp.where(a < na - 1, recv_x[1, k : k + 1, :], 0.0)
        cells[8:120, :] = whole[8:120]
        cells[0:8, :] = whole[0:8] + jnp.where(row8 == 0, from_down, 0.0)
        cells[120:128, :] = whole[120:128] + jnp.where(row8 == 7, from_up, 0.0)

    def transport(field, z):
        u = field(z)
        total = pltpu.roll(coef[0, z] * u, 1, 0) + pltpu.roll(coef[1, z] * u, 127, 0)
        total = total + pltpu.roll(coef[2, z] * u, 1, 1) + pltpu.roll(coef[3, z] * u, 127, 1)
        if z > 0:
            total = total + coef[4, z] * field(z - 1)
        if z < 3:
            total = total + coef[5, z] * field(z + 1)
        return total + 0.1 * u

    def advance(src, dst, v, z):
        u = src[v, z]
        total = mix_ref[v, 0] * src[0, z]
        for w in range(1, 8):
            total = total + mix_ref[v, w] * src[w, z]
        total = 0.3 * total + 0.1 * u
        total = total + pltpu.roll(coef[0, z] * u, 1, 0) + pltpu.roll(coef[1, z] * u, 127, 0)
        total = total + pltpu.roll(coef[2, z] * u, 1, 1) + pltpu.roll(coef[3, z] * u, 127, 1)
        if not (isinstance(z, int) and z == 0):
            total = total + coef[4, z] * src[v, z - 1 if isinstance(z, int) else jnp.maximum(z - 1, 0)]
        if not (isinstance(z, int) and z == 3):
            total = total + coef[5, z] * src[v, z + 1 if isinstance(z, int) else jnp.minimum(z + 1, 3)]
        dst[v, z] = total

    def advance_all(src, dst, vs, z):
        def one(v, carry):
            advance(src, dst, v, z)
            return carry

        lax.fori_loop(0, vs, one, 0)

    near = [(7, 0), (7, 1), (7, 2), (8, 0), (8, 1)]
    far = [(v, z) for z in range(4) for v in range(7)] + [(7, 3)]
    faced = [(7, 0), (7, 1)]
    later = [(v, z) for z in range(4) for v in range(8) if (v, z) not in faced]
    first = (first_send_x, first_send_y, first_recv_x, first_recv_y)
    rest = (rest_send_x, rest_send_y, rest_recv_x, rest_recv_y)
    of_faces = (face_send_x, face_send_y, face_recv_x, face_recv_y)
    last = (last_send_x, last_send_y, last_recv_x, last_recv_y)

    pack(u_ref, near, first_send_x, first_send_y)
    at_0, at_1 = near.index((7, 0)), near.index((7, 1))
    for side in range(2):
        for z, k in enumerate((at_0, at_1)):
            corner_send[2 * side + z : 2 * side + z + 1, :] = first_send_x[side, k : k + 1, :]
            corner_send[4 + 2 * side + z : 5 + 2 * side + z, :] = first_send_y[
                2 * k + side : 2 * k + side + 1, :
            ]
    for z in (0, 1):
        u1[7, z] = transport(lambda at: u_ref[7, at], z) + 0.3 * q_ref[z]
    columns = jnp.zeros((128, 128), F32)
    for z in (0, 1):
        upper = 0.15 + 0.15 * w_ref[0, z, 120:128, :]
        lower = 0.15 - 0.15 * w_ref[0, z, 0:8, :]
        face_send_x[0, z : z + 1, :] = (upper * u1[7, z, 120:128, :])[7:8, :]
        face_send_x[0, 2 + z : 3 + z, :] = upper[7:8, :]
        face_send_x[1, z : z + 1, :] = (lower * u1[7, z, 0:8, :])[0:1, :]
        face_send_x[1, 2 + z : 3 + z, :] = lower[0:1, :]
        factor = coef[6, z]
        scaled = factor * u1[7, z]
        columns = jnp.where(lane == z, pltpu.roll(scaled, 1 + z, 1), columns)
        columns = jnp.where(lane == 2 + z, pltpu.roll(factor, 3 + z, 1), columns)
        columns = jnp.where(lane == 4 + z, pltpu.roll(scaled, 4 + z, 1), columns)
        columns = jnp.where(lane == 6 + z, pltpu.roll(factor, 6 + z, 1), columns)
    face_send_y[...] = columns.T[0:8, :]
    pl.semaphore_wait(barrier, len(greeted))
    send_edges(1, *of_faces)
    send_edges(0, *first)
    for at, target in enumerate(corners):
        remote(corner_send, corner_recv.at[at], corner_sems.at[0, at], corner_sems.at[1, at], target)
    for move in y_moves:
        signal(ready.at[0], device(move))
    u1[7, 2] = transport(lambda at: u_ref[7, at], 2) + 0.3 * q_ref[2]
    for z in (0, 1):
        source_ref[z] = transport(lambda at: q_ref[at], z) + 0.3 * weighted(second, z)
    if y_moves:
        pl.semaphore_wait(ready.at[0], len(y_moves))
    for move in blk_moves:
        signal(ready.at[1], device(move))

    owner = jnp.broadcast_to(owner_ref[...].astype(F32), (128, 256)).T.astype(I32)
    owner_hot = jnp.where(iota((256, 128), 1) == owner, 1.0, 0.0)
    earlier = jnp.where(iota((256, 256), 0) > iota((256, 256), 1), 1.0, 0.0).astype(BF16)
    before = dot(earlier, owner_hot.astype(BF16))
    rank = jnp.sum(before * owner_hot, axis=1, keepdims=True)
    slot = owner.astype(F32) * float(cap) + rank
    slot_row = slot.T[0:1, :]
    sel = jnp.where(iota((slots, 256), 0).astype(F32) == slot_row, 1.0, 0.0).astype(BF16)
    flip = jnp.where(iota((256, 256), 0) == (iota((256, 256), 1) ^ 7), 1.0, 0.0).astype(BF16)
    sel_t[...] = dot(sel, flip).astype(BF16)
    tile_high, tile_low = split(jnp.broadcast_to(tile_ref[...].astype(F32), (128, 256)).T)
    label_ref[...] = dot(sel, tile_high) + dot(sel, tile_low)

    wait_edges(0, first_recv_x, first_recv_y)
    for k, (v, z) in enumerate(near):
        mend(source_ref.at[z] if v == 8 else u1.at[v, z], first_recv_x, k)
    for z in (0, 1):
        out_ref[7, z] = transport(lambda at: u1[7, at], z) + 0.3 * source_ref[z]

    for side in range(2):
        take(face_recv_x.at[side], edge_sems.at[1, 1, side])
        take(face_recv_y.at[side], edge_sems.at[1, 1, 2 + side])
    for at in range(4):
        take(corner_recv.at[at], corner_sems.at[1, at])
    own = corner_send[...]
    low_low = jnp.where((a > 0) & (b > 0), corner_recv[0], 0.0)
    low_high = jnp.where((a > 0) & (b < nb - 1), corner_recv[1], 0.0)
    high_low = jnp.where((a < na - 1) & (b > 0), corner_recv[2], 0.0)
    high_high = jnp.where((a < na - 1) & (b < nb - 1), corner_recv[3], 0.0)
    low_low, high_high = pltpu.roll(low_low, 1, 1), pltpu.roll(high_high, 127, 1)
    lane2 = iota((2, 128), 1)

    def beyond(came, rows, first_rows, last_rows):
        brought = rows + jnp.where(lane2 == 0, first_rows, 0.0)
        brought = brought + jnp.where(lane2 == 127, last_rows, 0.0)
        return came[0:2] + came[2:4] * brought

    from_left = beyond(face_recv_y[0, 0:4], own[6:8], low_low[0:2], high_low[2:4])
    from_right = beyond(face_recv_y[1, 4:8], own[4:6], low_high[0:2], high_high[2:4])
    from_left = jnp.where(b > 0, from_left, 0.0)
    from_right = jnp.where(b < nb - 1, from_right, 0.0)
    ring_x[0, 0:2, :] = beyond(face_recv_x[0, 0:4], own[2:4], low_low[4:6], low_high[6:8])
    ring_x[1, 0:2, :] = beyond(face_recv_x[1, 0:4], own[0:2], high_low[4:6], high_high[6:8])
    beside = [from_right[0:1], from_left[0:1], from_right[1:2], from_left[1:2]]
    turned[...] = jnp.concatenate(beside + [jnp.zeros((124, 128), F32)], axis=0).T
    for k, (v, z) in enumerate(faced):
        mend(out_ref.at[v, z], ring_x, k)
    current = out_ref[7, 1] - out_ref[7, 0]

    halves = [pltpu.roll(current, 64, 1).reshape(16, 8, 128), current.reshape(16, 8, 128)]
    group = iota((16, 8, 128), 2) // 8
    faces = []
    for half in range(2):
        face = jnp.zeros((16, 8, 128), F32)
        for r in range(8):
            spread = jnp.broadcast_to(halves[half][:, r : r + 1, :], (16, 8, 128))
            moved = pltpu.roll(spread, 8 * r + 8, 2, stride=8, stride_axis=1)
            face = jnp.where(group == r, moved, face)
        faces.append(face)
    faces = jnp.stack(faces, axis=1).reshape(256, 128)
    face_high, face_low = split(faces)
    routed = dot(sel_t[...], face_high) + dot(sel_t[...], face_low)
    lane_slot = iota((slots, 128), 1)
    routed = jnp.where(lane_slot < 64, routed, label_ref[...])
    face_send[...] = routed.reshape(count, cap, 128)

    def send_all(src, dst, at):
        for move in moves:
            peer_of_a, peer_of_b = device(move)
            remote(
                src.at[peer_of_a * nb + peer_of_b],
                dst.at[me],
                send_sems.at[at],
                recv_sems.at[at],
                (peer_of_a, peer_of_b),
            )
        dst[me] = src[me]

    pl.semaphore_wait(ready.at[1], len(blk_moves))
    send_all(face_send, face_recv, 0)

    fetches[3].wait()
    pack(u_ref, far, rest_send_x, rest_send_y)
    send_edges(2, *rest)

    fetches[4].wait()
    fetches[5].wait()

    def per_row(column):
        return jnp.sum(
            jnp.where(iota((orders, 128), 1) == column, twiddle_ref[...], 0.0),
            axis=1,
            keepdims=True,
        )

    def rows_of(even, odd):
        return jnp.concatenate([even, odd], axis=2).reshape(spec_rows, lon)

    def waves():
        cos_turn, sin_turn = per_row(b), per_row(b + 32)
        cos_wave, sin_wave = wave_ref[0], wave_ref[1]
        cosine = (cos_turn * cos_wave - sin_turn * sin_wave).reshape(nb, 2, 1, PAIRS, lon)
        sine = (sin_turn * cos_wave + cos_turn * sin_wave).reshape(nb, 2, 1, PAIRS, lon)
        return cosine, sine

    cosine, sine = waves()
    base_high, base_low = split(rows_of(cosine, sine) * (1.0 / cols_total))
    base_ref[0] = base_high
    base_ref[1] = base_low

    for z in range(3):
        advance_all(u_ref, u1, 7, z)

    take(face_recv.at[pl.ds(0, count - 1)], recv_sems.at[0])
    got = face_recv[...].reshape(slots, 128)
    swapped = pltpu.roll(got, 64, 1)
    label = jnp.where(lane_slot < 64, swapped, got).astype(I32)
    face = jnp.where(lane_slot < 64, got, swapped)
    tile_row, tile_col = label >> 5, label & 31
    tile_row_t = tile_row.astype(F32).T.astype(I32)
    scatter = jnp.where(iota((32, slots), 0) == tile_row_t[0:32, :], 1.0, 0.0).astype(BF16)
    scatter = jnp.concatenate([scatter, scatter], axis=1)
    col_masks = [
        jnp.where((lane_slot >> 3) + 16 * half == tile_col, 1.0, 0.0).astype(BF16)
        for half in range(2)
    ]

    def spread_bit(value, width):
        moved = pltpu.roll(value, width, 1)
        bit = (lane_slot & width) == 0
        return [jnp.where(bit, value, moved), jnp.where(bit, moved, value)]

    lines = [face]
    for width in (32, 16, 8):
        lines = [part for line in lines for part in spread_bit(line, width)]
    for r in range(8):
        line_high, line_low = split(lines[r])
        right = jnp.concatenate(
            [
                jnp.concatenate([part * mask for mask in col_masks], axis=1)
                for part in (line_high, line_low)
            ],
            axis=0,
        )
        rows = dot(scatter, right)
        forcing[0, pl.ds(r, 32, stride=8), :] = rows[:, 0:128]
        forcing[1, pl.ds(r, 32, stride=8), :] = rows[:, 128:256]

    middle_row, quarter = lat // 2, lat // 4
    for half in range(2):
        whole = [forcing[0], forcing[1]]
        if half == 0:
            rows = [jnp.concatenate([part[0:quarter], part[lat - quarter :]], axis=0) for part in whole]
        else:
            rows = [part[quarter : lat - quarter] for part in whole]
        force = split(jnp.concatenate(rows, axis=1))
        spectrum = dot3((base_ref[0], base_ref[1]), force, ((1,), (1,)))
        spec_send[half] = spectrum.reshape(nb, 4 * PAIRS, middle_row)
        for move in inner_moves:
            peer = peer_b[move[2:]]
            remote(
                spec_send.at[half, peer],
                spec_recv.at[half, b],
                send_sems.at[1 + 4 * half],
                recv_sems.at[1 + 4 * half],
                (a, peer),
            )
        spec_recv[half, b] = spec_send[half, b]

    fetches[6].wait()
    place = iota((PAIRS, lat), 1)
    place = jnp.where(
        place < quarter,
        place,
        jnp.where(place < middle_row, place + middle_row, place - quarter),
    )
    row_of_lane = a * lat + place
    x = -1.0 + (2.0 * row_of_lane.astype(F32) + 1.0) / rows_total
    log_sine = jnp.log(jnp.sqrt(1.0 - x * x))
    turns = steps // 16
    heads = ratios[turns]
    low_start = jnp.exp(heads[:, 1:2] + heads[:, 0:1] * log_sine)
    high_start = jnp.exp(heads[:, 3:4] + heads[:, 2:3] * log_sine)

    def build(turn, carry):
        previous, older = carry
        block = ratios[turn]
        made = []
        for offset in range(16):
            up = block[:, offset : offset + 1]
            down = block[:, 16 + offset : 17 + offset]
            begin_low = block[:, 32 + offset : 33 + offset]
            begin_high = block[:, 48 + offset : 49 + offset]
            present = (
                begin_low * low_start + begin_high * high_start + up * x * previous - down * older
            )
            made.append(present)
            older, previous = previous, present
        where = pl.ds(pl.multiple_of(turn * 128, 128), 128)
        for at, part in enumerate(split3(jnp.concatenate(made, axis=0))):
            leg[at, where, :] = part
        return previous, older

    empty = jnp.zeros((PAIRS, lat), F32)
    lax.fori_loop(0, turns, build, (empty, empty))

    width = steps * PAIRS
    at_step = iota((PAIRS, width), 1) // PAIRS
    at_pair = lax.rem(iota((PAIRS, width), 1), PAIRS)
    order_low = b * PAIRS + at_pair
    is_high = at_step <= order_low
    degree = jnp.where(is_high, orders - 1 - order_low + at_step, at_step - 1).astype(F32)
    scale = (2.0 / rows_total) * GAIN / (degree * (degree + 1.0) + SCREENING)
    scale = jnp.where(at_step <= orders, scale, 0.0)
    mine = at_pair == iota((PAIRS, width), 0)
    mask_ref[0] = jnp.where(mine & jnp.logical_not(is_high), scale, 0.0)
    mask_ref[1] = jnp.where(mine & is_high, scale, 0.0)

    advance_all(u_ref, u1, 8, 3)
    wait_edges(2, rest_recv_x, rest_recv_y)
    for k, (v, z) in enumerate(far):
        mend(u1.at[v, z], rest_recv_x, k)
    pack(u1, later, last_send_x, last_send_y)
    send_edges(3, *last)

    wide_sums = None
    for half in range(2):
        take(spec_recv.at[half, pl.ds(0, nb - 1)], recv_sems.at[1 + 4 * half])
        spec = spec_recv[half, 0]
        for at in range(1, nb):
            spec = spec + spec_recv[half, at]
        spec_high, spec_low = split(spec)
        cols = slice(half * middle_row, (half + 1) * middle_row)
        both = dot(jnp.concatenate([spec_high, spec_low], axis=0), leg[0, :, cols], ((1,), (1,)))
        part = both[0:32] + both[32:64] + dot(spec_high, leg[1, :, cols], ((1,), (1,)))
        wide_sums = part if wide_sums is None else wide_sums + part
    for parity in range(2):
        low_rows = wide_sums[parity * 8 : parity * 8 + 8]
        high_rows = wide_sums[16 + parity * 8 : 24 + parity * 8]
        kept = low_rows * mask_ref[0] + high_rows * mask_ref[1]
        coef_send[parity : parity + 1, :] = jnp.sum(kept, axis=0, keepdims=True)
    for move in blk_moves:
        remote(
            coef_send,
            coef_recv.at[a],
            send_sems.at[2],
            recv_sems.at[2],
            (peer_a[move[:2]], b),
        )
    coef_recv[a] = coef_send[...]
    for z in (0, 1):
        advance_all(u1, out_ref, 7, z)
    take(coef_recv.at[pl.ds(0, na - 1)], recv_sems.at[2])
    solved = coef_recv[0]
    for at in range(1, na):
        solved = solved + coef_recv[at]
    expanded = []
    for kind in range(2):
        for parity in range(2):
            expanded.append(
                jnp.where(
                    mask_ref[kind] != 0.0,
                    jnp.broadcast_to(solved[parity : parity + 1, :], (PAIRS, width)),
                    0.0,
                )
            )
    solved_high, solved_low = split(jnp.concatenate(expanded, axis=0))
    solved_both = jnp.concatenate([solved_high, solved_low], axis=0)
    fine = dot(solved_high, leg[2])
    both = dot(solved_both, leg[0])
    middle = dot(solved_both, leg[1])
    syn = both[0:32] + (both[32:64] + (middle[0:32] + (middle[32:64] + fine)))
    for half in range(2):
        syn_all[half, b] = syn[:, half * middle_row : (half + 1) * middle_row]
    for half in range(2):
        for move in inner_moves:
            remote(
                syn_all.at[half, b],
                syn_all.at[half, b],
                send_sems.at[3 + 3 * half],
                recv_sems.at[3 + 3 * half],
                (a, peer_b[move[2:]]),
            )
    order_col, weight_col = per_row(64), per_row(65)
    cosine, sine = waves()
    weight = weight_col.reshape(nb, 2, 1, PAIRS, 1)
    slope_weight = (weight_col * order_col).reshape(nb, 2, 1, PAIRS, 1)
    value_high, value_low = split(rows_of(cosine * weight, sine * weight))
    values_ref[0, :, 0:lon] = value_high
    values_ref[1, :, 0:lon] = value_low
    slope_high, slope_low = split(rows_of(-sine * slope_weight, cosine * slope_weight))
    values_ref[0, :, lon : 2 * lon] = slope_high
    values_ref[1, :, lon : 2 * lon] = slope_low

    for z in (2, 3):
        advance_all(u1, out_ref, 8, z)
    wait_edges(3, last_recv_x, last_recv_y)
    for k, (v, z) in enumerate(later):
        mend(out_ref.at[v, z], last_recv_x, k)

    def potential_of(high, middle, low):
        rows = high.shape[0]
        coarse = dot(jnp.concatenate([high, middle, low], axis=0), values_ref[0, :, 0:lon])
        rest_of = dot(jnp.concatenate([high, middle], axis=0), values_ref[1, :, 0:lon])
        return coarse[0:rows] + (
            coarse[rows : 2 * rows] + (rest_of[0:rows] + (coarse[2 * rows :] + rest_of[rows:]))
        )

    potentials, slopes = [], []
    for half in range(2):
        take(syn_all.at[half, pl.ds(0, nb - 1)], recv_sems.at[3 + 3 * half])
        parts = split3(syn_all[half].reshape(spec_rows, middle_row).T)
        if half == 0:
            rims = potential_of(
                *(jnp.concatenate([part[0:16], part[middle_row - 16 :]], axis=0) for part in parts)
            )
            rim_send[0] = rims[0:8]
            rim_send[1] = rims[24:32]
            for side, target in enumerate(((down_a, b), (up_a, b))):
                remote(
                    rim_send.at[side],
                    rim_recv.at[1 - side],
                    rim_sems.at[0, side],
                    rim_sems.at[1, 1 - side],
                    target,
                )
        potentials.append(potential_of(*parts))
        coarse = dot(jnp.concatenate(parts[0:2], axis=0), values_ref[0, :, lon : 2 * lon])
        finer = dot(parts[0], values_ref[1, :, lon : 2 * lon])
        slopes.append(coarse[0:middle_row] + (coarse[middle_row:] + finer))

    def in_order(outer, inner):
        return jnp.concatenate([outer[0:quarter], inner, outer[quarter:]], axis=0)

    potential = in_order(*potentials)
    azimuthal = in_order(*slopes)
    pot_ref[...] = potential
    fetches[7].wait()
    grid_row = iota((lat, 1), 0)
    global_row = a * lat + grid_row
    x_col = -1.0 + (2.0 * global_row.astype(F32) + 1.0) / rows_total
    sine_col = jnp.sqrt(1.0 - x_col * x_col)
    eastward = azimuthal / sine_col
    inverse = rows_total / 2.0

    def heat_of(first_row, last_row, above, below):
        part = slice(first_row, last_row)
        at_first, at_last = global_row[part] == 0, global_row[part] == rows_total - 1
        here = potential[part]
        slope = (jnp.where(at_last, here, above) - jnp.where(at_first, here, below)) * (
            jnp.where(at_first | at_last, inverse, 0.5 * inverse)
        )
        polar = sine_col[part] * slope
        return ped_ref[part, :] * (polar * polar + eastward[part] * eastward[part])

    above, below = pltpu.roll(potential, lat - 1, 0), pltpu.roll(potential, 1, 0)
    heating = heat_of(0, lat, above, below)
    heat_ref[...] = heating

    grids[0] = potential[:, 0:128]
    grids[1] = potential[:, 128:256]
    grids[2] = heating[:, 0:128]
    grids[3] = heating[:, 128:256]
    pick = iota((slots, 128), 1)
    pick = jnp.where((pick < 96) & ((pick & 31) == tile_row), 1.0, 0.0).astype(BF16)
    bits = [(tile_col & (1 << at)) != 0 for at in range(5)]
    upper = lane_slot >= 64

    def pick_row(r):
        rows = jnp.concatenate([grids[at, pl.ds(r, 32, stride=8), :] for at in range(4)], axis=1)
        high, middle, low = split3(rows)
        parts = jnp.concatenate([high, middle, low, jnp.zeros_like(low)], axis=0)
        picked = dot(pick, parts)
        pot = jnp.where(bits[4], picked[:, 128:256], picked[:, 0:128])
        heat = jnp.where(bits[4], picked[:, 384:512], picked[:, 256:384])
        wide[r] = jnp.where(
            upper,
            jnp.where(bits[3], heat, pltpu.roll(heat, 64, 1)),
            jnp.where(bits[3], pltpu.roll(pot, 64, 1), pot),
        )

    for r in range(1, 7):
        pick_row(r)
    take(rim_recv.at[0], rim_sems.at[1, 0])
    take(rim_recv.at[1], rim_sems.at[1, 1])
    edge8 = iota((8, lon), 0)
    top = heat_of(0, 8, above[0:8], jnp.where(edge8 == 0, rim_recv[0, 7:8, :], below[0:8]))
    bottom = heat_of(
        lat - 8, lat, jnp.where(edge8 == 7, rim_recv[1, 0:1, :], above[lat - 8 :]), below[lat - 8 :]
    )
    for first_row, part in ((0, top), (lat - 8, bottom)):
        heat_ref[first_row : first_row + 8, :] = part
        grids[2, first_row : first_row + 8, :] = part[:, 0:128]
        grids[3, first_row : first_row + 8, :] = part[:, 128:256]
    for r in (0, 7):
        pick_row(r)

    def join(first, second, at):
        width = 8 << at
        return jnp.where(
            (lane_slot & width) == 0,
            jnp.where(bits[at], pltpu.roll(first, 128 - width, 1), first),
            jnp.where(bits[at], second, pltpu.roll(second, width, 1)),
        )

    quads = [join(wide[r], wide[r + 4], 2) for r in range(4)]
    twos = [join(quads[r], quads[r + 2], 1) for r in range(2)]
    reply_send[...] = join(twos[0], twos[1], 0).reshape(count, cap, 128)
    send_all(reply_send, reply_recv, 4)
    chosen = jnp.where(iota((256, slots), 1).astype(F32) == slot[:, 0:1], 1.0, 0.0).astype(BF16)
    take(reply_recv.at[pl.ds(0, count - 1)], recv_sems.at[4])
    back_high, back_low = split(reply_recv[...].reshape(slots, 128))
    blocks_ref[...] = dot(chosen, back_high) + dot(chosen, back_low)

    for at, (sent_x, sent_y, _, _) in enumerate((first, of_faces, rest, last)):
        drain_edges(at, sent_x, sent_y)
    take(face_send.at[pl.ds(0, count - 1)], send_sems.at[0])
    for half in range(2):
        take(spec_send.at[half, pl.ds(0, nb - 1)], send_sems.at[1 + 4 * half])
        take(syn_all.at[half, pl.ds(0, nb - 1)], send_sems.at[3 + 3 * half])
    take(coef_recv.at[pl.ds(0, na - 1)], send_sems.at[2])
    take(reply_send.at[pl.ds(0, count - 1)], send_sems.at[4])
    for at in range(4):
        take(corner_send, corner_sems.at[0, at])
    take(rim_send.at[0], rim_sems.at[0, 0])
    take(rim_send.at[1], rim_sems.at[0, 1])


def write_out(slab, potential, heating, blocks, *refs):
    pieces = [(slab.at[v], refs[0].at[v]) for v in range(8)]
    pieces += [(potential, refs[1]), (heating, refs[2]), (blocks, refs[3])]
    copies = [
        pltpu.make_async_copy(src, dst, refs[4].at[k]) for k, (src, dst) in enumerate(pieces)
    ]
    for copy in copies:
        copy.start()
    for copy in copies:
        copy.wait()


def solution(mesh):
    na, nb = mesh.shape["blk"], mesh.shape["inner"]
    count = na * nb

    def shards(slab, speeds, source_matrix, pedersen, owners, tile_positions):
        lat, lon = pedersen.shape
        blocks = owners.shape[0]
        cap = max(2, 2 * blocks // count)
        slots = count * cap
        orders = PAIRS * 2 * nb
        wave, twiddle, table, steps = spectral_tables(na, nb, lat, lon)
        width = steps * PAIRS
        vmem = pl.BlockSpec(memory_space=pltpu.VMEM)
        hbm = pl.BlockSpec(memory_space=pl.ANY)
        dma = pltpu.SemaphoreType.DMA
        shapes = (slab.shape, (lat, lon), (lat, lon), (blocks, 128))

        def edges(rows_x, rows_y):
            return [
                pltpu.VMEM((2, rows_x, 128), F32),
                pltpu.VMEM((rows_y, 128), F32),
                pltpu.VMEM((2, rows_x, 128), F32),
                pltpu.VMEM((2, rows_y, 128), F32),
            ]

        results = pl.pallas_call(
            functools.partial(kernel, (na, nb, steps)),
            out_shape=tuple(pltpu.VMEM(shape, F32) for shape in shapes),
            in_specs=[
                hbm,
                hbm,
                pl.BlockSpec(memory_space=pltpu.SMEM),
                hbm,
                vmem,
                vmem,
                hbm,
                hbm,
                hbm,
            ],
            out_specs=(vmem,) * 4,
            scratch_shapes=[
                pltpu.VMEM(slab.shape, F32),
                pltpu.VMEM(speeds.shape, F32),
                pltpu.VMEM((lat, lon), F32),
                pltpu.VMEM(wave.shape, F32),
                pltpu.VMEM(twiddle.shape, F32),
                pltpu.VMEM((steps // 16 + 1, PAIRS, 128), F32),
                pltpu.VMEM((7, 4, 128, 128), F32),
                pltpu.VMEM((8, 4, 128, 128), F32),
                pltpu.VMEM((3, 128, 128), F32),
                pltpu.VMEM((2, 128, 128), F32),
                *edges(8, 16),
                *edges(32, 64),
                *edges(8, 8),
                pltpu.VMEM((2, 8, 128), F32),
                pltpu.VMEM((8, 128), F32),
                pltpu.VMEM((4, 8, 128), F32),
                *edges(32, 64),
                pltpu.VMEM((128, 128), F32),
                pltpu.VMEM((slots, 256), BF16),
                pltpu.VMEM((slots, 128), F32),
                pltpu.VMEM((count, cap, 128), F32),
                pltpu.VMEM((count, cap, 128), F32),
                pltpu.VMEM((2, lat, 128), F32),
                pltpu.VMEM((2, 2 * orders, lon), BF16),
                pltpu.VMEM((2, 2 * orders, 2 * lon), BF16),
                pltpu.VMEM((2, nb, 4 * PAIRS, lat // 2), F32),
                pltpu.VMEM((2, nb, 4 * PAIRS, lat // 2), F32),
                pltpu.VMEM((3, width, lat), BF16),
                pltpu.VMEM((2, PAIRS, width), F32),
                pltpu.VMEM((2, width), F32),
                pltpu.VMEM((na, 2, width), F32),
                pltpu.VMEM((2, nb, 4 * PAIRS, lat // 2), F32),
                pltpu.VMEM((2, 8, lon), F32),
                pltpu.VMEM((2, 8, lon), F32),
                pltpu.VMEM((4, lat, 128), F32),
                pltpu.VMEM((8, slots, 128), F32),
                pltpu.VMEM((count, cap, 128), F32),
                pltpu.VMEM((count, cap, 128), F32),
                dma((2, 4, 4)),
                dma((7,)),
                dma((7,)),
                dma((2, 2)),
                dma((2, 4)),
                dma((8,)),
                pltpu.SemaphoreType.REGULAR((2,)),
            ],
            compiler_params=pltpu.CompilerParams(
                collective_id=0, has_side_effects=True, vmem_limit_bytes=VMEM_LIMIT
            ),
        )(
            slab,
            speeds,
            source_matrix,
            pedersen,
            owners.reshape(1, blocks),
            tile_positions.reshape(1, blocks),
            jnp.asarray(wave),
            jnp.asarray(twiddle),
            jnp.asarray(table),
        )
        return pl.pallas_call(
            write_out,
            out_shape=tuple(jax.ShapeDtypeStruct(shape, F32) for shape in shapes),
            in_specs=[vmem] * 4,
            out_specs=(hbm,) * 4,
            scratch_shapes=[dma((11,))],
            compiler_params=pltpu.CompilerParams(vmem_limit_bytes=16 * 1024 * 1024),
        )(*results)

    in_specs = (
        P(None, None, "blk", "inner"),
        P(None, None, "blk", "inner"),
        P(),
        P("blk", "inner"),
        P(("blk", "inner"), None),
        P(("blk", "inner")),
    )
    out_specs = (
        P(None, None, "blk", "inner"),
        P("blk", "inner"),
        P("blk", "inner"),
        P(("blk", "inner"), None),
    )
    return jax.shard_map(shards, mesh=mesh, in_specs=in_specs, out_specs=out_specs, check_vma=False)
```
